32 devices in a mesh: section: 2 (over core), tensor: 4 (over y, x), dp: 4 (over z).
Axes of the slice: x: 2, y: 2, z: 4, core: 2. Of those that a mesh axis runs over, the one named last changes fastest.
Arguments:
- hidden_in: bfloat16 [2, 512, 1024], P(None, 'dp', 'tensor'), may hold values from -6 to 6
- cotangent: bfloat16 [2, 512, 1024], P(None, 'dp', 'tensor'), may hold values from -6 to 6
- lengths: int32 [2, 8], replicated, may hold values from 1 to 256, as said below
- w_qkv: bfloat16 [2, 1024, 3, 1024], P('section', None, None, 'tensor'), may hold values from -0.1875 to 0.1875
- w_out: bfloat16 [2, 1024, 1024], P('section', 'tensor'), may hold values from -0.1875 to 0.1875
- w_ug: bfloat16 [2, 1024, 2, 4096], P('section', None, None, 'tensor'), may hold values from -0.1875 to 0.1875
- w_down: bfloat16 [2, 4096, 1024], P('section', 'tensor'), may hold values from -0.09375 to 0.09375
- s_qk: float32 [2, 1024], P('section', 'tensor'), may hold values from 0.6 to 1.6
- s_uv: float32 [2, 2, 4096], P('section', None, 'tensor'), may hold values from 0.5 to 2
- alpha: float32 [2, 2, 1024], P('section', None, 'tensor'), may hold values from 0.15 to 0.6
Outputs:
- layer_outputs: bfloat16 [2, 2, 512, 1024], P('section', None, 'dp', 'tensor')
- input_grads: bfloat16 [2, 2, 512, 1024], P('section', None, 'dp', 'tensor')
- grad_w_qkv: float32 [2, 1024, 3, 1024], P('section', 'dp', None, 'tensor')
- grad_w_out: float32 [2, 1024, 1024], P('section', ('tensor', 'dp'))
- grad_w_ug: float32 [2, 1024, 2, 4096], P('section', 'dp', None, 'tensor')
- grad_w_down: float32 [2, 4096, 1024], P('section', ('tensor', 'dp'))
- grad_s_qk: float32 [2, 1024], P('section', ('tensor', 'dp'))
- grad_s_uv: float32 [2, 2, 4096], P('section', None, ('tensor', 'dp'))
- grad_alpha: float32 [2, 2, 1024], P('section', None, ('tensor', 'dp'))
The draws below stay inside these ranges and needn't reach their ends.
Inputs may be any that keep to these rules, and one draw needn't show every extreme that they name: In each row the 8 lengths sum to 512; the first is exactly 256 and none is longer.
All inputs are finite; a program needn't handle non-finite values.
Results may differ from the reference program's by a relative error of at most 0.038.
Values may be sent and summed in bfloat16 or wider, within the bound.
A program may use at most 128 MiB of HBM per device.

```python
import math
import jax
import jax.numpy as jnp
from jax import lax

D = 1024
HEAD_DIM = 64
FF = 4096
MICRO = 2
NSEQ = 8
LAYERS = 2
TOKENS = 512
MAXLEN = 256


def draw_lengths(key, part):
    rest = TOKENS - MAXLEN
    count = NSEQ - 1
    base = rest // count
    extra = rest % count
    column = jnp.arange(count, dtype=jnp.int32)
    pieces = jnp.broadcast_to(base + (column < extra).astype(jnp.int32), (MICRO, count)).astype(jnp.int32)
    for round_no in range(6):
        offset = round_no % 2
        pairs = (count - offset) // 2
        if pairs > 0:
            middle = pieces[:, offset:offset + 2 * pairs].reshape(MICRO, pairs, 2)
            total = middle[:, :, 0] + middle[:, :, 1]
            lower = jnp.maximum(1, total - MAXLEN).astype(jnp.int32)
            upper = jnp.minimum(MAXLEN, total - 1).astype(jnp.int32)
            first = jax.random.randint(jax.random.fold_in(key, 17 + round_no), (MICRO, pairs), lower, upper + 1, dtype=jnp.int32)
            second = (total - first).astype(jnp.int32)
            changed = jnp.stack([first, second], axis=2).reshape(MICRO, 2 * pairs)
            pieces = jnp.concatenate([pieces[:, :offset], changed, pieces[:, offset + 2 * pairs:]], axis=1).astype(jnp.int32)
    head = jnp.full((MICRO, 1), MAXLEN, jnp.int32)
    return jnp.concatenate([head, pieces], axis=1).astype(jnp.int32)


def steps_of(stream_key, shape, cuts, least, top_value):
    gain, own = 1.0, jax.random.fold_in(stream_key, 6)
    for axis_at, parts in cuts:
        heights = jnp.exp(jax.random.uniform(jax.random.fold_in(own, axis_at), (parts,), jnp.float32, least / len(cuts), top_value / len(cuts)))
        gain = gain * jnp.repeat(heights, shape[axis_at] // parts).reshape([-1 if axis == axis_at else 1 for axis in range(len(shape))])
    return gain


def scatter_about(own_key, extent, width, bound, cuts=(), kind=jnp.bfloat16):
    array = width * jax.random.normal(own_key, extent, jnp.float32)
    if cuts:
        array = array * steps_of(own_key, extent, cuts, -0.22, 0.18)
    return jnp.clip(array, -bound, bound).astype(kind)


def setup_inputs(seed: int = 0) -> dict:
    keys = jax.random.split(jax.random.key(seed), 11)
    hidden_in = scatter_about(keys[0], (MICRO, TOKENS, D), 1.0, 6.0, ((1, 4), (2, 4)))
    cotangent = scatter_about(keys[1], (MICRO, TOKENS, D), 1.0, 6.0, ((1, 4), (2, 4)))
    lengths = draw_lengths(jax.random.fold_in(keys[10], 71), 0)
    w_qkv = scatter_about(keys[3], (LAYERS, D, 3, D), D ** -0.5, 0.1875, ((0, 2), (3, 4)))
    w_out = scatter_about(keys[4], (LAYERS, D, D), D ** -0.5, 0.1875, ((0, 2), (1, 4)))
    w_ug = scatter_about(keys[5], (LAYERS, D, 2, FF), D ** -0.5, 0.1875, ((0, 2), (3, 4)))
    w_down = scatter_about(keys[6], (LAYERS, FF, D), FF ** -0.5, 0.09375, ((0, 2), (1, 4)))
    s_qk = jnp.clip(0.6 + 1.0 * jax.random.uniform(keys[7], (LAYERS, D), jnp.float32) ** steps_of(keys[7], (LAYERS, D), ((0, 2), (1, 4)), -0.2, 0.2), 0.6, 1.6)
    s_uv = jnp.clip(jnp.exp(math.log(2.0) - 1.3862944 * jax.random.uniform(keys[8], (LAYERS, 2, FF), jnp.float32) ** steps_of(keys[8], (LAYERS, 2, FF), ((0, 2), (2, 4)), -0.2, 0.2)), 0.5, 2.0)
    alpha = jnp.clip(0.15 + 0.45000002 * jax.random.uniform(keys[9], (LAYERS, 2, D), jnp.float32) ** steps_of(keys[9], (LAYERS, 2, D), ((0, 2), (2, 4)), -0.2, 0.2), 0.15, 0.6)
    return dict(hidden_in=hidden_in, cotangent=cotangent, lengths=lengths, w_qkv=w_qkv, w_out=w_out, w_ug=w_ug, w_down=w_down, s_qk=s_qk, s_uv=s_uv, alpha=alpha)


EPSILON = 1e-05
HIGHEST = lax.Precision.HIGHEST
NEG_LARGE = -1e+30

@jax.custom_vjp
def low(v):
    return lax.optimization_barrier(v.astype(jnp.bfloat16)).astype(jnp.float32)

@jax.custom_vjp
def low_back(v):
    return v

def low_keep(v):
    return (low(v), None)

def low_pass(kept, grad):
    return (grad,)

def back_keep(v):
    return (v, None)

def back_low(kept, grad):
    return (low(grad),)
low.defvjp(low_keep, low_pass)
low_back.defvjp(back_keep, back_low)

def mat_mul(left_op, right_op):
    return jnp.dot(left_op, right_op, precision=HIGHEST, preferred_element_type=jnp.float32)

def sphere(values):
    return values * lax.rsqrt(lax.optimization_barrier(jnp.mean(values * values, axis=-1, keepdims=True)) + EPSILON)

def seq_table(lengths_row, positions):
    seq_end = jnp.cumsum(lengths_row).astype(jnp.int32)
    seq_start = (seq_end - lengths_row).astype(jnp.int32)
    segment = lax.optimization_barrier(jnp.sum((positions[:, None] >= seq_end[None, :]).astype(jnp.int32), axis=1)).astype(jnp.int32)
    labels = jnp.arange(lengths_row.shape[0], dtype=jnp.int32)
    first_tok = lax.optimization_barrier(jnp.sum(jnp.where(segment[:, None] == labels[None, :], seq_start[None, :], 0), axis=1)).astype(jnp.int32)
    return (segment, (positions - first_tok).astype(jnp.int32))

def rope_tables(places, col_width):
    column = jnp.arange(col_width, dtype=jnp.int32) % HEAD_DIM
    half_dim = HEAD_DIM // 2
    rope_rates = 10000.0 ** (-(column % half_dim).astype(jnp.float32) / half_dim)
    angles = places.astype(jnp.float32)[:, None] * rope_rates[None, :]
    return (jnp.cos(angles), jnp.sin(angles), column < half_dim)

def partner(values, lower_half):
    half_dim = HEAD_DIM // 2
    return jnp.where(lower_half[None, :], -jnp.roll(values, -half_dim, axis=1), jnp.roll(values, half_dim, axis=1))

def head_norm(rotated, scale_vec):
    tok_count = rotated.shape[0]
    split_heads = rotated.reshape(tok_count, D // HEAD_DIM, HEAD_DIM)
    head_ratio = lax.rsqrt(lax.optimization_barrier(jnp.mean(split_heads * split_heads, axis=-1, keepdims=True)) + EPSILON)
    return (split_heads * head_ratio).reshape(tok_count, D) * scale_vec[None, :]

def attention(query, keys_n, values_n, segment):
    tok_count = query.shape[0]
    blk_len = min(512, tok_count)
    window = MAXLEN + blk_len
    head_count = D // HEAD_DIM
    q_heads = query.reshape(tok_count, head_count, HEAD_DIM)
    padding = jnp.zeros((MAXLEN, head_count, HEAD_DIM), jnp.float32)
    k_padded = jnp.concatenate([padding, keys_n.reshape(tok_count, head_count, HEAD_DIM)], axis=0)
    v_padded = jnp.concatenate([padding, values_n.reshape(tok_count, head_count, HEAD_DIM)], axis=0)
    seg_padded = jnp.concatenate([jnp.full((MAXLEN,), -1, jnp.int32), segment.astype(jnp.int32)], axis=0)

    def one_block(number):
        first_row = (number * blk_len).astype(jnp.int32)
        q_blk = lax.dynamic_slice_in_dim(q_heads, first_row, blk_len, 0)
        q_seg = lax.dynamic_slice_in_dim(segment.astype(jnp.int32), first_row, blk_len, 0)
        k_win = lax.dynamic_slice_in_dim(k_padded, first_row, window, 0)
        v_win = lax.dynamic_slice_in_dim(v_padded, first_row, window, 0)
        k_seg = lax.dynamic_slice_in_dim(seg_padded, first_row, window, 0)
        q_index = first_row + jnp.arange(blk_len, dtype=jnp.int32)
        k_index = first_row - MAXLEN + jnp.arange(window, dtype=jnp.int32)
        key_mask = (q_seg[:, None] == k_seg[None, :]) & (k_index[None, :] <= q_index[:, None])
        raw = low_back(jnp.einsum('qhd,khd->hqk', q_blk, k_win, precision=HIGHEST) / math.sqrt(HEAD_DIM))
        masked = jnp.where(key_mask[None], raw, NEG_LARGE)
        attn_prob = jax.nn.softmax(masked, axis=-1)
        return jnp.einsum('hqk,khd->qhd', low(attn_prob), v_win, precision=HIGHEST)
    blocks_out = lax.map(jax.checkpoint(one_block), jnp.arange(tok_count // blk_len, dtype=jnp.int32))
    return blocks_out.reshape(tok_count, D)

def layer(hidden, segment, places, w_qkv, w_out, w_ug, w_down, s_qk, s_uv, alpha):
    cosine, sine_tab, lower_half = rope_tables(places, D)
    qkv = low_back(mat_mul(low(hidden), w_qkv.reshape(D, 3 * D)))
    q_raw = qkv[:, :D]
    k_raw = qkv[:, D:2 * D]
    query = low(head_norm(q_raw * cosine + partner(q_raw, lower_half) * sine_tab, s_qk))
    keys_n = low(head_norm(k_raw * cosine + partner(k_raw, lower_half) * sine_tab, s_qk))
    values_n = low(qkv[:, 2 * D:])
    attended = attention(query, keys_n, values_n, segment)
    attn_raw = low_back(mat_mul(low(low_back(attended)), w_out))
    mix_one = hidden + alpha[0][None, :] * (sphere(attn_raw) - hidden)
    normed_one = sphere(mix_one)
    upgate = low_back(mat_mul(low(normed_one), w_ug.reshape(D, 2 * FF)))
    up_s = upgate[:, :FF] * s_uv[0][None, :]
    gate_s = upgate[:, FF:] * s_uv[1][None, :]
    act_b = low(up_s * jax.nn.silu(gate_s))
    mlp_raw = low_back(mat_mul(act_b, w_down))
    mix_two = normed_one + alpha[1][None, :] * (sphere(mlp_raw) - normed_one)
    return sphere(mix_two)

def reference(hidden_in, cotangent, lengths, w_qkv, w_out, w_ug, w_down, s_qk, s_uv, alpha):
    inputs = hidden_in.astype(jnp.float32)
    weights = (w_qkv.astype(jnp.float32), w_out.astype(jnp.float32), w_ug.astype(jnp.float32), w_down.astype(jnp.float32), s_qk.astype(jnp.float32), s_uv.astype(jnp.float32), alpha.astype(jnp.float32))
    positions = jnp.arange(TOKENS, dtype=jnp.int32)
    tables = [seq_table(lengths[micro_no].astype(jnp.int32), positions) for micro_no in range(MICRO)]
    checked = jax.checkpoint(layer)
    probe = jnp.zeros((LAYERS, MICRO, TOKENS, D), jnp.float32)

    def forward(probe_in, params):
        per_layer = [[] for number in range(LAYERS)]
        for micro_no in range(MICRO):
            segment, places = tables[micro_no]
            layer_in = inputs[micro_no] + probe_in[0, micro_no]
            for layer_no in range(LAYERS):
                layer_out = checked(layer_in, segment, places, *[weight_arr[layer_no] for weight_arr in params])
                per_layer[layer_no].append(low(layer_out))
                if layer_no + 1 < LAYERS:
                    layer_in = low(low_back(layer_out)) + probe_in[layer_no + 1, micro_no]
        return jnp.stack([jnp.stack(layer_list) for layer_list in per_layer])
    outputs, pull_back = jax.vjp(forward, probe, weights)
    cot_full = jnp.zeros((LAYERS, MICRO, TOKENS, D), jnp.float32).at[LAYERS - 1].set(cotangent.astype(jnp.float32))
    d_probe, d_params = pull_back(cot_full)
    return (outputs.astype(jnp.bfloat16), d_probe.astype(jnp.bfloat16), d_params[0], d_params[1], d_params[2], d_params[3], d_params[4], d_params[5], d_params[6])
```

```python
import functools
import math
import types

import jax
import jax.numpy as jnp
from jax import lax
from jax.experimental import pallas as pl
from jax.experimental.pallas import tpu as pltpu
from jax.sharding import PartitionSpec as P

D = 1024
HEAD_DIM = 64
SEQ_CAP = 4096


EPSILON = 1e-05
HIGHEST = lax.Precision.HIGHEST
NEG_LARGE = -1e30


def passed_along(array, axis, by):
    count = lax.axis_size(axis)
    return lax.ppermute(array, axis, [(i, (i + by) % count) for i in range(count)])


def from_behind(array, axis, by):
    count = lax.axis_size(axis)
    pairs = [(i, i + by) for i in range(count) if 0 <= i + by < count]
    return lax.ppermute(array, axis, pairs)


def seq_table(lengths_row, positions):
    count = lengths_row.shape[0]
    order = jnp.arange(count, dtype=jnp.int32)
    seq_end = jnp.sum(jnp.where(order[None, :] <= order[:, None], lengths_row[None, :], 0), axis=1)
    seq_start = seq_end - lengths_row
    segment = jnp.sum((positions[:, None] >= seq_end[None, :]).astype(jnp.int32), axis=1)
    labels = jnp.arange(lengths_row.shape[0], dtype=jnp.int32)
    first_tok = jnp.sum(
        jnp.where(segment[:, None] == labels[None, :], seq_start[None, :], 0), axis=1
    )
    return (segment, positions - first_tok)


def rope_tables(places, col_width):
    column = jnp.arange(col_width, dtype=jnp.int32) % HEAD_DIM
    half_dim = HEAD_DIM // 2
    rope_rates = 10000.0 ** (-(column % half_dim).astype(jnp.float32) / half_dim)
    angles = places.astype(jnp.float32)[:, None] * rope_rates[None, :]
    return (jnp.cos(angles), jnp.sin(angles), column < half_dim)


def partner(values, lower_half):
    half_dim = HEAD_DIM // 2
    return jnp.where(
        lower_half[None, :],
        -jnp.roll(values, -half_dim, axis=1),
        jnp.roll(values, half_dim, axis=1),
    )


def contract_rows(left_op, right_op):
    return lax.dot_general(
        left_op, right_op, (((0,), (0,)), ((), ())), preferred_element_type=jnp.float32
    )


def contract_cols(left_op, right_op):
    return lax.dot_general(
        left_op, right_op, (((1,), (1,)), ((), ())), preferred_element_type=jnp.float32
    )


def full_rows(columns):
    return lax.all_gather(columns, "tensor", axis=1, tiled=True)


def to_cols(partial_sum):
    return lax.psum_scatter(
        partial_sum.astype(jnp.bfloat16), "tensor", scatter_dimension=1, tiled=True
    ).astype(jnp.float32)


def grad_rows(columns):
    return lax.all_gather(columns, "tensor", axis=1, tiled=True)


def grad_cols(partial_sum):
    return lax.psum_scatter(
        partial_sum.astype(jnp.bfloat16), "tensor", scatter_dimension=1, tiled=True
    ).astype(jnp.float32)


def row_total(values):
    return lax.psum(jnp.sum(values, axis=1), "tensor")


def sphere(values):
    row_ratio = lax.rsqrt(row_total(values * values) / D + EPSILON)[:, None]
    return (values * row_ratio, row_ratio)


def sphere_back(source, row_ratio, grad_in):
    inner_sum = row_total(grad_in * source)[:, None]
    return row_ratio * grad_in - source * (row_ratio * row_ratio * row_ratio) * inner_sum / D


def pass_on(dkv_sum):
    return passed_along(dkv_sum.astype(jnp.bfloat16), "dp", 1).astype(dkv_sum.dtype)


def unchanged(previous):
    return previous


def per_device(hidden_in, cotangent, lengths, w_qkv, w_out, w_ug, w_down, s_qk, s_uv, alpha):
    micro_n = hidden_in.shape[0]
    tok_rows = hidden_in.shape[1]
    col_width = hidden_in.shape[2]
    heads_here = col_width // HEAD_DIM
    ff_here = w_down.shape[1]
    dp_ranks = lax.axis_size("dp")
    dp_rank = lax.axis_index("dp")
    longest = min(SEQ_CAP, tok_rows * dp_ranks // 2)
    reach_len = min(dp_ranks - 1, (longest + tok_rows - 2) // tok_rows)
    first_section = lax.axis_index("section") == 0
    score_div = math.sqrt(HEAD_DIM)
    qkv_mat = w_qkv[0].reshape(D, 3 * col_width)
    out_mat = w_out[0]
    ug_mat = w_ug[0].reshape(D, 2 * ff_here)
    down_mat = w_down[0]
    scale_qk = s_qk[0]
    scale_up = s_uv[0, 0]
    scale_gate = s_uv[0, 1]
    alpha_attn = alpha[0, 0]
    alpha_mlp = alpha[0, 1]
    local_rows = jnp.arange(tok_rows, dtype=jnp.int32)
    q_index = dp_rank * tok_rows + local_rows
    indicator = (
        jnp.arange(col_width, dtype=jnp.int32)[:, None] // HEAD_DIM
        == jnp.arange(heads_here, dtype=jnp.int32)[None, :]
    ).astype(jnp.float32)

    def head_sum(values):
        return jnp.dot(values, indicator, precision=HIGHEST, preferred_element_type=jnp.float32)

    def spread(small):
        return jnp.dot(small, indicator.T, precision=HIGHEST, preferred_element_type=jnp.float32)

    def block_info(lengths_row, q_segment, offset):
        source = dp_rank - offset
        k_index = source * tok_rows + local_rows
        k_segment, unused = seq_table(lengths_row, k_index)
        key_mask = (
            (k_segment[None, :] == q_segment[:, None])
            & (k_index[None, :] <= q_index[:, None])
            & (k_index[None, :] >= 0)
        )
        needed = (source * tok_rows + tok_rows - 1 >= 0) & (k_segment[tok_rows - 1] >= q_segment[0])
        return (key_mask, needed)

    def block_scores(q_heads, kv_block):
        key_heads = kv_block[:, :col_width].reshape(tok_rows, heads_here, HEAD_DIM)
        return (
            jnp.einsum("qhd,khd->hqk", q_heads, key_heads, preferred_element_type=jnp.float32)
            / score_div
        )

    def prep_back(grad_n, rotated, head_ratio, record):
        unit_vec = rotated * head_ratio
        d_scale = jnp.sum(grad_n * unit_vec, axis=0)
        d_unit = grad_n * scale_qk[None, :]
        d_rot = head_ratio * d_unit - rotated * (head_ratio * head_ratio * head_ratio) * spread(
            head_sum(d_unit * rotated) / HEAD_DIM
        )
        return (
            d_rot * record["cosine"] - partner(d_rot * record["sine_tab"], record["lower_half"]),
            d_scale,
        )

    received_in = jnp.zeros((tok_rows, col_width), jnp.bfloat16)
    records = []
    results = []
    for tick_no in range(micro_n + 1):
        early_mb = min(tick_no, micro_n - 1)
        late_mb = max(tick_no - 1, 0)
        lengths_row = jnp.where(first_section, lengths[early_mb], lengths[late_mb])
        layer_in = jnp.where(first_section, hidden_in[early_mb], received_in)
        hidden = layer_in.astype(jnp.float32)
        forward_q_segment, places = seq_table(lengths_row, q_index)
        cosine, sine_tab, lower_half = rope_tables(places, col_width)
        full_in = full_rows(hidden.astype(jnp.bfloat16))
        qkv = jnp.dot(full_in, qkv_mat, preferred_element_type=jnp.float32)
        q_raw = qkv[:, :col_width]
        k_raw = qkv[:, col_width : 2 * col_width]
        q_rot = q_raw * cosine + partner(q_raw, lower_half) * sine_tab
        k_rot = k_raw * cosine + partner(k_raw, lower_half) * sine_tab
        q_ratio = spread(lax.rsqrt(head_sum(q_rot * q_rot) / HEAD_DIM + EPSILON))
        k_ratio = spread(lax.rsqrt(head_sum(k_rot * k_rot) / HEAD_DIM + EPSILON))
        query_b = (q_rot * q_ratio * scale_qk[None, :]).astype(jnp.bfloat16)
        key_b = (k_rot * k_ratio * scale_qk[None, :]).astype(jnp.bfloat16)
        value_b = qkv[:, 2 * col_width :].astype(jnp.bfloat16)
        forward_q_heads = query_b.reshape(tok_rows, heads_here, HEAD_DIM)
        own_block = jnp.concatenate([key_b, value_b], axis=1)

        def lse_step(lse_state, kv_block, offset):
            key_mask, needed = block_info(lengths_row, forward_q_segment, offset)

            def update(previous):
                run_max, run_sum = previous
                masked = jnp.where(
                    key_mask[None], block_scores(forward_q_heads, kv_block), NEG_LARGE
                )
                new_max = jnp.maximum(run_max, jnp.max(masked, axis=2))
                exp_terms = jnp.where(key_mask[None], jnp.exp(masked - new_max[:, :, None]), 0.0)
                return (new_max, run_sum * jnp.exp(run_max - new_max) + jnp.sum(exp_terms, axis=2))

            return lax.cond(needed, update, unchanged, lse_state)

        init_state = (
            jnp.full((heads_here, tok_rows), NEG_LARGE, jnp.float32),
            jnp.zeros((heads_here, tok_rows), jnp.float32),
        )
        lse_state = lse_step(init_state, own_block, jnp.int32(0))

        def cycle_step(state_in, offset):
            kv_block, lse_now = state_in
            kv_block = from_behind(kv_block, "dp", 1)
            return ((kv_block, lse_step(lse_now, kv_block, offset)), kv_block)

        (forward_unused_block, lse_state), received = lax.scan(
            cycle_step, (own_block, lse_state), jnp.arange(1, reach_len + 1, dtype=jnp.int32)
        )
        kv_stack = jnp.concatenate([own_block[None], received], axis=0)
        forward_log_total = lse_state[0] + jnp.log(lse_state[1])

        def value_step(acc_heads, scan_item):
            kv_block, offset = scan_item
            key_mask, needed = block_info(lengths_row, forward_q_segment, offset)

            def add_values(previous):
                attn_prob = jnp.where(
                    key_mask[None],
                    jnp.exp(
                        block_scores(forward_q_heads, kv_block) - forward_log_total[:, :, None]
                    ),
                    0.0,
                ).astype(jnp.bfloat16)
                val_heads = kv_block[:, col_width:].reshape(tok_rows, heads_here, HEAD_DIM)
                return previous + jnp.einsum(
                    "hqk,khd->hqd", attn_prob, val_heads, preferred_element_type=jnp.float32
                )

            return (lax.cond(needed, add_values, unchanged, acc_heads), None)

        acc_heads, forward_unused_out = lax.scan(
            value_step,
            jnp.zeros((heads_here, tok_rows, HEAD_DIM), jnp.float32),
            (kv_stack, jnp.arange(reach_len + 1, dtype=jnp.int32)),
        )
        attended = jnp.transpose(acc_heads, (1, 0, 2)).reshape(tok_rows, col_width)
        attended_b = attended.astype(jnp.bfloat16)
        attn_raw = to_cols(jnp.dot(attended_b, out_mat, preferred_element_type=jnp.float32))
        attn_n, ratio_a = sphere(attn_raw)
        mix_one = hidden + alpha_attn[None, :] * (attn_n - hidden)
        normed_one, ratio_one = sphere(mix_one)
        inner_full = full_rows(normed_one.astype(jnp.bfloat16))
        forward_upgate = jnp.dot(inner_full, ug_mat, preferred_element_type=jnp.float32)
        forward_up_s = forward_upgate[:, :ff_here] * scale_up[None, :]
        forward_gate_s = forward_upgate[:, ff_here:] * scale_gate[None, :]
        act_b = (forward_up_s * jax.nn.silu(forward_gate_s)).astype(jnp.bfloat16)
        mlp_raw = to_cols(jnp.dot(act_b, down_mat, preferred_element_type=jnp.float32))
        mlp_n, ratio_m = sphere(mlp_raw)
        mix_two = normed_one + alpha_mlp[None, :] * (mlp_n - normed_one)
        result, ratio_two = sphere(mix_two)
        kept_blocks = own_block[None]
        forward_record = {
            "lengths_row": lengths_row,
            "q_segment": forward_q_segment,
            "cosine": cosine,
            "sine_tab": sine_tab,
            "lower_half": lower_half,
            "full_in": full_in,
            "q_rot": q_rot,
            "k_rot": k_rot,
            "q_ratio": q_ratio,
            "k_ratio": k_ratio,
            "query_b": query_b,
            "blocks": kept_blocks,
            "log_total": forward_log_total,
            "attended": attended,
            "attended_b": attended_b,
            "hidden": hidden,
            "attn_raw": attn_raw,
            "ratio_a": ratio_a,
            "attn_n": attn_n,
            "mix_one": mix_one,
            "ratio_one": ratio_one,
            "normed_one": normed_one,
            "inner_full": inner_full,
            "upgate": forward_upgate,
            "act_b": act_b,
            "mlp_raw": mlp_raw,
            "ratio_m": ratio_m,
            "mlp_n": mlp_n,
            "mix_two": mix_two,
            "ratio_two": ratio_two,
        }
        record, result = (forward_record, result)
        result_b = result.astype(jnp.bfloat16)
        records.append(record)
        results.append(result_b)
        if tick_no < micro_n:
            received_in = from_behind(result_b, "section", 1)
    layer_outputs = jnp.stack(
        [
            jnp.where(first_section, results[number], results[number + 1])
            for number in range(micro_n)
        ]
    )
    back_in = jnp.zeros((tok_rows, col_width), jnp.bfloat16)
    grad_totals = None
    back_results = []
    for tick_no in range(micro_n + 1):
        record = records[micro_n - tick_no]
        late_cot = cotangent[max(micro_n - 1 - tick_no, 0)].astype(jnp.float32)
        live_flag = jnp.where(
            first_section, 1.0 if tick_no >= 1 else 0.0, 1.0 if tick_no < micro_n else 0.0
        )
        grad_out = jnp.where(first_section, back_in.astype(jnp.float32), late_cot) * live_flag
        backward_lengths_row = record["lengths_row"]
        backward_q_segment = record["q_segment"]
        dz_two = sphere_back(record["mix_two"], record["ratio_two"], grad_out)
        d_normed = (1.0 - alpha_mlp)[None, :] * dz_two
        d_mlp_n = alpha_mlp[None, :] * dz_two
        d_alpha_mlp = jnp.sum(dz_two * (record["mlp_n"] - record["normed_one"]), axis=0)
        d_mlp = sphere_back(record["mlp_raw"], record["ratio_m"], d_mlp_n)
        d_mlp_full = grad_rows(d_mlp.astype(jnp.bfloat16))
        dw_down = contract_rows(record["act_b"], d_mlp_full)
        d_act = contract_cols(d_mlp_full, down_mat)
        upgate = record["upgate"]
        up_s = upgate[:, :ff_here] * scale_up[None, :]
        gate_s = upgate[:, ff_here:] * scale_gate[None, :]
        gate_sig = jax.nn.sigmoid(gate_s)
        d_up = d_act * gate_s * gate_sig
        d_gate = d_act * up_s * gate_sig * (1.0 + gate_s * (1.0 - gate_sig))
        d_scale_up = jnp.sum(d_up * upgate[:, :ff_here], axis=0)
        d_scale_gate = jnp.sum(d_gate * upgate[:, ff_here:], axis=0)
        d_upgate = jnp.concatenate(
            [d_up * scale_up[None, :], d_gate * scale_gate[None, :]], axis=1
        ).astype(jnp.bfloat16)
        dw_ug = contract_rows(record["inner_full"], d_upgate)
        d_normed = d_normed + grad_cols(contract_cols(d_upgate, ug_mat))
        dz_one = sphere_back(record["mix_one"], record["ratio_one"], d_normed)
        d_hidden = (1.0 - alpha_attn)[None, :] * dz_one
        d_attn_n = alpha_attn[None, :] * dz_one
        d_alpha_attn = jnp.sum(dz_one * (record["attn_n"] - record["hidden"]), axis=0)
        d_attn = sphere_back(record["attn_raw"], record["ratio_a"], d_attn_n)
        d_attn_full = grad_rows(d_attn.astype(jnp.bfloat16))
        dw_out = contract_rows(record["attended_b"], d_attn_full)
        d_attended = contract_cols(d_attn_full, out_mat).astype(jnp.bfloat16)
        row_delta = jnp.transpose(head_sum(d_attended.astype(jnp.float32) * record["attended"]))
        do_heads = d_attended.reshape(tok_rows, heads_here, HEAD_DIM)
        backward_q_heads = record["query_b"].reshape(tok_rows, heads_here, HEAD_DIM)
        log_total = record["log_total"]

        def block_grads(dq_now, kv_block, offset):
            key_mask, needed = block_info(backward_lengths_row, backward_q_segment, offset)

            def compute(previous):
                key_heads = kv_block[:, :col_width].reshape(tok_rows, heads_here, HEAD_DIM)
                val_heads = kv_block[:, col_width:].reshape(tok_rows, heads_here, HEAD_DIM)
                attn_prob = jnp.where(
                    key_mask[None],
                    jnp.exp(block_scores(backward_q_heads, kv_block) - log_total[:, :, None]),
                    0.0,
                )
                d_prob = jnp.einsum(
                    "qhd,khd->hqk", do_heads, val_heads, preferred_element_type=jnp.float32
                )
                d_val = jnp.einsum(
                    "hqk,qhd->khd",
                    attn_prob.astype(jnp.bfloat16),
                    do_heads,
                    preferred_element_type=jnp.float32,
                )
                d_score = (attn_prob * (d_prob - row_delta[:, :, None])).astype(jnp.bfloat16)
                new_dq = (
                    previous
                    + jnp.einsum(
                        "hqk,khd->hqd", d_score, key_heads, preferred_element_type=jnp.float32
                    )
                    / score_div
                )
                d_key = (
                    jnp.einsum(
                        "hqk,qhd->khd",
                        d_score,
                        backward_q_heads,
                        preferred_element_type=jnp.float32,
                    )
                    / score_div
                )
                return (
                    jnp.concatenate(
                        [d_key.reshape(tok_rows, col_width), d_val.reshape(tok_rows, col_width)],
                        axis=1,
                    ),
                    new_dq,
                )

            def skipped(previous):
                return (jnp.zeros((tok_rows, 2 * col_width), jnp.float32), previous)

            return lax.cond(needed, compute, skipped, dq_now)

        own_part, dq_acc = block_grads(
            jnp.zeros((heads_here, tok_rows, HEAD_DIM), jnp.float32),
            record["blocks"][0],
            jnp.int32(0),
        )
        offsets = jnp.arange(1, reach_len + 1, dtype=jnp.int32)

        def again_step(state_in, offset):
            dkv_sum, kv_block, dq_now = state_in
            dkv_sum = pass_on(dkv_sum)
            kv_block = from_behind(kv_block, "dp", 1)
            dkv_part, dq_now = block_grads(dq_now, kv_block, offset)
            return ((dkv_sum + dkv_part, kv_block, dq_now), None)

        (dkv_sum, unused_block, dq_acc), unused_out = lax.scan(
            again_step, (own_part, record["blocks"][0], dq_acc), offsets
        )
        dkv_home = passed_along(dkv_sum.astype(jnp.bfloat16), "dp", -reach_len).astype(
            dkv_sum.dtype
        )
        dq_full = jnp.transpose(dq_acc, (1, 0, 2)).reshape(tok_rows, col_width)
        dq_raw, ds_query = prep_back(dq_full, record["q_rot"], record["q_ratio"], record)
        dk_raw, ds_key = prep_back(
            dkv_home[:, :col_width], record["k_rot"], record["k_ratio"], record
        )
        d_qkv = jnp.concatenate([dq_raw, dk_raw, dkv_home[:, col_width:]], axis=1).astype(
            jnp.bfloat16
        )
        dw_qkv = contract_rows(record["full_in"], d_qkv)
        d_hidden = d_hidden + grad_cols(contract_cols(d_qkv, qkv_mat))
        grads = (
            dw_qkv.reshape(D, 3, col_width),
            dw_out,
            dw_ug.reshape(D, 2, ff_here),
            dw_down,
            ds_query + ds_key,
            jnp.stack([d_scale_up, d_scale_gate]),
            jnp.stack([d_alpha_attn, d_alpha_mlp]),
        )
        d_hidden, grads = (d_hidden, grads)
        grad_b = d_hidden.astype(jnp.bfloat16)
        back_results.append(grad_b)
        grad_totals = grads if grad_totals is None else jax.tree.map(jnp.add, grad_totals, grads)
        if tick_no < micro_n:
            back_in = from_behind(grad_b, "section", -1)
    input_grads = jnp.stack(
        [
            jnp.where(
                first_section, back_results[micro_n - number], back_results[micro_n - 1 - number]
            )
            for number in range(micro_n)
        ]
    )
    summed = (
        lax.psum_scatter(
            grad_totals[0].astype(jnp.bfloat16), "dp", scatter_dimension=0, tiled=True
        ).astype(jnp.float32),
        lax.psum_scatter(
            grad_totals[1].astype(jnp.bfloat16), "dp", scatter_dimension=0, tiled=True
        ).astype(jnp.float32),
        lax.psum_scatter(
            grad_totals[2].astype(jnp.bfloat16), "dp", scatter_dimension=0, tiled=True
        ).astype(jnp.float32),
        lax.psum_scatter(
            grad_totals[3].astype(jnp.bfloat16), "dp", scatter_dimension=0, tiled=True
        ).astype(jnp.float32),
        lax.psum_scatter(
            grad_totals[4].astype(jnp.bfloat16), "dp", scatter_dimension=0, tiled=True
        ).astype(jnp.float32),
        lax.psum_scatter(
            grad_totals[5].astype(jnp.bfloat16), "dp", scatter_dimension=1, tiled=True
        ).astype(jnp.float32),
        lax.psum_scatter(
            grad_totals[6].astype(jnp.bfloat16), "dp", scatter_dimension=1, tiled=True
        ).astype(jnp.float32),
    )
    return (
        layer_outputs[None],
        input_grads[None],
        summed[0][None],
        summed[1][None],
        summed[2][None],
        summed[3][None],
        summed[4][None],
        summed[5][None],
        summed[6][None],
    )


MESH = pl.DeviceIdType.MESH
MICRO = 2
F32 = jnp.float32
BF16 = jnp.bfloat16


def mul(left_op, right_op):
    return jnp.dot(left_op, right_op, preferred_element_type=F32)


def remote(src, dst, send_sem, recv_sem, device):
    return pltpu.make_async_remote_copy(
        src_ref=src, dst_ref=dst, send_sem=send_sem, recv_sem=recv_sem, device_id=device, device_id_type=MESH
    )


def ball(values, width):
    ratio = lax.rsqrt(jnp.sum(values * values, axis=1, keepdims=True) / width + EPSILON)
    return values * ratio, ratio


def ball_back(source, ratio, grad_in, width):
    inner = jnp.sum(grad_in * source, axis=1, keepdims=True)
    return ratio * grad_in - source * (ratio * ratio * ratio) * (inner / width)


def buffers(nt, nz, rows, width, cols, hidden, shard, section, chunk):
    vmem, dma = pltpu.VMEM, pltpu.SemaphoreType.DMA
    pair = 2 * rows
    return dict(
        wq=vmem((2, 3, width, cols), BF16),
        wo=vmem((2, cols, width), BF16),
        wu=vmem((2, 2, width, hidden), BF16),
        wd=vmem((2, hidden, width), BF16),
        par=vmem((2, 8, hidden), F32),
        alp=vmem((2, 8, width), F32),
        full_in=vmem((2, rows, width), BF16),
        mid_full=vmem((2, rows, width), BF16),
        dml_full=vmem((2, rows, width), BF16),
        dat_full=vmem((2, rows, width), BF16),
        fi_p=vmem((rows, width), BF16),
        at_p=vmem((rows, cols), BF16),
        da_p=vmem((rows, width), BF16),
        dq_p=vmem((rows, 3 * cols), BF16),
        xa=vmem((nt, nz * 2 * shard, width), BF16),
        da=vmem((nt, nz * 2 * shard, width), BF16),
        kv=vmem((2, pair, 2 * cols), BF16),
        dkv_f=vmem((pair, 2 * cols), F32),
        dkv_s=vmem((2, rows, 2 * cols), BF16),
        dkv_r=vmem((2, rows, 2 * cols), BF16),
        rs_s=vmem((8, rows, width), BF16),
        rs_r=vmem((8, nt - 1, shard, width), BF16),
        rot=vmem((2, 2, rows, cols), F32),
        rat=vmem((2, 2, rows, cols), F32),
        qb=vmem((2, rows, cols), BF16),
        prob=vmem((2, cols // HEAD_DIM, rows, pair), F32),
        at=vmem((2, rows, cols), BF16),
        araw=vmem((2, shard, width), F32),
        mraw=vmem((2, shard, width), F32),
        mid=vmem((2, shard, width), F32),
        zone=vmem((2, shard, width), F32),
        ztwo=vmem((2, shard, width), F32),
        up=vmem((2, rows, hidden), F32),
        gate=vmem((2, rows, hidden), F32),
        act=vmem((rows, hidden), BF16),
        duv=vmem((2, rows, hidden), BF16),
        dqkv=vmem((2, rows, 3 * cols), BF16),
        cot_rows=vmem((shard, width), BF16),
        out_s=vmem((2, shard, width), BF16),
        ig_s=vmem((2, shard, width), BF16),
        cosb=vmem((rows, cols), F32),
        sinb=vmem((rows, cols), F32),
        bias=vmem((rows, pair), F32),
        blk=vmem((cols, cols), BF16),
        al_s=vmem((2, 8, width), F32),
        al_r=vmem((2, nt - 1, 8, cols), F32),
        small=vmem((2, 8, cols), F32),
        sm_r=vmem((nz, 2, 8, cols), F32),
        wq_s=vmem((nz - 1, section, 3 * cols), BF16),
        wq_r=vmem((nz - 1, section, 3 * cols), BF16),
        wo_f=vmem((cols, width), F32),
        wo_s=vmem((cols, width), BF16),
        wo_r=vmem((nz - 1, chunk, width), BF16),
        act_b=vmem((nz * 2 * shard, hidden), BF16),
        suv_b=vmem((2, hidden), F32),
        acc=vmem((2, section, hidden), F32),
        w_l=dma((2, 4)), w_rs=dma((4,)),
        par_l=dma((2,)), par_s=dma((1,)),
        alp_r=dma((2, nt)), alp_s=dma((2, nt)),
        hid_r=dma((nt,)), hid_s=dma((2, nt)),
        cot_r=dma((nt,)), cot_s=dma((2, nt)),
        fi_rs=dma((2,)), at_rs=dma((2,)), dap_rs=dma((2,)), dq_rs=dma((2,)),
        kv_rs=dma((2, 2)), dkv_rs=dma((2, 2)),
        ag_ss=dma((7, nt - 1)), ag_rr=dma((7, nt - 1)),
        rs_ss=dma((8, nt - 1)), rs_rr=dma((8, nt - 1)),
        xa_r=dma((nz, 2)), xa_ss=dma((2, nz)),
        da_r=dma((nz, 2)), da_ss=dma((2, nz)),
        xf_ss=dma((nt - 1,)), xf_rr=dma((nt - 1,)), df_ss=dma((nt - 1,)), df_rr=dma((nt - 1,)),
        lo_ss=dma((2, nt)), lo_r=dma((2, nt)),
        ig_ss=dma((2, nt)), ig_r=dma((2, nt)),
        al_ss=dma((2, nt - 1)), al_rr=dma((2, nt - 1)),
        sm_ss=dma((2, nz)), sm_rr=dma((nz, 2)),
        wq_ss=dma((nz - 1,)), wq_rr=dma((nz - 1,)),
        wo_ss=dma((nz - 1,)), wo_rr=dma((nz - 1,)),
    )


def fused_kernel(names, nt, nz, *refs):
    hid, cot, lens, wq_in, wo_in, wu_in, wd_in, par_in, rates = refs[:9]
    lo, ig, gq, go, gu, gd, gsqk, gsuv, gal = refs[9:18]
    b = types.SimpleNamespace(**dict(zip(names, refs[18:])))
    rows, width = b.full_in.shape[1:]
    cols, hidden = b.qb.shape[2], b.wd.shape[1]
    shard = b.mid.shape[1]
    heads = cols // HEAD_DIM
    pair = 2 * rows
    section_rows = width // nz
    chunk = cols // nz
    tile = 512
    s, t, z = lax.axis_index("section"), lax.axis_index("tensor"), lax.axis_index("dp")
    p = lax.rem(z, 2)
    base = z - p
    peer = (1 - s, t, z)
    pending = []

    def around(k):
        return lax.rem(t + k, nt)

    def along(k):
        return lax.rem(z + k, nz)

    def later(copy, when=None):
        pending.append((copy, when))

    def lanes(index, size):
        return pl.ds(pl.multiple_of(index * size, size), size)

    weights = [(wq_in, b.wq), (wo_in, b.wo), (wu_in, b.wu), (wd_in, b.wd)]
    for i, (src, dst) in enumerate(weights):
        pltpu.make_async_copy(src, dst.at[s], b.w_l.at[s, i]).start()
    pltpu.make_async_copy(par_in.at[:, pl.ds(0, hidden)], b.par.at[s], b.par_l.at[s]).start()

    barrier = pltpu.get_barrier_semaphore()
    greeted = 0
    for dz in range(2):
        for dt in range(nt):
            for dc in range(2):
                if dz or dt or dc:
                    device = (lax.rem(s + dc, 2), around(dt), base + lax.rem(p + dz, 2))
                    pl.semaphore_signal(barrier, inc=1, device_id=device, device_id_type=MESH)
                    greeted += 1
    for dz in range(2, nz):
        for dc in range(2):
            device = (lax.rem(s + dc, 2), t, lax.rem(base + dz, nz))
            pl.semaphore_signal(barrier, inc=1, device_id=device, device_id_type=MESH)
            greeted += 1
    pl.semaphore_wait(barrier, greeted)

    is_source = s == p
    for src, rs, ss in ((hid, b.hid_r, b.hid_s), (cot, b.cot_r, b.cot_s)):
        for dz in range(2):
            to_mb = lax.rem(p + dz, 2)
            for dt in range(nt):
                to_t = around(dt)
                if src is hid:
                    piece, place = src.at[to_mb], b.full_in.at[0, :, lanes(t, cols)]
                else:
                    piece = src.at[to_mb, pl.ds(pl.multiple_of(to_t * shard, shard), shard), :]
                    place = b.cot_rows.at[:, lanes(t, cols)]
                if dz == 0 and dt == 0:

                    @pl.when(is_source)
                    def _(piece=piece, place=place, rs=rs):
                        pltpu.make_async_copy(piece, place, rs.at[0]).start()
                else:
                    copy = remote(piece, place, ss.at[dz, dt], rs.at[dt], (s, to_t, base + to_mb))
                    pl.when(is_source)(copy.start)
                    later(copy, is_source)
        if src is hid:
            copy = remote(par_in.at[:, pl.ds(0, hidden)], b.par.at[s], b.par_s.at[0], b.par_l.at[s], peer)
            copy.start()
            later(copy)
            alp_src, alp_dst = par_in.at[:, pl.ds(hidden, cols)], b.alp.at[s, :, lanes(t, cols)]
            for dc in range(2):
                for dt in range(nt):
                    if dc == 0 and dt == 0:
                        pltpu.make_async_copy(alp_src, alp_dst, b.alp_r.at[s, 0]).start()
                    else:
                        copy = remote(alp_src, alp_dst, b.alp_s.at[dc, dt], b.alp_r.at[s, dt], (lax.rem(s + dc, 2), around(dt), z))
                        copy.start()
                        later(copy)
            for i, (src_w, dst_w) in enumerate(weights):
                copy = remote(src_w, dst_w.at[s], b.w_rs.at[i], b.w_l.at[s, i], peer)
                copy.start()
                later(copy)

    def wait_weight(layer, i):
        src_w, dst_w = weights[i]
        pltpu.make_async_copy(src_w, dst_w.at[layer], b.w_l.at[layer, i]).wait()

    token0 = (base // 2) * pair
    pos_q = token0 + s * rows + lax.broadcasted_iota(jnp.int32, (rows, 1), 0)
    pos_k = token0 + lax.broadcasted_iota(jnp.int32, (1, pair), 1)

    def sequences(pos):
        seg = jnp.zeros_like(pos)
        first = jnp.zeros_like(pos)
        end = jnp.int32(0)
        for i in range(lens.shape[1]):
            end = end + lens[p, i]
            past = pos >= end
            seg = seg + past.astype(jnp.int32)
            first = jnp.where(past, end, first)
        return seg, pos - first

    seg_q, place_q = sequences(pos_q)
    seg_k, _ = sequences(pos_k)
    allowed = (seg_q == seg_k) & (pos_k <= pos_q)
    b.bias[...] = jnp.where(allowed, 0.0, NEG_LARGE)
    angle = place_q.astype(F32) * rates[...]
    b.cosb[...] = jnp.cos(angle)
    b.sinb[...] = jnp.sin(angle)
    col = lax.broadcasted_iota(jnp.int32, (1, cols), 1)
    lower = (col & (HEAD_DIM // 2)) == 0
    head_of = lax.shift_right_logical(col, 6)
    head_row = lax.shift_right_logical(lax.broadcasted_iota(jnp.int32, (cols, 1), 0), 6)
    b.blk[...] = jnp.where(head_row == head_of, 1.0, 0.0).astype(BF16)
    picks = [jnp.where(head_of == h, 1.0, 0.0) for h in range(heads)]
    b.al_s[...] = jnp.zeros_like(b.al_s)
    b.small[...] = jnp.zeros_like(b.small)

    def partner_cols(x):
        half = HEAD_DIM // 2
        return jnp.where(lower, -pltpu.roll(x, cols - half, 1), pltpu.roll(x, half, 1))

    def head_total(x):
        high = x.astype(BF16)
        low = (x - high.astype(F32)).astype(BF16)
        return mul(high, b.blk[...]) + mul(low, b.blk[...])

    def gather(stage, ref):
        mine = ref.at[pl.ds(pl.multiple_of(t * shard, shard), shard), :]
        for k in range(1, nt):
            copy = remote(mine, mine, b.ag_ss.at[stage, k - 1], b.ag_rr.at[stage, k - 1], (s, around(k), z))
            copy.start()
            later(copy)

    def gather_wait(stage, ref):
        for k in range(1, nt):
            theirs = ref.at[pl.ds(pl.multiple_of(around(nt - k) * shard, shard), shard), :]
            remote(theirs, theirs, b.ag_ss.at[stage, k - 1], b.ag_rr.at[stage, k - 1], (s, around(k), z)).wait_recv()

    def scatter(stage):
        for k in range(1, nt):
            piece = b.rs_s.at[stage, pl.ds(pl.multiple_of(around(k) * shard, shard), shard), :]
            copy = remote(piece, b.rs_r.at[stage, k - 1], b.rs_ss.at[stage, k - 1], b.rs_rr.at[stage, k - 1], (s, around(k), z))
            copy.start()
            later(copy)

    def scatter_wait(stage):
        total = b.rs_s[stage, pl.ds(pl.multiple_of(t * shard, shard), shard), :].astype(F32)
        for k in range(1, nt):
            place = b.rs_r.at[stage, k - 1]
            remote(place, place, b.rs_ss.at[stage, k - 1], b.rs_rr.at[stage, k - 1], (s, around(k), z)).wait_recv()
            total = total + place[...].astype(F32)
        return total

    slot = pl.ds(pl.multiple_of((z * 2 + s) * shard, shard), shard)

    def my_rows(ref):
        return ref.at[pl.ds(pl.multiple_of(t * shard, shard), shard), :]

    def to_owner(layer, ref, place_of, send_sems, recv_sems):
        for k in range(nz):
            copy = remote(ref, place_of, send_sems.at[layer, k], recv_sems.at[k, s], (layer, t, along(k)))
            if k == 0:

                @pl.when(s == layer)
                def _():
                    pltpu.make_async_copy(ref, place_of, recv_sems.at[0, s]).start()

                pl.when(s != layer)(copy.start)
                later(copy, s != layer)
            else:
                copy.start()
                later(copy)

    def bundle(layer, ref, recv_sems, fwd_ss, fwd_rr):
        @pl.when(s == layer)
        def _():
            for k in range(nz):
                for core in range(2):
                    row = pl.multiple_of((along(nz - k) * 2 + core) * shard, shard)
                    place = ref.at[t, pl.ds(row, shard), :]
                    pltpu.make_async_copy(place, place, recv_sems.at[k, core]).wait()

        for k in range(1, nt):
            copy = remote(ref.at[t], ref.at[t], fwd_ss.at[k - 1], fwd_rr.at[k - 1], (s, around(k), z))
            pl.when(s == layer)(copy.start)
            later(copy, s == layer)

    def to_output(layer, ref, out, send_sems, recv_sems):
        to_z = base + s
        place = out.at[p, pl.ds(pl.multiple_of(t * shard, shard), shard), :]
        for k in range(nt):
            to_t = around(k)
            piece = ref.at[:, lanes(to_t, cols)]
            copy = remote(piece, place, send_sems.at[layer, k], recv_sems.at[p, k], (layer, to_t, to_z))
            if k == 0:
                here = (s == layer) & (to_z == z)

                @pl.when(here)
                def _(piece=piece):
                    pltpu.make_async_copy(piece, place, recv_sems.at[p, 0]).start()

                away = jnp.logical_not(here)
                pl.when(away)(copy.start)
                later(copy, away)
            else:
                copy.start()
                later(copy)

    for layer in range(2):
        full_in = b.full_in.at[layer]
        if layer == 0:
            for dt in range(nt):
                place = b.full_in.at[0, :, lanes(around(nt - dt), cols)]
                pltpu.make_async_copy(hid.at[0], place, b.hid_r.at[dt]).wait()
            for src_core in range(2):
                pltpu.make_async_copy(par_in.at[:, pl.ds(0, hidden)], b.par.at[src_core], b.par_l.at[src_core]).wait()
                for dt in range(nt):
                    place = b.alp.at[src_core, :, lanes(around(nt - dt), cols)]
                    pltpu.make_async_copy(par_in.at[:, pl.ds(hidden, cols)], place, b.alp_r.at[src_core, dt]).wait()
        else:
            gather_wait(6, full_in)
            bundle(0, b.xa, b.xa_r, b.xf_ss, b.xf_rr)
        copy = remote(full_in, b.fi_p, b.fi_rs.at[0], b.fi_rs.at[1], peer)
        pl.when(s != layer)(copy.start)
        later(copy, s != layer)
        scale_qk = b.par[layer, 2:3, 0:cols]
        wait_weight(layer, 0)
        x = full_in[...]
        own = pl.ds(pl.multiple_of(s * rows, rows), rows)
        for i in range(2):
            raw = mul(x, b.wq[layer, i])
            rotated = raw * b.cosb[...] + partner_cols(raw) * b.sinb[...]
            ratio = lax.rsqrt(head_total(rotated * rotated) / HEAD_DIM + EPSILON)
            b.rot[layer, i] = rotated
            b.rat[layer, i] = ratio
            normed = (rotated * ratio * scale_qk).astype(BF16)
            if i == 0:
                b.qb[layer] = normed
            else:
                b.kv[layer, own, 0:cols] = normed
        b.kv[layer, own, cols : 2 * cols] = mul(x, b.wq[layer, 2]).astype(BF16)
        mine = b.kv.at[layer, own, :]
        copy = remote(mine, mine, b.kv_rs.at[layer, 0], b.kv_rs.at[layer, 1], peer)
        copy.start()
        later(copy)
        copy.wait_recv()
        att = jnp.zeros((rows, cols), F32)
        for h in range(heads):
            q_h = (b.qb[layer].astype(F32) * picks[h]).astype(BF16)
            scores = contract_cols(q_h, b.kv[layer, :, 0:cols]) * (1.0 / math.sqrt(HEAD_DIM)) + b.bias[...]
            top = jnp.max(scores, axis=1, keepdims=True)
            terms = jnp.exp(scores - top)
            prob = terms / jnp.sum(terms, axis=1, keepdims=True)
            b.prob[layer, h] = prob
            att = att + picks[h] * mul(prob.astype(BF16), b.kv[layer, :, cols : 2 * cols])
        b.at[layer] = att.astype(BF16)
        wait_weight(layer, 1)
        for n in range(0, width, tile):
            b.rs_s[layer, :, n : n + tile] = mul(b.at[layer], b.wo[layer, :, n : n + tile]).astype(BF16)
        scatter(layer)
        hin = my_rows(full_in)[...].astype(F32)
        rate_a = b.alp[layer, 0:1, :]
        rate_m = b.alp[layer, 1:2, :]
        araw = scatter_wait(layer)
        b.araw[layer] = araw
        zone = hin + rate_a * (ball(araw, width)[0] - hin)
        b.zone[layer] = zone
        mid = ball(zone, width)[0]
        b.mid[layer] = mid
        mid_full = b.mid_full.at[layer]
        my_rows(mid_full)[...] = mid.astype(BF16)
        gather(layer, mid_full)
        to_owner(layer, my_rows(mid_full), b.xa.at[t, slot, :], b.xa_ss, b.xa_r)
        wait_weight(layer, 2)
        wait_weight(layer, 3)
        gather_wait(layer, mid_full)
        x = mid_full[...]
        for n in range(0, hidden, tile):
            cut = slice(n, n + tile)
            up = mul(x, b.wu[layer, 0, :, cut])
            gate = mul(x, b.wu[layer, 1, :, cut])
            b.up[layer, :, cut] = up
            b.gate[layer, :, cut] = gate
            gate_s = gate * b.par[layer, 1:2, cut]
            b.act[:, cut] = (up * b.par[layer, 0:1, cut] * (gate_s / (1.0 + jnp.exp(-gate_s)))).astype(BF16)
        for n in range(0, width, tile):
            b.rs_s[2 + layer, :, n : n + tile] = mul(b.act[...], b.wd[layer, :, n : n + tile]).astype(BF16)
        scatter(2 + layer)
        mraw = scatter_wait(2 + layer)
        b.mraw[layer] = mraw
        ztwo = mid + rate_m * (ball(mraw, width)[0] - mid)
        b.ztwo[layer] = ztwo
        b.out_s[layer] = ball(ztwo, width)[0].astype(BF16)
        if layer == 0:
            my_rows(b.full_in.at[1])[...] = b.out_s[0]
            gather(6, b.full_in.at[1])
        to_output(layer, b.out_s.at[layer], lo, b.lo_ss, b.lo_r)

    for dt in range(nt):
        place = b.cot_rows.at[:, lanes(around(nt - dt), cols)]
        pltpu.make_async_copy(cot.at[0, pl.ds(0, shard), :], place, b.cot_r.at[dt]).wait()
    grad_out = b.cot_rows[...].astype(F32)
    for layer in (1, 0):
        own = pl.ds(pl.multiple_of(s * rows, rows), rows)
        other = pl.ds(pl.multiple_of((1 - s) * rows, rows), rows)
        rate_a = b.alp[layer, 0:1, :]
        rate_m = b.alp[layer, 1:2, :]
        scale_qk = b.par[layer, 2:3, 0:cols]
        mid = b.mid[layer]
        mraw_n, ratio_m = ball(b.mraw[layer], width)
        ratio_two = ball(b.ztwo[layer], width)[1]
        d_two = ball_back(b.ztwo[layer], ratio_two, grad_out, width)
        d_mid = (1.0 - rate_m) * d_two
        b.al_s[layer, 1:2, :] = jnp.sum(d_two * (mraw_n - mid), axis=0, keepdims=True)
        dml_full = b.dml_full.at[layer]
        my_rows(dml_full)[...] = ball_back(b.mraw[layer], ratio_m, rate_m * d_two, width).astype(BF16)
        gather(2 + layer, dml_full)
        to_owner(layer, my_rows(dml_full), b.da.at[t, slot, :], b.da_ss, b.da_r)
        gather_wait(2 + layer, dml_full)
        if layer == 1:
            bundle(1, b.xa, b.xa_r, b.xf_ss, b.xf_rr)
        x = dml_full[...]
        for n in range(0, hidden, tile):
            cut = slice(n, n + tile)
            d_act = contract_cols(x, b.wd[layer, cut, :])
            scale_up, scale_gate = b.par[layer, 0:1, cut], b.par[layer, 1:2, cut]
            up_s = b.up[layer, :, cut] * scale_up
            gate_s = b.gate[layer, :, cut] * scale_gate
            sig = 1.0 / (1.0 + jnp.exp(-gate_s))
            b.duv[0, :, cut] = (d_act * gate_s * sig * scale_up).astype(BF16)
            b.duv[1, :, cut] = (d_act * up_s * sig * (1.0 + gate_s * (1.0 - sig)) * scale_gate).astype(BF16)
        for n in range(0, width, tile):
            cut = slice(n, n + tile)
            part = contract_cols(b.duv[0], b.wu[layer, 0, cut, :]) + contract_cols(b.duv[1], b.wu[layer, 1, cut, :])
            b.rs_s[4 + layer, :, cut] = part.astype(BF16)
        scatter(4 + layer)
        hin = my_rows(b.full_in.at[layer])[...].astype(F32)
        araw_n, ratio_a = ball(b.araw[layer], width)
        ratio_one = ball(b.zone[layer], width)[1]
        d_mid = d_mid + scatter_wait(4 + layer)
        d_one = ball_back(b.zone[layer], ratio_one, d_mid, width)
        b.al_s[layer, 0:1, :] = jnp.sum(d_one * (araw_n - hin), axis=0, keepdims=True)
        dat_full = b.dat_full.at[layer]
        my_rows(dat_full)[...] = ball_back(b.araw[layer], ratio_a, rate_a * d_one, width).astype(BF16)
        gather(4 + layer, dat_full)
        for k in range(1, nt):
            copy = remote(b.al_s.at[layer, :, lanes(around(k), cols)], b.al_r.at[layer, k - 1], b.al_ss.at[layer, k - 1], b.al_rr.at[layer, k - 1], (s, around(k), z))
            copy.start()
            later(copy)
        gather_wait(4 + layer, dat_full)
        bundle(layer, b.da, b.da_r, b.df_ss, b.df_rr)
        for src_v, dst_v, sems in ((dat_full, b.da_p, b.dap_rs), (b.at.at[layer], b.at_p, b.at_rs)):
            copy = remote(src_v, dst_v, sems.at[0], sems.at[1], peer)
            pl.when(s != layer)(copy.start)
            later(copy, s != layer)
        d_att = contract_cols(dat_full[...], b.wo[layer])
        dq = jnp.zeros((rows, cols), F32)
        dk = jnp.zeros((pair, cols), F32)
        dv = jnp.zeros((pair, cols), F32)
        for h in range(heads):
            d_att_h = (d_att * picks[h]).astype(BF16)
            q_h = (b.qb[layer].astype(F32) * picks[h]).astype(BF16)
            prob = b.prob[layer, h]
            d_prob = contract_cols(d_att_h, b.kv[layer, :, cols : 2 * cols])
            d_score = (prob * (d_prob - jnp.sum(prob * d_prob, axis=1, keepdims=True))).astype(BF16)
            dv = dv + contract_rows(prob.astype(BF16), d_att_h)
            dq = dq + picks[h] * mul(d_score, b.kv[layer, :, 0:cols])
            dk = dk + contract_rows(d_score, q_h)
        b.dkv_f[:, 0:cols] = dk * (1.0 / math.sqrt(HEAD_DIM))
        b.dkv_f[:, cols : 2 * cols] = dv
        b.dkv_s[layer] = b.dkv_f[other, :].astype(BF16)
        copy = remote(b.dkv_s.at[layer], b.dkv_r.at[layer], b.dkv_rs.at[layer, 0], b.dkv_rs.at[layer, 1], peer)
        copy.start()
        later(copy)
        d_scale = jnp.zeros((1, cols), F32)
        for i in range(2):
            if i == 0:
                grad_n = dq * (1.0 / math.sqrt(HEAD_DIM))
            else:
                copy.wait_recv()
                grad_n = b.dkv_f[own, 0:cols] + b.dkv_r[layer, :, 0:cols].astype(F32)
            rotated, ratio = b.rot[layer, i], b.rat[layer, i]
            d_scale = d_scale + jnp.sum(grad_n * rotated * ratio, axis=0, keepdims=True)
            d_unit = grad_n * scale_qk
            d_rot = ratio * d_unit - rotated * (ratio * ratio * ratio) * (head_total(d_unit * rotated) / HEAD_DIM)
            d_raw = d_rot * b.cosb[...] - partner_cols(d_rot * b.sinb[...])
            b.dqkv[layer, :, i * cols : (i + 1) * cols] = d_raw.astype(BF16)
        d_val = b.dkv_f[own, cols : 2 * cols] + b.dkv_r[layer, :, cols : 2 * cols].astype(F32)
        b.dqkv[layer, :, 2 * cols : 3 * cols] = d_val.astype(BF16)
        for n in range(0, width, tile):
            part = contract_cols(b.dqkv[layer, :, 0:cols], b.wq[layer, 0, n : n + tile, :])
            for i in range(1, 3):
                part = part + contract_cols(b.dqkv[layer, :, i * cols : (i + 1) * cols], b.wq[layer, i, n : n + tile, :])
            b.rs_s[6 + layer, :, n : n + tile] = part.astype(BF16)
        scatter(6 + layer)
        copy = remote(b.dqkv.at[layer], b.dq_p, b.dq_rs.at[0], b.dq_rs.at[1], peer)
        pl.when(s != layer)(copy.start)
        later(copy, s != layer)
        total = b.al_s[layer, :, lanes(t, cols)]
        for k in range(1, nt):
            place = b.al_r.at[layer, k - 1]
            remote(place, place, b.al_ss.at[layer, k - 1], b.al_rr.at[layer, k - 1], peer).wait_recv()
            total = total + place[...]
        b.small[layer] = total
        b.small[layer, 2:3, :] = d_scale
        to_owner(layer, b.small.at[layer], b.sm_r.at[lax.rem(z, nz), s], b.sm_ss, b.sm_rr)

        @pl.when(s == layer)
        def _(layer=layer):
            for dst_v, sems in ((b.fi_p, b.fi_rs), (b.da_p, b.dap_rs), (b.at_p, b.at_rs), (b.dq_p, b.dq_rs)):
                remote(dst_v, dst_v, sems.at[0], sems.at[1], peer).wait_recv()
            for k in (1, 2, 3, 0):
                cut = lanes(along(k), section_rows)
                part = contract_rows(b.full_in[layer, :, cut], b.dqkv[layer]) + contract_rows(b.fi_p[:, cut], b.dq_p[...])
                if k:
                    b.wq_s[k - 1] = part.astype(BF16)
                    remote(b.wq_s.at[k - 1], b.wq_r.at[k - 1], b.wq_ss.at[k - 1], b.wq_rr.at[k - 1], (layer, t, along(k))).start()
                else:
                    for i in range(3):
                        gq[i] = part[:, i * cols : (i + 1) * cols]
            for n in range(0, width, tile):
                cut = slice(n, n + tile)
                part = contract_rows(b.at[layer], b.dat_full[layer, :, cut]) + contract_rows(b.at_p[...], b.da_p[:, cut])
                b.wo_f[:, cut] = part
                b.wo_s[:, cut] = part.astype(BF16)
            for k in range(1, nz):
                piece = b.wo_s.at[pl.ds(pl.multiple_of(along(k) * chunk, chunk), chunk), :]
                remote(piece, b.wo_r.at[k - 1], b.wo_ss.at[k - 1], b.wo_rr.at[k - 1], (layer, t, along(k))).start()

        d_hin = (1.0 - rate_a) * d_one + scatter_wait(6 + layer)
        b.ig_s[layer] = d_hin.astype(BF16)
        to_output(layer, b.ig_s.at[layer], ig, b.ig_ss, b.ig_r)
        grad_out = b.ig_s[layer].astype(F32)

    mine_cols = lanes(z, section_rows)
    for ref in (b.acc, gd, gsuv):
        ref[...] = jnp.zeros_like(ref)
    suv_total = jnp.zeros((2, hidden), F32)

    def block(k, suv_now):
        at = lax.rem(t + nt - k, nt)

        @pl.when(k > 0)
        def _():
            for ref, ss, rr in ((b.xa, b.xf_ss, b.xf_rr), (b.da, b.df_ss, b.df_rr)):
                remote(ref.at[at], ref.at[at], ss.at[k - 1], rr.at[k - 1], peer).wait_recv()

        new = []
        for n in range(0, hidden, tile):
            cut = slice(n, n + tile)
            up = mul(b.xa[at], b.wu[s, 0, :, cut])
            gate = mul(b.xa[at], b.wu[s, 1, :, cut])
            d_act = contract_cols(b.da[at], b.wd[s, cut, :])
            scale_up, scale_gate = b.par[s, 0:1, cut], b.par[s, 1:2, cut]
            up_s = up * scale_up
            gate_s = gate * scale_gate
            sig = 1.0 / (1.0 + jnp.exp(-gate_s))
            b.act_b[:, cut] = (up_s * gate_s * sig).astype(BF16)
            d_up = d_act * gate_s * sig
            d_gate = d_act * up_s * sig * (1.0 + gate_s * (1.0 - sig))
            new.append((jnp.sum(d_up * up, axis=0, keepdims=True), jnp.sum(d_gate * gate, axis=0, keepdims=True)))
            x_cut = b.xa[at, :, mine_cols]
            b.acc[0, :, cut] += contract_rows(x_cut, (d_up * scale_up).astype(BF16))
            b.acc[1, :, cut] += contract_rows(x_cut, (d_gate * scale_gate).astype(BF16))
        for n in range(0, width, tile):
            gd[:, n : n + tile] += contract_rows(b.act_b[:, lanes(z, hidden // nz)], b.da[at, :, n : n + tile])
        return tuple(
            jnp.concatenate([pair_of[i] for pair_of in new], axis=1) + suv_now[i] for i in range(2)
        )

    suv = lax.fori_loop(0, nt, block, (suv_total[0:1], suv_total[1:2]))
    for i in range(2):
        b.suv_b[i : i + 1, :] = suv[i]
    gsuv[...] = b.suv_b[:, lanes(z, hidden // nz)]
    per_row = 2 * hidden // 128
    for j in range(hidden // 128):
        for i in range(2):
            gu[pl.ds(2 * j + i, section_rows, stride=per_row), :] = b.acc[i, :, j * 128 : (j + 1) * 128]

    for k in range(1, nz):
        place = b.wq_r.at[k - 1]
        remote(place, place, b.wq_ss.at[k - 1], b.wq_rr.at[k - 1], peer).wait_recv()
        for i in range(3):
            gq[i] += b.wq_r[k - 1, :, i * cols : (i + 1) * cols].astype(F32)
    total = b.wo_f[pl.ds(pl.multiple_of(z * chunk, chunk), chunk), :]
    for k in range(1, nz):
        place = b.wo_r.at[k - 1]
        remote(place, place, b.wo_ss.at[k - 1], b.wo_rr.at[k - 1], peer).wait_recv()
        total = total + place[...].astype(F32)
    go[...] = total
    total = jnp.zeros((8, cols), F32)
    for k in range(nz):
        for core in range(2):
            place = b.sm_r.at[lax.rem(z + nz - k, nz), core]
            pltpu.make_async_copy(place, place, b.sm_rr.at[k, core]).wait()
            total = total + place[...]
    turned = pltpu.roll(total, lax.rem(cols - z * chunk, cols), 1)
    gal[...] = turned[0:2, 0:chunk]
    gsqk[...] = turned[2:3, 0:chunk]
    for out, sems in ((lo, b.lo_r), (ig, b.ig_r)):
        for m in range(2):
            for k in range(nt):
                place = out.at[m, pl.ds(pl.multiple_of(around(nt - k) * shard, shard), shard), :]
                pltpu.make_async_copy(place, place, sems.at[m, k]).wait()
    for k in range(nz - 1):
        remote(b.wq_s.at[k], b.wq_r.at[k], b.wq_ss.at[k], b.wq_rr.at[k], peer).wait_send()
        piece = b.wo_s.at[pl.ds(0, chunk), :]
        remote(piece, b.wo_r.at[k], b.wo_ss.at[k], b.wo_rr.at[k], peer).wait_send()
    for copy, when in pending:
        if when is None:
            copy.wait_send()
        else:
            pl.when(when)(copy.wait_send)


def per_device_fused(hidden_in, cotangent, lengths, w_qkv, w_out, w_ug, w_down, s_qk, s_uv, alpha):
    nt, nz = lax.axis_size("tensor"), lax.axis_size("dp")
    rows, cols = hidden_in.shape[1:]
    width, hidden = w_out.shape[2], w_down.shape[1]
    shard, section, chunk = rows // nt, width // nz, cols // nz
    params = jnp.concatenate(
        [
            jnp.concatenate([s_uv[0], jnp.pad(s_qk, ((0, 0), (0, hidden - cols))), jnp.zeros((5, hidden), F32)], axis=0),
            jnp.pad(alpha[0], ((0, 6), (0, 0))),
        ],
        axis=1,
    )
    steps = jnp.arange(cols, dtype=jnp.int32) % (HEAD_DIM // 2)
    rates = (10000.0 ** (-steps.astype(F32) / (HEAD_DIM // 2)))[None, :]
    scratch = buffers(nt, nz, rows, width, cols, hidden, shard, section, chunk)
    anywhere = pl.BlockSpec(memory_space=pl.ANY)
    vmem = pl.BlockSpec(memory_space=pltpu.VMEM)
    smem = pl.BlockSpec(memory_space=pltpu.SMEM)
    outs = pl.pallas_call(
        functools.partial(fused_kernel, tuple(scratch), nt, nz),
        out_shape=(
            jax.ShapeDtypeStruct((MICRO, rows, cols), BF16),
            jax.ShapeDtypeStruct((MICRO, rows, cols), BF16),
            jax.ShapeDtypeStruct((3, section, cols), F32),
            jax.ShapeDtypeStruct((chunk, width), F32),
            jax.ShapeDtypeStruct((section * 2 * hidden // 128, 128), F32),
            jax.ShapeDtypeStruct((hidden // nz, width), F32),
            jax.ShapeDtypeStruct((1, chunk), F32),
            jax.ShapeDtypeStruct((2, hidden // nz), F32),
            jax.ShapeDtypeStruct((2, chunk), F32),
        ),
        in_specs=[anywhere, anywhere, smem, anywhere, anywhere, anywhere, anywhere, vmem, vmem],
        out_specs=(anywhere, anywhere) + (vmem,) * 7,
        scratch_shapes=list(scratch.values()),
        compiler_params=pltpu.CompilerParams(
            collective_id=0, has_side_effects=True, vmem_limit_bytes=60 * 2**20
        ),
    )(
        hidden_in,
        cotangent,
        lengths,
        jnp.transpose(w_qkv[0], (1, 0, 2)),
        w_out[0],
        jnp.transpose(w_ug[0], (1, 0, 2)),
        w_down[0],
        params,
        rates,
    )
    lo, ig, gq, go, gu, gd, gsqk, gsuv, gal = outs
    gu = gu.reshape(section, hidden // 128, 2, 128).transpose(0, 2, 1, 3).reshape(section, 2, hidden)
    return (
        lo[None],
        ig[None],
        jnp.transpose(gq, (1, 0, 2))[None],
        go[None],
        gu[None],
        gd[None],
        gsqk,
        gsuv[None],
        gal[None],
    )


def solution(mesh):
    placed = (
        P(None, "dp", "tensor"),
        P(None, "dp", "tensor"),
        P(),
        P("section", None, None, "tensor"),
        P("section", "tensor", None),
        P("section", None, None, "tensor"),
        P("section", "tensor", None),
        P("section", "tensor"),
        P("section", None, "tensor"),
        P("section", None, "tensor"),
    )
    per_rank = per_device_fused if mesh.shape["dp"] == 2 * MICRO and mesh.shape["tensor"] == 4 else per_device
    return jax.shard_map(
        per_rank,
        mesh=mesh,
        in_specs=placed,
        out_specs=(
            P("section", None, "dp", "tensor"),
            P("section", None, "dp", "tensor"),
            P("section", "dp", None, "tensor"),
            P("section", ("tensor", "dp"), None),
            P("section", "dp", None, "tensor"),
            P("section", ("tensor", "dp"), None),
            P("section", ("tensor", "dp")),
            P("section", None, ("tensor", "dp")),
            P("section", None, ("tensor", "dp")),
        ),
        check_vma=False,
    )
```

```python
import functools
import math
import types

import jax
import jax.numpy as jnp
import numpy as np
from jax import lax
from jax.experimental import pallas as pl
from jax.experimental.pallas import tpu as pltpu
from jax.sharding import PartitionSpec as P

D = 1024
HEAD_DIM = 64
SEQ_CAP = 4096


EPSILON = 1e-05
HIGHEST = lax.Precision.HIGHEST
NEG_LARGE = -1e30


def passed_along(array, axis, by):
    count = lax.axis_size(axis)
    return lax.ppermute(array, axis, [(i, (i + by) % count) for i in range(count)])


def from_behind(array, axis, by):
    count = lax.axis_size(axis)
    pairs = [(i, i + by) for i in range(count) if 0 <= i + by < count]
    return lax.ppermute(array, axis, pairs)


def seq_table(lengths_row, positions):
    count = lengths_row.shape[0]
    order = jnp.arange(count, dtype=jnp.int32)
    seq_end = jnp.sum(jnp.where(order[None, :] <= order[:, None], lengths_row[None, :], 0), axis=1)
    seq_start = seq_end - lengths_row
    segment = jnp.sum((positions[:, None] >= seq_end[None, :]).astype(jnp.int32), axis=1)
    labels = jnp.arange(lengths_row.shape[0], dtype=jnp.int32)
    first_tok = jnp.sum(
        jnp.where(segment[:, None] == labels[None, :], seq_start[None, :], 0), axis=1
    )
    return (segment, positions - first_tok)


def rope_tables(places, col_width):
    column = jnp.arange(col_width, dtype=jnp.int32) % HEAD_DIM
    half_dim = HEAD_DIM // 2
    rope_rates = 10000.0 ** (-(column % half_dim).astype(jnp.float32) / half_dim)
    angles = places.astype(jnp.float32)[:, None] * rope_rates[None, :]
    return (jnp.cos(angles), jnp.sin(angles), column < half_dim)


def partner(values, lower_half):
    half_dim = HEAD_DIM // 2
    return jnp.where(
        lower_half[None, :],
        -jnp.roll(values, -half_dim, axis=1),
        jnp.roll(values, half_dim, axis=1),
    )


def contract_rows(left_op, right_op):
    return lax.dot_general(
        left_op, right_op, (((0,), (0,)), ((), ())), preferred_element_type=jnp.float32
    )


def contract_cols(left_op, right_op):
    return lax.dot_general(
        left_op, right_op, (((1,), (1,)), ((), ())), preferred_element_type=jnp.float32
    )


def full_rows(columns):
    return lax.all_gather(columns, "tensor", axis=1, tiled=True)


def to_cols(partial_sum):
    return lax.psum_scatter(
        partial_sum.astype(jnp.bfloat16), "tensor", scatter_dimension=1, tiled=True
    ).astype(jnp.float32)


def grad_rows(columns):
    return lax.all_gather(columns, "tensor", axis=1, tiled=True)


def grad_cols(partial_sum):
    return lax.psum_scatter(
        partial_sum.astype(jnp.bfloat16), "tensor", scatter_dimension=1, tiled=True
    ).astype(jnp.float32)


def row_total(values):
    return lax.psum(jnp.sum(values, axis=1), "tensor")


def sphere(values):
    row_ratio = lax.rsqrt(row_total(values * values) / D + EPSILON)[:, None]
    return (values * row_ratio, row_ratio)


def sphere_back(source, row_ratio, grad_in):
    inner_sum = row_total(grad_in * source)[:, None]
    return row_ratio * grad_in - source * (row_ratio * row_ratio * row_ratio) * inner_sum / D


def pass_on(dkv_sum):
    return passed_along(dkv_sum.astype(jnp.bfloat16), "dp", 1).astype(dkv_sum.dtype)


def unchanged(previous):
    return previous


def per_device(hidden_in, cotangent, lengths, w_qkv, w_out, w_ug, w_down, s_qk, s_uv, alpha):
    micro_n = hidden_in.shape[0]
    tok_rows = hidden_in.shape[1]
    col_width = hidden_in.shape[2]
    heads_here = col_width // HEAD_DIM
    ff_here = w_down.shape[1]
    dp_ranks = lax.axis_size("dp")
    dp_rank = lax.axis_index("dp")
    longest = min(SEQ_CAP, tok_rows * dp_ranks // 2)
    reach_len = min(dp_ranks - 1, (longest + tok_rows - 2) // tok_rows)
    first_section = lax.axis_index("section") == 0
    score_div = math.sqrt(HEAD_DIM)
    qkv_mat = w_qkv[0].reshape(D, 3 * col_width)
    out_mat = w_out[0]
    ug_mat = w_ug[0].reshape(D, 2 * ff_here)
    down_mat = w_down[0]
    scale_qk = s_qk[0]
    scale_up = s_uv[0, 0]
    scale_gate = s_uv[0, 1]
    alpha_attn = alpha[0, 0]
    alpha_mlp = alpha[0, 1]
    local_rows = jnp.arange(tok_rows, dtype=jnp.int32)
    q_index = dp_rank * tok_rows + local_rows
    indicator = (
        jnp.arange(col_width, dtype=jnp.int32)[:, None] // HEAD_DIM
        == jnp.arange(heads_here, dtype=jnp.int32)[None, :]
    ).astype(jnp.float32)

    def head_sum(values):
        return jnp.dot(values, indicator, precision=HIGHEST, preferred_element_type=jnp.float32)

    def spread(small):
        return jnp.dot(small, indicator.T, precision=HIGHEST, preferred_element_type=jnp.float32)

    def block_info(lengths_row, q_segment, offset):
        source = dp_rank - offset
        k_index = source * tok_rows + local_rows
        k_segment, unused = seq_table(lengths_row, k_index)
        key_mask = (
            (k_segment[None, :] == q_segment[:, None])
            & (k_index[None, :] <= q_index[:, None])
            & (k_index[None, :] >= 0)
        )
        needed = (source * tok_rows + tok_rows - 1 >= 0) & (k_segment[tok_rows - 1] >= q_segment[0])
        return (key_mask, needed)

    def block_scores(q_heads, kv_block):
        key_heads = kv_block[:, :col_width].reshape(tok_rows, heads_here, HEAD_DIM)
        return (
            jnp.einsum("qhd,khd->hqk", q_heads, key_heads, preferred_element_type=jnp.float32)
            / score_div
        )

    def prep_back(grad_n, rotated, head_ratio, record):
        unit_vec = rotated * head_ratio
        d_scale = jnp.sum(grad_n * unit_vec, axis=0)
        d_unit = grad_n * scale_qk[None, :]
        d_rot = head_ratio * d_unit - rotated * (head_ratio * head_ratio * head_ratio) * spread(
            head_sum(d_unit * rotated) / HEAD_DIM
        )
        return (
            d_rot * record["cosine"] - partner(d_rot * record["sine_tab"], record["lower_half"]),
            d_scale,
        )

    received_in = jnp.zeros((tok_rows, col_width), jnp.bfloat16)
    records = []
    results = []
    for tick_no in range(micro_n + 1):
        early_mb = min(tick_no, micro_n - 1)
        late_mb = max(tick_no - 1, 0)
        lengths_row = jnp.where(first_section, lengths[early_mb], lengths[late_mb])
        layer_in = jnp.where(first_section, hidden_in[early_mb], received_in)
        hidden = layer_in.astype(jnp.float32)
        forward_q_segment, places = seq_table(lengths_row, q_index)
        cosine, sine_tab, lower_half = rope_tables(places, col_width)
        full_in = full_rows(hidden.astype(jnp.bfloat16))
        qkv = jnp.dot(full_in, qkv_mat, preferred_element_type=jnp.float32)
        q_raw = qkv[:, :col_width]
        k_raw = qkv[:, col_width : 2 * col_width]
        q_rot = q_raw * cosine + partner(q_raw, lower_half) * sine_tab
        k_rot = k_raw * cosine + partner(k_raw, lower_half) * sine_tab
        q_ratio = spread(lax.rsqrt(head_sum(q_rot * q_rot) / HEAD_DIM + EPSILON))
        k_ratio = spread(lax.rsqrt(head_sum(k_rot * k_rot) / HEAD_DIM + EPSILON))
        query_b = (q_rot * q_ratio * scale_qk[None, :]).astype(jnp.bfloat16)
        key_b = (k_rot * k_ratio * scale_qk[None, :]).astype(jnp.bfloat16)
        value_b = qkv[:, 2 * col_width :].astype(jnp.bfloat16)
        forward_q_heads = query_b.reshape(tok_rows, heads_here, HEAD_DIM)
        own_block = jnp.concatenate([key_b, value_b], axis=1)

        def lse_step(lse_state, kv_block, offset):
            key_mask, needed = block_info(lengths_row, forward_q_segment, offset)

            def update(previous):
                run_max, run_sum = previous
                masked = jnp.where(
                    key_mask[None], block_scores(forward_q_heads, kv_block), NEG_LARGE
                )
                new_max = jnp.maximum(run_max, jnp.max(masked, axis=2))
                exp_terms = jnp.where(key_mask[None], jnp.exp(masked - new_max[:, :, None]), 0.0)
                return (new_max, run_sum * jnp.exp(run_max - new_max) + jnp.sum(exp_terms, axis=2))

            return lax.cond(needed, update, unchanged, lse_state)

        init_state = (
            jnp.full((heads_here, tok_rows), NEG_LARGE, jnp.float32),
            jnp.zeros((heads_here, tok_rows), jnp.float32),
        )
        lse_state = lse_step(init_state, own_block, jnp.int32(0))

        def cycle_step(state_in, offset):
            kv_block, lse_now = state_in
            kv_block = from_behind(kv_block, "dp", 1)
            return ((kv_block, lse_step(lse_now, kv_block, offset)), kv_block)

        (forward_unused_block, lse_state), received = lax.scan(
            cycle_step, (own_block, lse_state), jnp.arange(1, reach_len + 1, dtype=jnp.int32)
        )
        kv_stack = jnp.concatenate([own_block[None], received], axis=0)
        forward_log_total = lse_state[0] + jnp.log(lse_state[1])

        def value_step(acc_heads, scan_item):
            kv_block, offset = scan_item
            key_mask, needed = block_info(lengths_row, forward_q_segment, offset)

            def add_values(previous):
                attn_prob = jnp.where(
                    key_mask[None],
                    jnp.exp(
                        block_scores(forward_q_heads, kv_block) - forward_log_total[:, :, None]
                    ),
                    0.0,
                ).astype(jnp.bfloat16)
                val_heads = kv_block[:, col_width:].reshape(tok_rows, heads_here, HEAD_DIM)
                return previous + jnp.einsum(
                    "hqk,khd->hqd", attn_prob, val_heads, preferred_element_type=jnp.float32
                )

            return (lax.cond(needed, add_values, unchanged, acc_heads), None)

        acc_heads, forward_unused_out = lax.scan(
            value_step,
            jnp.zeros((heads_here, tok_rows, HEAD_DIM), jnp.float32),
            (kv_stack, jnp.arange(reach_len + 1, dtype=jnp.int32)),
        )
        attended = jnp.transpose(acc_heads, (1, 0, 2)).reshape(tok_rows, col_width)
        attended_b = attended.astype(jnp.bfloat16)
        attn_raw = to_cols(jnp.dot(attended_b, out_mat, preferred_element_type=jnp.float32))
        attn_n, ratio_a = sphere(attn_raw)
        mix_one = hidden + alpha_attn[None, :] * (attn_n - hidden)
        normed_one, ratio_one = sphere(mix_one)
        inner_full = full_rows(normed_one.astype(jnp.bfloat16))
        forward_upgate = jnp.dot(inner_full, ug_mat, preferred_element_type=jnp.float32)
        forward_up_s = forward_upgate[:, :ff_here] * scale_up[None, :]
        forward_gate_s = forward_upgate[:, ff_here:] * scale_gate[None, :]
        act_b = (forward_up_s * jax.nn.silu(forward_gate_s)).astype(jnp.bfloat16)
        mlp_raw = to_cols(jnp.dot(act_b, down_mat, preferred_element_type=jnp.float32))
        mlp_n, ratio_m = sphere(mlp_raw)
        mix_two = normed_one + alpha_mlp[None, :] * (mlp_n - normed_one)
        result, ratio_two = sphere(mix_two)
        kept_blocks = own_block[None]
        forward_record = {
            "lengths_row": lengths_row,
            "q_segment": forward_q_segment,
            "cosine": cosine,
            "sine_tab": sine_tab,
            "lower_half": lower_half,
            "full_in": full_in,
            "q_rot": q_rot,
            "k_rot": k_rot,
            "q_ratio": q_ratio,
            "k_ratio": k_ratio,
            "query_b": query_b,
            "blocks": kept_blocks,
            "log_total": forward_log_total,
            "attended": attended,
            "attended_b": attended_b,
            "hidden": hidden,
            "attn_raw": attn_raw,
            "ratio_a": ratio_a,
            "attn_n": attn_n,
            "mix_one": mix_one,
            "ratio_one": ratio_one,
            "normed_one": normed_one,
            "inner_full": inner_full,
            "upgate": forward_upgate,
            "act_b": act_b,
            "mlp_raw": mlp_raw,
            "ratio_m": ratio_m,
            "mlp_n": mlp_n,
            "mix_two": mix_two,
            "ratio_two": ratio_two,
        }
        record, result = (forward_record, result)
        result_b = result.astype(jnp.bfloat16)
        records.append(record)
        results.append(result_b)
        if tick_no < micro_n:
            received_in = from_behind(result_b, "section", 1)
    layer_outputs = jnp.stack(
        [
            jnp.where(first_section, results[number], results[number + 1])
            for number in range(micro_n)
        ]
    )
    back_in = jnp.zeros((tok_rows, col_width), jnp.bfloat16)
    grad_totals = None
    back_results = []
    for tick_no in range(micro_n + 1):
        record = records[micro_n - tick_no]
        late_cot = cotangent[max(micro_n - 1 - tick_no, 0)].astype(jnp.float32)
        live_flag = jnp.where(
            first_section, 1.0 if tick_no >= 1 else 0.0, 1.0 if tick_no < micro_n else 0.0
        )
        grad_out = jnp.where(first_section, back_in.astype(jnp.float32), late_cot) * live_flag
        backward_lengths_row = record["lengths_row"]
        backward_q_segment = record["q_segment"]
        dz_two = sphere_back(record["mix_two"], record["ratio_two"], grad_out)
        d_normed = (1.0 - alpha_mlp)[None, :] * dz_two
        d_mlp_n = alpha_mlp[None, :] * dz_two
        d_alpha_mlp = jnp.sum(dz_two * (record["mlp_n"] - record["normed_one"]), axis=0)
        d_mlp = sphere_back(record["mlp_raw"], record["ratio_m"], d_mlp_n)
        d_mlp_full = grad_rows(d_mlp.astype(jnp.bfloat16))
        dw_down = contract_rows(record["act_b"], d_mlp_full)
        d_act = contract_cols(d_mlp_full, down_mat)
        upgate = record["upgate"]
        up_s = upgate[:, :ff_here] * scale_up[None, :]
        gate_s = upgate[:, ff_here:] * scale_gate[None, :]
        gate_sig = jax.nn.sigmoid(gate_s)
        d_up = d_act * gate_s * gate_sig
        d_gate = d_act * up_s * gate_sig * (1.0 + gate_s * (1.0 - gate_sig))
        d_scale_up = jnp.sum(d_up * upgate[:, :ff_here], axis=0)
        d_scale_gate = jnp.sum(d_gate * upgate[:, ff_here:], axis=0)
        d_upgate = jnp.concatenate(
            [d_up * scale_up[None, :], d_gate * scale_gate[None, :]], axis=1
        ).astype(jnp.bfloat16)
        dw_ug = contract_rows(record["inner_full"], d_upgate)
        d_normed = d_normed + grad_cols(contract_cols(d_upgate, ug_mat))
        dz_one = sphere_back(record["mix_one"], record["ratio_one"], d_normed)
        d_hidden = (1.0 - alpha_attn)[None, :] * dz_one
        d_attn_n = alpha_attn[None, :] * dz_one
        d_alpha_attn = jnp.sum(dz_one * (record["attn_n"] - record["hidden"]), axis=0)
        d_attn = sphere_back(record["attn_raw"], record["ratio_a"], d_attn_n)
        d_attn_full = grad_rows(d_attn.astype(jnp.bfloat16))
        dw_out = contract_rows(record["attended_b"], d_attn_full)
        d_attended = contract_cols(d_attn_full, out_mat).astype(jnp.bfloat16)
        row_delta = jnp.transpose(head_sum(d_attended.astype(jnp.float32) * record["attended"]))
        do_heads = d_attended.reshape(tok_rows, heads_here, HEAD_DIM)
        backward_q_heads = record["query_b"].reshape(tok_rows, heads_here, HEAD_DIM)
        log_total = record["log_total"]

        def block_grads(dq_now, kv_block, offset):
            key_mask, needed = block_info(backward_lengths_row, backward_q_segment, offset)

            def compute(previous):
                key_heads = kv_block[:, :col_width].reshape(tok_rows, heads_here, HEAD_DIM)
                val_heads = kv_block[:, col_width:].reshape(tok_rows, heads_here, HEAD_DIM)
                attn_prob = jnp.where(
                    key_mask[None],
                    jnp.exp(block_scores(backward_q_heads, kv_block) - log_total[:, :, None]),
                    0.0,
                )
                d_prob = jnp.einsum(
                    "qhd,khd->hqk", do_heads, val_heads, preferred_element_type=jnp.float32
                )
                d_val = jnp.einsum(
                    "hqk,qhd->khd",
                    attn_prob.astype(jnp.bfloat16),
                    do_heads,
                    preferred_element_type=jnp.float32,
                )
                d_score = (attn_prob * (d_prob - row_delta[:, :, None])).astype(jnp.bfloat16)
                new_dq = (
                    previous
                    + jnp.einsum(
                        "hqk,khd->hqd", d_score, key_heads, preferred_element_type=jnp.float32
                    )
                    / score_div
                )
                d_key = (
                    jnp.einsum(
                        "hqk,qhd->khd",
                        d_score,
                        backward_q_heads,
                        preferred_element_type=jnp.float32,
                    )
                    / score_div
                )
                return (
                    jnp.concatenate(
                        [d_key.reshape(tok_rows, col_width), d_val.reshape(tok_rows, col_width)],
                        axis=1,
                    ),
                    new_dq,
                )

            def skipped(previous):
                return (jnp.zeros((tok_rows, 2 * col_width), jnp.float32), previous)

            return lax.cond(needed, compute, skipped, dq_now)

        own_part, dq_acc = block_grads(
            jnp.zeros((heads_here, tok_rows, HEAD_DIM), jnp.float32),
            record["blocks"][0],
            jnp.int32(0),
        )
        offsets = jnp.arange(1, reach_len + 1, dtype=jnp.int32)

        def again_step(state_in, offset):
            dkv_sum, kv_block, dq_now = state_in
            dkv_sum = pass_on(dkv_sum)
            kv_block = from_behind(kv_block, "dp", 1)
            dkv_part, dq_now = block_grads(dq_now, kv_block, offset)
            return ((dkv_sum + dkv_part, kv_block, dq_now), None)

        (dkv_sum, unused_block, dq_acc), unused_out = lax.scan(
            again_step, (own_part, record["blocks"][0], dq_acc), offsets
        )
        dkv_home = passed_along(dkv_sum.astype(jnp.bfloat16), "dp", -reach_len).astype(
            dkv_sum.dtype
        )
        dq_full = jnp.transpose(dq_acc, (1, 0, 2)).reshape(tok_rows, col_width)
        dq_raw, ds_query = prep_back(dq_full, record["q_rot"], record["q_ratio"], record)
        dk_raw, ds_key = prep_back(
            dkv_home[:, :col_width], record["k_rot"], record["k_ratio"], record
        )
        d_qkv = jnp.concatenate([dq_raw, dk_raw, dkv_home[:, col_width:]], axis=1).astype(
            jnp.bfloat16
        )
        dw_qkv = contract_rows(record["full_in"], d_qkv)
        d_hidden = d_hidden + grad_cols(contract_cols(d_qkv, qkv_mat))
        grads = (
            dw_qkv.reshape(D, 3, col_width),
            dw_out,
            dw_ug.reshape(D, 2, ff_here),
            dw_down,
            ds_query + ds_key,
            jnp.stack([d_scale_up, d_scale_gate]),
            jnp.stack([d_alpha_attn, d_alpha_mlp]),
        )
        d_hidden, grads = (d_hidden, grads)
        grad_b = d_hidden.astype(jnp.bfloat16)
        back_results.append(grad_b)
        grad_totals = grads if grad_totals is None else jax.tree.map(jnp.add, grad_totals, grads)
        if tick_no < micro_n:
            back_in = from_behind(grad_b, "section", -1)
    input_grads = jnp.stack(
        [
            jnp.where(
                first_section, back_results[micro_n - number], back_results[micro_n - 1 - number]
            )
            for number in range(micro_n)
        ]
    )
    summed = (
        lax.psum_scatter(
            grad_totals[0].astype(jnp.bfloat16), "dp", scatter_dimension=0, tiled=True
        ).astype(jnp.float32),
        lax.psum_scatter(
            grad_totals[1].astype(jnp.bfloat16), "dp", scatter_dimension=0, tiled=True
        ).astype(jnp.float32),
        lax.psum_scatter(
            grad_totals[2].astype(jnp.bfloat16), "dp", scatter_dimension=0, tiled=True
        ).astype(jnp.float32),
        lax.psum_scatter(
            grad_totals[3].astype(jnp.bfloat16), "dp", scatter_dimension=0, tiled=True
        ).astype(jnp.float32),
        lax.psum_scatter(
            grad_totals[4].astype(jnp.bfloat16), "dp", scatter_dimension=0, tiled=True
        ).astype(jnp.float32),
        lax.psum_scatter(
            grad_totals[5].astype(jnp.bfloat16), "dp", scatter_dimension=1, tiled=True
        ).astype(jnp.float32),
        lax.psum_scatter(
            grad_totals[6].astype(jnp.bfloat16), "dp", scatter_dimension=1, tiled=True
        ).astype(jnp.float32),
    )
    return (
        layer_outputs[None],
        input_grads[None],
        summed[0][None],
        summed[1][None],
        summed[2][None],
        summed[3][None],
        summed[4][None],
        summed[5][None],
        summed[6][None],
    )


MESH = pl.DeviceIdType.MESH
MICRO = 2
F32 = jnp.float32
BF16 = jnp.bfloat16


def mul(left_op, right_op):
    return jnp.dot(left_op, right_op, preferred_element_type=F32)


def remote(src, dst, send_sem, recv_sem, device):
    return pltpu.make_async_remote_copy(
        src_ref=src, dst_ref=dst, send_sem=send_sem, recv_sem=recv_sem, device_id=device, device_id_type=MESH
    )


def ball(values, width):
    ratio = lax.rsqrt(jnp.sum(values * values, axis=1, keepdims=True) / width + EPSILON)
    return values * ratio, ratio


def ball_back(source, ratio, grad_in, width):
    inner = jnp.sum(grad_in * source, axis=1, keepdims=True)
    return ratio * grad_in - source * (ratio * ratio * ratio) * (inner / width)


def buffers(nt, nz, rows, width, cols, hidden, shard, section, chunk):
    vmem, dma = pltpu.VMEM, pltpu.SemaphoreType.DMA
    pair = 2 * rows
    return dict(
        wq=vmem((2, 3, width, cols), BF16),
        wo=vmem((2, cols, width), BF16),
        wu=vmem((2, 2, width, hidden), BF16),
        wd=vmem((2, hidden, width), BF16),
        sqk=vmem((2, 1, cols), F32),
        suv=vmem((2, 2, hidden), F32),
        alp=vmem((2, 2, width), F32),
        raw=vmem((2 * hidden // 128 * width, 128), BF16),
        raw_f=vmem((2 * hidden // 128 * 64, 128), F32),
        full_in=vmem((2, rows, width), BF16),
        mid_full=vmem((2, nt, shard, width), BF16),
        dml_full=vmem((2, nt, shard, width), BF16),
        dat_full=vmem((2, rows, width), BF16),
        fi_p=vmem((rows, width), BF16),
        at_p=vmem((rows, cols), BF16),
        da_p=vmem((rows, width), BF16),
        dq_p=vmem((rows, 3 * cols), BF16),
        xa=vmem((nt, nz * 2 * shard, width), BF16),
        da=vmem((nt, nz * 2 * shard, width), BF16),
        kv=vmem((2, pair, 2 * cols), BF16),
        dkv_f=vmem((pair, 2 * cols), F32),
        dkv_s=vmem((2, rows, 2 * cols), BF16),
        dkv_r=vmem((2, rows, 2 * cols), BF16),
        rs_s=vmem((8, rows, width), BF16),
        rs_r=vmem((8, nt - 1, shard, width), BF16),
        rot=vmem((2, 2, rows, cols), F32),
        rat=vmem((2, 2, rows, cols), F32),
        qb=vmem((2, rows, cols), BF16),
        prob=vmem((2, cols // HEAD_DIM, rows, pair), F32),
        at=vmem((2, rows, cols), BF16),
        araw=vmem((2, shard, width), F32),
        mraw=vmem((2, shard, width), F32),
        mid=vmem((2, shard, width), F32),
        zone=vmem((2, shard, width), F32),
        ztwo=vmem((2, shard, width), F32),
        up=vmem((2, rows, hidden), F32),
        gate=vmem((2, rows, hidden), F32),
        act=vmem((rows, hidden), BF16),
        duv=vmem((2, rows, hidden), BF16),
        dqkv=vmem((2, rows, 3 * cols), BF16),
        cot_rows=vmem((shard, width), BF16),
        out_s=vmem((2, shard, width), BF16),
        ig_s=vmem((2, shard, width), BF16),
        cosb=vmem((rows, cols), F32),
        sinb=vmem((rows, cols), F32),
        bias=vmem((rows, pair), F32),
        blk=vmem((cols, cols), BF16),
        al_s=vmem((2, 8, width), F32),
        al_r=vmem((2, nt - 1, 8, cols), F32),
        small=vmem((2, 8, cols), F32),
        sm_r=vmem((nz, 2, 8, cols), F32),
        wq_s=vmem((nz - 1, section, 3 * cols), BF16),
        wq_r=vmem((nz - 1, section, 3 * cols), BF16),
        wo_f=vmem((cols, width), F32),
        wo_s=vmem((cols, width), BF16),
        wo_r=vmem((nz - 1, chunk, width), BF16),
        act_b=vmem((nz * 2 * shard, hidden), BF16),
        suv_b=vmem((2, hidden), F32),
        acc=vmem((2, section, hidden), F32),
        w_l=dma((2, 4)), w_rs=dma((4,)),
        par_l=dma((2, 2)), par_s=dma((2,)),
        alp_r=dma((2, nt)), alp_s=dma((2, nt)),
        hid_r=dma((nt,)), hid_s=dma((2, nt)),
        cot_r=dma((nt,)), cot_s=dma((2, nt)),
        fi_rs=dma((2,)), at_rs=dma((2,)), dap_rs=dma((2,)), dq_rs=dma((2,)),
        kv_rs=dma((2, 2)), dkv_rs=dma((2, 2)),
        ag_ss=dma((7, nt - 1)), ag_rr=dma((7, nt - 1)),
        rs_ss=dma((8, nt - 1)), rs_rr=dma((8, nt - 1)),
        xa_r=dma((nz, 2)), xa_ss=dma((2, nz)),
        da_r=dma((nz, 2)), da_ss=dma((2, nz)),
        df_ss=dma((nz - 1, nt - 1)), df_rr=dma((nz - 1, nt - 1)),
        lo_ss=dma((2, nt)), lo_r=dma((2, nt)),
        ig_ss=dma((2, nt)), ig_r=dma((2, nt)),
        al_ss=dma((2, nt - 1)), al_rr=dma((2, nt - 1)),
        sm_ss=dma((2, nz)), sm_rr=dma((nz, 2)),
        wq_ss=dma((nz - 1,)), wq_rr=dma((nz - 1,)),
        wo_ss=dma((nz - 1,)), wo_rr=dma((nz - 1,)),
    )


def fused_kernel(names, nt, nz, *refs):
    hid, cot, lens, wq_in, wo_in, wu_in, wd_in, sqk_in, suv_in, alp_in, rates = refs[:11]
    lo, ig, gq, go, gu, gd, gsqk, gsuv, gal = refs[11:20]
    b = types.SimpleNamespace(**dict(zip(names, refs[20:])))
    rows, width = b.full_in.shape[1:]
    cols, hidden = b.qb.shape[2], b.wd.shape[1]
    shard = b.mid.shape[1]
    heads = cols // HEAD_DIM
    pair = 2 * rows
    section_rows = width // nz
    chunk = cols // nz
    tile = 512
    s, t, z = lax.axis_index("section"), lax.axis_index("tensor"), lax.axis_index("dp")
    p = lax.rem(z, 2)
    base = z - p
    peer = (1 - s, t, z)
    pending = []

    def around(k):
        return lax.rem(t + k, nt)

    def along(k):
        return lax.rem(z + k, nz)

    def later(copy, when=None):
        pending.append((copy, when))

    def lanes(index, size):
        return pl.ds(pl.multiple_of(index * size, size), size)

    weights = [(wq_in, b.wq), (wo_in, b.wo), (None, b.wu), (wd_in, b.wd)]
    raw_copy = pltpu.make_async_copy(wu_in, b.raw, b.w_l.at[s, 2])
    raw_copy.start()
    for i in (0, 1, 3):
        src, dst = weights[i]
        pltpu.make_async_copy(src, dst.at[s], b.w_l.at[s, i]).start()
    params = [(sqk_in, b.sqk), (suv_in, b.suv)]
    for i, (src, dst) in enumerate(params):
        pltpu.make_async_copy(src, dst.at[s], b.par_l.at[s, i]).start()

    barrier = pltpu.get_barrier_semaphore()
    greeted = 0
    for dz in range(2):
        for dt in range(nt):
            for dc in range(2):
                if dz or dt or dc:
                    device = (lax.rem(s + dc, 2), around(dt), base + lax.rem(p + dz, 2))
                    pl.semaphore_signal(barrier, inc=1, device_id=device, device_id_type=MESH)
                    greeted += 1
    for dz in range(2, nz):
        for dc in range(2):
            device = (lax.rem(s + dc, 2), t, lax.rem(base + dz, nz))
            pl.semaphore_signal(barrier, inc=1, device_id=device, device_id_type=MESH)
            greeted += 1
    token0 = (base // 2) * pair
    pos_q = token0 + s * rows + lax.broadcasted_iota(jnp.int32, (rows, 1), 0)
    pos_k = token0 + lax.broadcasted_iota(jnp.int32, (1, pair), 1)

    def sequences(pos):
        seg = jnp.zeros_like(pos)
        first = jnp.zeros_like(pos)
        end = jnp.int32(0)
        for i in range(lens.shape[1]):
            end = end + lens[p, i]
            past = pos >= end
            seg = seg + past.astype(jnp.int32)
            first = jnp.where(past, end, first)
        return seg, pos - first

    seg_q, place_q = sequences(pos_q)
    seg_k, _ = sequences(pos_k)
    allowed = (seg_q == seg_k) & (pos_k <= pos_q)
    b.bias[...] = jnp.where(allowed, 0.0, NEG_LARGE)
    angle = place_q.astype(F32) * rates[...]
    b.cosb[...] = jnp.cos(angle)
    b.sinb[...] = jnp.sin(angle)
    col = lax.broadcasted_iota(jnp.int32, (1, cols), 1)
    lower = (col & (HEAD_DIM // 2)) == 0
    head_of = lax.shift_right_logical(col, 6)
    head_row = lax.shift_right_logical(lax.broadcasted_iota(jnp.int32, (cols, 1), 0), 6)
    b.blk[...] = jnp.where(head_row == head_of, 1.0, 0.0).astype(BF16)
    picks = [jnp.where(head_of == h, 1.0, 0.0) for h in range(heads)]
    b.al_s[...] = jnp.zeros_like(b.al_s)
    b.small[...] = jnp.zeros_like(b.small)

    @pl.when(s == 0)
    def _():
        b.kv[:, rows:pair, :] = jnp.zeros((2, rows, 2 * cols), BF16)

    @pl.when(s == 1)
    def _():
        b.dkv_r[...] = jnp.zeros_like(b.dkv_r)


    def to_order():
        raw_copy.wait()
        lines = 2 * hidden // 128

        def in_order(step, carry):
            b.raw_f[...] = b.raw[pl.ds(pl.multiple_of(step * lines * 64, lines * 64), lines * 64), :].astype(F32)
            at = pl.ds(pl.multiple_of(step * 64, 64), 64)
            for n in range(hidden // 128):
                for i in range(2):
                    b.wu[s, i, at, n * 128 : (n + 1) * 128] = b.raw_f[pl.ds(2 * n + i, 64, stride=lines), :].astype(BF16)
            return carry

        lax.fori_loop(0, width // 64, in_order, 0)

    pl.semaphore_wait(barrier, greeted)
    pl.when(s == 1)(to_order)

    is_source = s == p
    for src, rs, ss in ((hid, b.hid_r, b.hid_s), (cot, b.cot_r, b.cot_s)):
        for dz in range(2):
            to_mb = lax.rem(p + dz, 2)
            for dt in range(nt):
                to_t = around(dt)
                if src is hid:
                    piece, place = src.at[to_mb], b.full_in.at[0, :, lanes(t, cols)]
                else:
                    piece = src.at[to_mb, pl.ds(pl.multiple_of(to_t * shard, shard), shard), :]
                    place = b.cot_rows.at[:, lanes(t, cols)]
                if dz == 0 and dt == 0:

                    @pl.when(is_source)
                    def _(piece=piece, place=place, rs=rs):
                        pltpu.make_async_copy(piece, place, rs.at[0]).start()
                else:
                    copy = remote(piece, place, ss.at[dz, dt], rs.at[dt], (s, to_t, base + to_mb))
                    pl.when(is_source)(copy.start)
                    later(copy, is_source)
        if src is hid:
            for i, (src_p, dst_p) in enumerate(params):
                copy = remote(src_p, dst_p.at[s], b.par_s.at[i], b.par_l.at[s, i], peer)
                copy.start()
                later(copy)
            alp_src, alp_dst = alp_in, b.alp.at[s, :, lanes(t, cols)]
            for dc in range(2):
                for dt in range(nt):
                    if dc == 0 and dt == 0:
                        pltpu.make_async_copy(alp_src, alp_dst, b.alp_r.at[s, 0]).start()
                    else:
                        copy = remote(alp_src, alp_dst, b.alp_s.at[dc, dt], b.alp_r.at[s, dt], (lax.rem(s + dc, 2), around(dt), z))
                        copy.start()
                        later(copy)
            for i in (0, 1, 3):
                src_w, dst_w = weights[i]
                copy = remote(src_w, dst_w.at[s], b.w_rs.at[i], b.w_l.at[s, i], peer)
                copy.start()
                later(copy)

    def wait_weight(layer, i):
        dst_w = weights[i][1].at[layer]
        wait = pltpu.make_async_copy(dst_w, dst_w, b.w_l.at[layer, i]).wait
        if i == 2:
            pl.when(s != layer)(wait)
        else:
            wait()

    pl.when(s == 0)(to_order)
    copy = remote(b.wu.at[s], b.wu.at[s], b.w_rs.at[2], b.w_l.at[s, 2], peer)
    copy.start()
    later(copy)

    def partner_cols(x):
        half = HEAD_DIM // 2
        return jnp.where(lower, -pltpu.roll(x, cols - half, 1), pltpu.roll(x, half, 1))

    def head_total(x):
        high = x.astype(BF16)
        low = (x - high.astype(F32)).astype(BF16)
        return mul(high, b.blk[...]) + mul(low, b.blk[...])

    def shard_of(ref, index):
        return ref.at[index] if len(ref.shape) == 3 else ref.at[pl.ds(pl.multiple_of(index * shard, shard), shard), :]

    def gather(stage, ref):
        mine = shard_of(ref, t)
        for k in range(1, nt):
            copy = remote(mine, mine, b.ag_ss.at[stage, k - 1], b.ag_rr.at[stage, k - 1], (s, around(k), z))
            copy.start()
            later(copy)

    def gather_wait(stage, ref):
        for k in range(1, nt):
            theirs = shard_of(ref, around(nt - k))
            remote(theirs, theirs, b.ag_ss.at[stage, k - 1], b.ag_rr.at[stage, k - 1], (s, around(k), z)).wait_recv()

    def scatter(stage):
        for k in range(1, nt):
            piece = b.rs_s.at[stage, pl.ds(pl.multiple_of(around(k) * shard, shard), shard), :]
            copy = remote(piece, b.rs_r.at[stage, k - 1], b.rs_ss.at[stage, k - 1], b.rs_rr.at[stage, k - 1], (s, around(k), z))
            copy.start()
            later(copy)

    def scatter_wait(stage):
        total = b.rs_s[stage, pl.ds(pl.multiple_of(t * shard, shard), shard), :].astype(F32)
        for k in range(1, nt):
            place = b.rs_r.at[stage, k - 1]
            remote(place, place, b.rs_ss.at[stage, k - 1], b.rs_rr.at[stage, k - 1], (s, around(k), z)).wait_recv()
            total = total + place[...].astype(F32)
        return total

    slot = pl.ds(pl.multiple_of((z * 2 + s) * shard, shard), shard)

    def my_rows(ref):
        return shard_of(ref, t)

    def to_owner(layer, ref, place_of, send_sems, recv_sems, hops=range(nz)):
        for k in hops:
            copy = remote(ref, place_of, send_sems.at[layer, k], recv_sems.at[k, s], (layer, t, along(k)))
            if k == 0:

                @pl.when(s == layer)
                def _():
                    pltpu.make_async_copy(ref, place_of, recv_sems.at[0, s]).start()

                pl.when(s != layer)(copy.start)
                later(copy, s != layer)
            else:
                copy.start()
                later(copy)

    def bundle(layer, hops):
        for k in hops:
            from_z = along(nz - k)
            rows_of = pl.ds(pl.multiple_of(from_z * 2 * shard, 2 * shard), 2 * shard)

            @pl.when(s == layer)
            def _(k=k, from_z=from_z):
                for core in range(2):
                    row = pl.multiple_of((from_z * 2 + core) * shard, shard)
                    place = b.da.at[t, pl.ds(row, shard), :]
                    pltpu.make_async_copy(place, place, b.da_r.at[k, core]).wait()

            for to in range(1, nt):
                place = b.da.at[t, rows_of, :]
                copy = remote(place, place, b.df_ss.at[k - 1, to - 1], b.df_rr.at[k - 1, to - 1], (s, around(to), z))
                pl.when(s == layer)(copy.start)
                later(copy, s == layer)

    def to_output(layer, ref, out, send_sems, recv_sems):
        to_z = base + s
        place = out.at[p, pl.ds(pl.multiple_of(t * shard, shard), shard), :]
        for k in range(nt):
            to_t = around(k)
            piece = ref.at[:, lanes(to_t, cols)]
            copy = remote(piece, place, send_sems.at[layer, k], recv_sems.at[p, k], (layer, to_t, to_z))
            if k == 0:
                here = (s == layer) & (to_z == z)

                @pl.when(here)
                def _(piece=piece):
                    pltpu.make_async_copy(piece, place, recv_sems.at[p, 0]).start()

                away = jnp.logical_not(here)
                pl.when(away)(copy.start)
                later(copy, away)
            else:
                copy.start()
                later(copy)

    for layer in range(2):
        full_in = b.full_in.at[layer]
        if layer == 0:
            for dt in range(nt):
                place = b.full_in.at[0, :, lanes(around(nt - dt), cols)]
                pltpu.make_async_copy(hid.at[0], place, b.hid_r.at[dt]).wait()
            for src_core in range(2):
                for i, (src_p, dst_p) in enumerate(params):
                    pltpu.make_async_copy(src_p, dst_p.at[src_core], b.par_l.at[src_core, i]).wait()
                for dt in range(nt):
                    place = b.alp.at[src_core, :, lanes(around(nt - dt), cols)]
                    pltpu.make_async_copy(alp_in, place, b.alp_r.at[src_core, dt]).wait()
        else:
            gather_wait(6, full_in)
        copy = remote(full_in, b.fi_p, b.fi_rs.at[0], b.fi_rs.at[1], peer)
        pl.when(s != layer)(copy.start)
        later(copy, s != layer)
        scale_qk = b.sqk[layer]
        wait_weight(layer, 0)
        x = full_in[...]
        own = pl.ds(pl.multiple_of(s * rows, rows), rows)
        for i in range(2):
            raw = mul(x, b.wq[layer, i])
            rotated = raw * b.cosb[...] + partner_cols(raw) * b.sinb[...]
            ratio = lax.rsqrt(head_total(rotated * rotated) / HEAD_DIM + EPSILON)
            b.rot[layer, i] = rotated
            b.rat[layer, i] = ratio
            normed = (rotated * ratio * scale_qk).astype(BF16)
            if i == 0:
                b.qb[layer] = normed
            else:
                b.kv[layer, own, 0:cols] = normed
        b.kv[layer, own, cols : 2 * cols] = mul(x, b.wq[layer, 2]).astype(BF16)
        mine = b.kv.at[layer, own, :]
        copy = remote(mine, mine, b.kv_rs.at[layer, 0], b.kv_rs.at[layer, 1], peer)
        pl.when(s == 0)(copy.start)
        later(copy, s == 0)
        pl.when(s == 1)(copy.wait_recv)
        att = jnp.zeros((rows, cols), F32)
        for h in range(heads):
            q_h = (b.qb[layer].astype(F32) * picks[h]).astype(BF16)
            scores = contract_cols(q_h, b.kv[layer, :, 0:cols]) * (1.0 / math.sqrt(HEAD_DIM)) + b.bias[...]
            top = jnp.max(scores, axis=1, keepdims=True)
            terms = jnp.exp(scores - top)
            prob = terms / jnp.sum(terms, axis=1, keepdims=True)
            b.prob[layer, h] = prob
            att = att + picks[h] * mul(prob.astype(BF16), b.kv[layer, :, cols : 2 * cols])
        b.at[layer] = att.astype(BF16)
        wait_weight(layer, 1)
        for n in range(0, width, tile):
            b.rs_s[layer, :, n : n + tile] = mul(b.at[layer], b.wo[layer, :, n : n + tile]).astype(BF16)
        scatter(layer)
        hin = my_rows(full_in)[...].astype(F32)
        rate_a = b.alp[layer, 0:1, :]
        rate_m = b.alp[layer, 1:2, :]
        araw = scatter_wait(layer)
        b.araw[layer] = araw
        zone = hin + rate_a * (ball(araw, width)[0] - hin)
        b.zone[layer] = zone
        mid = ball(zone, width)[0]
        b.mid[layer] = mid
        mid_full = b.mid_full.at[layer]
        my_rows(mid_full)[...] = mid.astype(BF16)
        gather(layer, mid_full)
        wait_weight(layer, 2)
        wait_weight(layer, 3)
        gather_wait(layer, mid_full)
        to_owner(layer, mid_full, b.xa.at[:, slot, :], b.xa_ss, b.xa_r)
        x = mid_full[...].reshape(rows, width)
        for n in range(0, hidden, tile):
            cut = slice(n, n + tile)
            up = mul(x, b.wu[layer, 0, :, cut])
            gate = mul(x, b.wu[layer, 1, :, cut])
            b.up[layer, :, cut] = up
            b.gate[layer, :, cut] = gate
            gate_s = gate * b.suv[layer, 1:2, cut]
            b.act[:, cut] = (up * b.suv[layer, 0:1, cut] * (gate_s / (1.0 + jnp.exp(-gate_s)))).astype(BF16)
        for n in range(0, width, tile):
            b.rs_s[2 + layer, :, n : n + tile] = mul(b.act[...], b.wd[layer, :, n : n + tile]).astype(BF16)
        scatter(2 + layer)
        mraw = scatter_wait(2 + layer)
        b.mraw[layer] = mraw
        ztwo = mid + rate_m * (ball(mraw, width)[0] - mid)
        b.ztwo[layer] = ztwo
        b.out_s[layer] = ball(ztwo, width)[0].astype(BF16)
        if layer == 0:
            my_rows(b.full_in.at[1])[...] = b.out_s[0]
            gather(6, b.full_in.at[1])
        to_output(layer, b.out_s.at[layer], lo, b.lo_ss, b.lo_r)

    mine_cols = lanes(z, section_rows)

    def block(k, suv_now):
        at = lax.rem(t + nt - k, nt)
        first = suv_now is None
        if first:
            for hop in range(nz):
                for core in range(2):
                    rows_of = pl.ds(pl.multiple_of((along(nz - hop) * 2 + core) * shard, shard), shard)
                    for ref, sems in ((b.xa, b.xa_r), (b.da, b.da_r)):
                        if ref is b.xa or hop == 0:
                            place = ref.at[:, rows_of, :]
                            pltpu.make_async_copy(place, place, sems.at[hop, core]).wait()
        else:
            for hop in range(1, nz):
                place = b.da.at[at, pl.ds(pl.multiple_of(along(nz - hop) * 2 * shard, 2 * shard), 2 * shard), :]
                remote(place, place, b.df_ss.at[hop - 1, k - 1], b.df_rr.at[hop - 1, k - 1], peer).wait_recv()

        def add(ref, value):
            ref[...] = value if first else ref[...] + value

        new = []
        for n in range(0, hidden, tile):
            cut = slice(n, n + tile)
            up = mul(b.xa[at], b.wu[s, 0, :, cut])
            gate = mul(b.xa[at], b.wu[s, 1, :, cut])
            d_act = contract_cols(b.da[at], b.wd[s, cut, :])
            scale_up, scale_gate = b.suv[s, 0:1, cut], b.suv[s, 1:2, cut]
            up_s = up * scale_up
            gate_s = gate * scale_gate
            sig = 1.0 / (1.0 + jnp.exp(-gate_s))
            b.act_b[:, cut] = (up_s * gate_s * sig).astype(BF16)
            d_up = d_act * gate_s * sig
            d_gate = d_act * up_s * sig * (1.0 + gate_s * (1.0 - sig))
            new.append((jnp.sum(d_up * up, axis=0, keepdims=True), jnp.sum(d_gate * gate, axis=0, keepdims=True)))
            x_cut = b.xa[at, :, mine_cols]
            add(b.acc.at[0, :, cut], contract_rows(x_cut, (d_up * scale_up).astype(BF16)))
            add(b.acc.at[1, :, cut], contract_rows(x_cut, (d_gate * scale_gate).astype(BF16)))
        for n in range(0, width, tile):
            cut = slice(n, n + tile)
            add(gd.at[:, cut], contract_rows(b.act_b[:, lanes(z, hidden // nz)], b.da[at, :, cut]))
        sums = tuple(jnp.concatenate([pair_of[i] for pair_of in new], axis=1) for i in range(2))
        return sums if first else tuple(now + more for now, more in zip(suv_now, sums))

    for dt in range(nt):
        place = b.cot_rows.at[:, lanes(around(nt - dt), cols)]
        pltpu.make_async_copy(cot.at[0, pl.ds(0, shard), :], place, b.cot_r.at[dt]).wait()
    grad_out = b.cot_rows[...].astype(F32)
    for layer in (1, 0):
        own = pl.ds(pl.multiple_of(s * rows, rows), rows)
        other = pl.ds(pl.multiple_of((1 - s) * rows, rows), rows)
        rate_a = b.alp[layer, 0:1, :]
        rate_m = b.alp[layer, 1:2, :]
        scale_qk = b.sqk[layer]
        mid = b.mid[layer]
        mraw_n, ratio_m = ball(b.mraw[layer], width)
        ratio_two = ball(b.ztwo[layer], width)[1]
        d_two = ball_back(b.ztwo[layer], ratio_two, grad_out, width)
        d_mid = (1.0 - rate_m) * d_two
        b.al_s[layer, 1:2, :] = jnp.sum(d_two * (mraw_n - mid), axis=0, keepdims=True)
        dml_full = b.dml_full.at[layer]
        my_rows(dml_full)[...] = ball_back(b.mraw[layer], ratio_m, rate_m * d_two, width).astype(BF16)
        gather(2 + layer, dml_full)
        to_owner(layer, my_rows(dml_full), b.da.at[t, slot, :], b.da_ss, b.da_r, range(1, nz))
        gather_wait(2 + layer, dml_full)
        to_owner(layer, dml_full, b.da.at[:, slot, :], b.da_ss, b.da_r, (0,))
        if layer == 0:
            bundle(1, (3,))
        x = dml_full[...].reshape(rows, width)
        for n in range(0, hidden, tile):
            cut = slice(n, n + tile)
            d_act = contract_cols(x, b.wd[layer, cut, :])
            scale_up, scale_gate = b.suv[layer, 0:1, cut], b.suv[layer, 1:2, cut]
            up_s = b.up[layer, :, cut] * scale_up
            gate_s = b.gate[layer, :, cut] * scale_gate
            sig = 1.0 / (1.0 + jnp.exp(-gate_s))
            b.duv[0, :, cut] = (d_act * gate_s * sig * scale_up).astype(BF16)
            b.duv[1, :, cut] = (d_act * up_s * sig * (1.0 + gate_s * (1.0 - sig)) * scale_gate).astype(BF16)
        for n in range(0, width, tile):
            cut = slice(n, n + tile)
            part = contract_cols(b.duv[0], b.wu[layer, 0, cut, :]) + contract_cols(b.duv[1], b.wu[layer, 1, cut, :])
            b.rs_s[4 + layer, :, cut] = part.astype(BF16)
        scatter(4 + layer)
        hin = my_rows(b.full_in.at[layer])[...].astype(F32)
        araw_n, ratio_a = ball(b.araw[layer], width)
        ratio_one = ball(b.zone[layer], width)[1]
        d_mid = d_mid + scatter_wait(4 + layer)
        d_one = ball_back(b.zone[layer], ratio_one, d_mid, width)
        b.al_s[layer, 0:1, :] = jnp.sum(d_one * (araw_n - hin), axis=0, keepdims=True)
        dat_full = b.dat_full.at[layer]
        my_rows(dat_full)[...] = ball_back(b.araw[layer], ratio_a, rate_a * d_one, width).astype(BF16)
        gather(4 + layer, dat_full)
        for k in range(1, nt):
            copy = remote(b.al_s.at[layer, :, lanes(around(k), cols)], b.al_r.at[layer, k - 1], b.al_ss.at[layer, k - 1], b.al_rr.at[layer, k - 1], (s, around(k), z))
            copy.start()
            later(copy)
        gather_wait(4 + layer, dat_full)
        bundle(layer, (1, 2))
        for src_v, dst_v, sems in ((dat_full, b.da_p, b.dap_rs), (b.at.at[layer], b.at_p, b.at_rs)):
            copy = remote(src_v, dst_v, sems.at[0], sems.at[1], peer)
            pl.when(s != layer)(copy.start)
            later(copy, s != layer)
        d_att = contract_cols(dat_full[...], b.wo[layer])
        dq = jnp.zeros((rows, cols), F32)
        dk = jnp.zeros((pair, cols), F32)
        dv = jnp.zeros((pair, cols), F32)
        for h in range(heads):
            d_att_h = (d_att * picks[h]).astype(BF16)
            q_h = (b.qb[layer].astype(F32) * picks[h]).astype(BF16)
            prob = b.prob[layer, h]
            d_prob = contract_cols(d_att_h, b.kv[layer, :, cols : 2 * cols])
            d_score = (prob * (d_prob - jnp.sum(prob * d_prob, axis=1, keepdims=True))).astype(BF16)
            dv = dv + contract_rows(prob.astype(BF16), d_att_h)
            dq = dq + picks[h] * mul(d_score, b.kv[layer, :, 0:cols])
            dk = dk + contract_rows(d_score, q_h)
        b.dkv_f[:, 0:cols] = dk * (1.0 / math.sqrt(HEAD_DIM))
        b.dkv_f[:, cols : 2 * cols] = dv
        b.dkv_s[layer] = b.dkv_f[other, :].astype(BF16)
        copy = remote(b.dkv_s.at[layer], b.dkv_r.at[layer], b.dkv_rs.at[layer, 0], b.dkv_rs.at[layer, 1], peer)
        pl.when(s == 1)(copy.start)
        later(copy, s == 1)

        @pl.when(s == layer)
        def _(layer=layer):
            for dst_v, sems in ((b.da_p, b.dap_rs), (b.at_p, b.at_rs)):
                remote(dst_v, dst_v, sems.at[0], sems.at[1], peer).wait_recv()
            for n in range(0, width, tile):
                cut = slice(n, n + tile)
                part = contract_rows(b.at[layer], b.dat_full[layer, :, cut]) + contract_rows(b.at_p[...], b.da_p[:, cut])
                b.wo_f[:, cut] = part
                b.wo_s[:, cut] = part.astype(BF16)
            for k in range(1, nz):
                piece = b.wo_s.at[pl.ds(pl.multiple_of(along(k) * chunk, chunk), chunk), :]
                remote(piece, b.wo_r.at[k - 1], b.wo_ss.at[k - 1], b.wo_rr.at[k - 1], (layer, t, along(k))).start()

        d_scale = jnp.zeros((1, cols), F32)
        for i in range(2):
            if i == 0:
                grad_n = dq * (1.0 / math.sqrt(HEAD_DIM))
            else:
                pl.when(s == 0)(copy.wait_recv)
                grad_n = b.dkv_f[own, 0:cols] + b.dkv_r[layer, :, 0:cols].astype(F32)
            rotated, ratio = b.rot[layer, i], b.rat[layer, i]
            d_scale = d_scale + jnp.sum(grad_n * rotated * ratio, axis=0, keepdims=True)
            d_unit = grad_n * scale_qk
            d_rot = ratio * d_unit - rotated * (ratio * ratio * ratio) * (head_total(d_unit * rotated) / HEAD_DIM)
            d_raw = d_rot * b.cosb[...] - partner_cols(d_rot * b.sinb[...])
            b.dqkv[layer, :, i * cols : (i + 1) * cols] = d_raw.astype(BF16)
        d_val = b.dkv_f[own, cols : 2 * cols] + b.dkv_r[layer, :, cols : 2 * cols].astype(F32)
        b.dqkv[layer, :, 2 * cols : 3 * cols] = d_val.astype(BF16)
        for n in range(0, width, tile):
            part = contract_cols(b.dqkv[layer, :, 0:cols], b.wq[layer, 0, n : n + tile, :])
            for i in range(1, 3):
                part = part + contract_cols(b.dqkv[layer, :, i * cols : (i + 1) * cols], b.wq[layer, i, n : n + tile, :])
            b.rs_s[6 + layer, :, n : n + tile] = part.astype(BF16)
        scatter(6 + layer)
        copy = remote(b.dqkv.at[layer], b.dq_p, b.dq_rs.at[0], b.dq_rs.at[1], peer)
        pl.when(s != layer)(copy.start)
        later(copy, s != layer)
        total = b.al_s[layer, :, lanes(t, cols)]
        for k in range(1, nt):
            place = b.al_r.at[layer, k - 1]
            remote(place, place, b.al_ss.at[layer, k - 1], b.al_rr.at[layer, k - 1], peer).wait_recv()
            total = total + place[...]
        b.small[layer] = total
        b.small[layer, 2:3, :] = d_scale
        to_owner(layer, b.small.at[layer], b.sm_r.at[lax.rem(z, nz), s], b.sm_ss, b.sm_rr)

        @pl.when(s == layer)
        def _(layer=layer):
            for dst_v, sems in ((b.fi_p, b.fi_rs), (b.dq_p, b.dq_rs)):
                remote(dst_v, dst_v, sems.at[0], sems.at[1], peer).wait_recv()
            for k in (1, 2, 3, 0):
                cut = lanes(along(k), section_rows)
                part = contract_rows(b.full_in[layer, :, cut], b.dqkv[layer]) + contract_rows(b.fi_p[:, cut], b.dq_p[...])
                if k:
                    b.wq_s[k - 1] = part.astype(BF16)
                    remote(b.wq_s.at[k - 1], b.wq_r.at[k - 1], b.wq_ss.at[k - 1], b.wq_rr.at[k - 1], (layer, t, along(k))).start()
                else:
                    for i in range(3):
                        gq[i] = part[:, i * cols : (i + 1) * cols]

        if layer == 0:
            bundle(0, (3,))
            suv = block(0, None)
        d_hin = (1.0 - rate_a) * d_one + scatter_wait(6 + layer)
        b.ig_s[layer] = d_hin.astype(BF16)
        to_output(layer, b.ig_s.at[layer], ig, b.ig_ss, b.ig_r)
        grad_out = b.ig_s[layer].astype(F32)

    suv = lax.fori_loop(1, nt, block, suv)
    for i in range(2):
        b.suv_b[i : i + 1, :] = suv[i]
    gsuv[...] = b.suv_b[:, lanes(z, hidden // nz)]
    per_row = 2 * hidden // 128
    for j in range(hidden // 128):
        for i in range(2):
            gu[pl.ds(2 * j + i, section_rows, stride=per_row), :] = b.acc[i, :, j * 128 : (j + 1) * 128]

    for k in range(1, nz):
        place = b.wq_r.at[k - 1]
        remote(place, place, b.wq_ss.at[k - 1], b.wq_rr.at[k - 1], peer).wait_recv()
        for i in range(3):
            gq[i] += b.wq_r[k - 1, :, i * cols : (i + 1) * cols].astype(F32)
    total = b.wo_f[pl.ds(pl.multiple_of(z * chunk, chunk), chunk), :]
    for k in range(1, nz):
        place = b.wo_r.at[k - 1]
        remote(place, place, b.wo_ss.at[k - 1], b.wo_rr.at[k - 1], peer).wait_recv()
        total = total + place[...].astype(F32)
    go[...] = total
    total = jnp.zeros((8, cols), F32)
    for k in range(nz):
        for core in range(2):
            place = b.sm_r.at[lax.rem(z + nz - k, nz), core]
            pltpu.make_async_copy(place, place, b.sm_rr.at[k, core]).wait()
            total = total + place[...]
    turned = pltpu.roll(total, lax.rem(cols - z * chunk, cols), 1)
    gal[...] = turned[0:2, 0:chunk]
    gsqk[...] = turned[2:3, 0:chunk]
    for out, sems in ((lo, b.lo_r), (ig, b.ig_r)):
        for m in range(2):
            for k in range(nt):
                place = out.at[m, pl.ds(pl.multiple_of(around(nt - k) * shard, shard), shard), :]
                pltpu.make_async_copy(place, place, sems.at[m, k]).wait()
    for k in range(nz - 1):
        remote(b.wq_s.at[k], b.wq_r.at[k], b.wq_ss.at[k], b.wq_rr.at[k], peer).wait_send()
        piece = b.wo_s.at[pl.ds(0, chunk), :]
        remote(piece, b.wo_r.at[k], b.wo_ss.at[k], b.wo_rr.at[k], peer).wait_send()
    for copy, when in pending:
        if when is None:
            copy.wait_send()
        else:
            pl.when(when)(copy.wait_send)


def copy_kernel(*refs):
    count = len(refs) // 3
    sems = refs[-1]
    reads = [pltpu.make_async_copy(refs[i], refs[2 * count + i], sems.at[0, i]) for i in range(count)]
    writes = [pltpu.make_async_copy(refs[2 * count + i], refs[count + i], sems.at[1, i]) for i in range(count)]
    for copy in reads:
        copy.start()
    for read, write in zip(reads, writes):
        read.wait()
        write.start()
    for copy in writes:
        copy.wait()


def per_device_fused(hidden_in, cotangent, lengths, w_qkv, w_out, w_ug, w_down, s_qk, s_uv, alpha):
    nt, nz = lax.axis_size("tensor"), lax.axis_size("dp")
    rows, cols = hidden_in.shape[1:]
    width, hidden = w_out.shape[2], w_down.shape[1]
    shard, section, chunk = rows // nt, width // nz, cols // nz
    half = HEAD_DIM // 2
    rates = (10000.0 ** (-(np.arange(cols) % half).astype(np.float32) / half)).astype(np.float32)[None, :]
    pairs = w_ug[0].reshape(width, 2, hidden // 128, 128).transpose(0, 2, 1, 3).reshape(2 * hidden // 128 * width, 128)
    scratch = buffers(nt, nz, rows, width, cols, hidden, shard, section, chunk)
    anywhere = pl.BlockSpec(memory_space=pl.ANY)
    vmem = pl.BlockSpec(memory_space=pltpu.VMEM)
    smem = pl.BlockSpec(memory_space=pltpu.SMEM)
    outs = pl.pallas_call(
        functools.partial(fused_kernel, tuple(scratch), nt, nz),
        out_shape=(
            jax.ShapeDtypeStruct((MICRO, rows, cols), BF16),
            jax.ShapeDtypeStruct((MICRO, rows, cols), BF16),
            jax.ShapeDtypeStruct((3, section, cols), F32),
            jax.ShapeDtypeStruct((chunk, width), F32),
            jax.ShapeDtypeStruct((section * 2 * hidden // 128, 128), F32),
            jax.ShapeDtypeStruct((hidden // nz, width), F32),
            jax.ShapeDtypeStruct((1, chunk), F32),
            jax.ShapeDtypeStruct((2, hidden // nz), F32),
            jax.ShapeDtypeStruct((2, chunk), F32),
        ),
        in_specs=[anywhere, anywhere, smem] + [anywhere] * 7 + [vmem],
        out_specs=(anywhere, anywhere) + (vmem,) * 7,
        scratch_shapes=list(scratch.values()),
        compiler_params=pltpu.CompilerParams(
            collective_id=0, has_side_effects=True, vmem_limit_bytes=60 * 2**20
        ),
    )(
        hidden_in,
        cotangent,
        lengths,
        jnp.transpose(w_qkv[0], (1, 0, 2)),
        w_out[0],
        pairs,
        w_down[0],
        s_qk,
        s_uv[0],
        alpha[0],
        jnp.asarray(rates),
    )
    lo, ig, gq, go, gu, gd, gsqk, gsuv, gal = pl.pallas_call(
        copy_kernel,
        out_shape=tuple(jax.ShapeDtypeStruct(o.shape, o.dtype) for o in outs),
        in_specs=[anywhere] * len(outs),
        out_specs=(anywhere,) * len(outs),
        scratch_shapes=[pltpu.VMEM(o.shape, o.dtype) for o in outs] + [pltpu.SemaphoreType.DMA((2, len(outs)))],
        compiler_params=pltpu.CompilerParams(vmem_limit_bytes=60 * 2**20),
    )(*outs)
    gu = gu.reshape(section, hidden // 128, 2, 128).transpose(0, 2, 1, 3).reshape(section, 2, hidden)
    return (
        lo[None],
        ig[None],
        jnp.transpose(gq, (1, 0, 2))[None],
        go[None],
        gu[None],
        gd[None],
        gsqk,
        gsuv[None],
        gal[None],
    )


def solution(mesh):
    placed = (
        P(None, "dp", "tensor"),
        P(None, "dp", "tensor"),
        P(),
        P("section", None, None, "tensor"),
        P("section", "tensor", None),
        P("section", None, None, "tensor"),
        P("section", "tensor", None),
        P("section", "tensor"),
        P("section", None, "tensor"),
        P("section", None, "tensor"),
    )
    per_rank = per_device_fused if mesh.shape["dp"] == 2 * MICRO and mesh.shape["tensor"] == 4 else per_device
    return jax.shard_map(
        per_rank,
        mesh=mesh,
        in_specs=placed,
        out_specs=(
            P("section", None, "dp", "tensor"),
            P("section", None, "dp", "tensor"),
            P("section", "dp", None, "tensor"),
            P("section", ("tensor", "dp"), None),
            P("section", "dp", None, "tensor"),
            P("section", ("tensor", "dp"), None),
            P("section", ("tensor", "dp")),
            P("section", None, ("tensor", "dp")),
            P("section", None, ("tensor", "dp")),
        ),
        check_vma=False,
    )
```

```python
import functools
import math
import types

import jax
import jax.numpy as jnp
import numpy as np
from jax import lax
from jax.experimental import pallas as pl
from jax.experimental.pallas import tpu as pltpu
from jax.sharding import PartitionSpec as P

D = 1024
HEAD_DIM = 64
SEQ_CAP = 4096


EPSILON = 1e-05
HIGHEST = lax.Precision.HIGHEST
NEG_LARGE = -1e30


def passed_along(array, axis, by):
    count = lax.axis_size(axis)
    return lax.ppermute(array, axis, [(i, (i + by) % count) for i in range(count)])


def from_behind(array, axis, by):
    count = lax.axis_size(axis)
    pairs = [(i, i + by) for i in range(count) if 0 <= i + by < count]
    return lax.ppermute(array, axis, pairs)


def seq_table(lengths_row, positions):
    count = lengths_row.shape[0]
    order = jnp.arange(count, dtype=jnp.int32)
    seq_end = jnp.sum(jnp.where(order[None, :] <= order[:, None], lengths_row[None, :], 0), axis=1)
    seq_start = seq_end - lengths_row
    segment = jnp.sum((positions[:, None] >= seq_end[None, :]).astype(jnp.int32), axis=1)
    labels = jnp.arange(lengths_row.shape[0], dtype=jnp.int32)
    first_tok = jnp.sum(
        jnp.where(segment[:, None] == labels[None, :], seq_start[None, :], 0), axis=1
    )
    return (segment, positions - first_tok)


def rope_tables(places, col_width):
    column = jnp.arange(col_width, dtype=jnp.int32) % HEAD_DIM
    half_dim = HEAD_DIM // 2
    rope_rates = 10000.0 ** (-(column % half_dim).astype(jnp.float32) / half_dim)
    angles = places.astype(jnp.float32)[:, None] * rope_rates[None, :]
    return (jnp.cos(angles), jnp.sin(angles), column < half_dim)


def partner(values, lower_half):
    half_dim = HEAD_DIM // 2
    return jnp.where(
        lower_half[None, :],
        -jnp.roll(values, -half_dim, axis=1),
        jnp.roll(values, half_dim, axis=1),
    )


def contract_rows(left_op, right_op):
    return lax.dot_general(
        left_op, right_op, (((0,), (0,)), ((), ())), preferred_element_type=jnp.float32
    )


def contract_cols(left_op, right_op):
    return lax.dot_general(
        left_op, right_op, (((1,), (1,)), ((), ())), preferred_element_type=jnp.float32
    )


def full_rows(columns):
    return lax.all_gather(columns, "tensor", axis=1, tiled=True)


def to_cols(partial_sum):
    return lax.psum_scatter(
        partial_sum.astype(jnp.bfloat16), "tensor", scatter_dimension=1, tiled=True
    ).astype(jnp.float32)


def grad_rows(columns):
    return lax.all_gather(columns, "tensor", axis=1, tiled=True)


def grad_cols(partial_sum):
    return lax.psum_scatter(
        partial_sum.astype(jnp.bfloat16), "tensor", scatter_dimension=1, tiled=True
    ).astype(jnp.float32)


def row_total(values):
    return lax.psum(jnp.sum(values, axis=1), "tensor")


def sphere(values):
    row_ratio = lax.rsqrt(row_total(values * values) / D + EPSILON)[:, None]
    return (values * row_ratio, row_ratio)


def sphere_back(source, row_ratio, grad_in):
    inner_sum = row_total(grad_in * source)[:, None]
    return row_ratio * grad_in - source * (row_ratio * row_ratio * row_ratio) * inner_sum / D


def pass_on(dkv_sum):
    return passed_along(dkv_sum.astype(jnp.bfloat16), "dp", 1).astype(dkv_sum.dtype)


def unchanged(previous):
    return previous


def per_device(hidden_in, cotangent, lengths, w_qkv, w_out, w_ug, w_down, s_qk, s_uv, alpha):
    micro_n = hidden_in.shape[0]
    tok_rows = hidden_in.shape[1]
    col_width = hidden_in.shape[2]
    heads_here = col_width // HEAD_DIM
    ff_here = w_down.shape[1]
    dp_ranks = lax.axis_size("dp")
    dp_rank = lax.axis_index("dp")
    longest = min(SEQ_CAP, tok_rows * dp_ranks // 2)
    reach_len = min(dp_ranks - 1, (longest + tok_rows - 2) // tok_rows)
    first_section = lax.axis_index("section") == 0
    score_div = math.sqrt(HEAD_DIM)
    qkv_mat = w_qkv[0].reshape(D, 3 * col_width)
    out_mat = w_out[0]
    ug_mat = w_ug[0].reshape(D, 2 * ff_here)
    down_mat = w_down[0]
    scale_qk = s_qk[0]
    scale_up = s_uv[0, 0]
    scale_gate = s_uv[0, 1]
    alpha_attn = alpha[0, 0]
    alpha_mlp = alpha[0, 1]
    local_rows = jnp.arange(tok_rows, dtype=jnp.int32)
    q_index = dp_rank * tok_rows + local_rows
    indicator = (
        jnp.arange(col_width, dtype=jnp.int32)[:, None] // HEAD_DIM
        == jnp.arange(heads_here, dtype=jnp.int32)[None, :]
    ).astype(jnp.float32)

    def head_sum(values):
        return jnp.dot(values, indicator, precision=HIGHEST, preferred_element_type=jnp.float32)

    def spread(small):
        return jnp.dot(small, indicator.T, precision=HIGHEST, preferred_element_type=jnp.float32)

    def block_info(lengths_row, q_segment, offset):
        source = dp_rank - offset
        k_index = source * tok_rows + local_rows
        k_segment, unused = seq_table(lengths_row, k_index)
        key_mask = (
            (k_segment[None, :] == q_segment[:, None])
            & (k_index[None, :] <= q_index[:, None])
            & (k_index[None, :] >= 0)
        )
        needed = (source * tok_rows + tok_rows - 1 >= 0) & (k_segment[tok_rows - 1] >= q_segment[0])
        return (key_mask, needed)

    def block_scores(q_heads, kv_block):
        key_heads = kv_block[:, :col_width].reshape(tok_rows, heads_here, HEAD_DIM)
        return (
            jnp.einsum("qhd,khd->hqk", q_heads, key_heads, preferred_element_type=jnp.float32)
            / score_div
        )

    def prep_back(grad_n, rotated, head_ratio, record):
        unit_vec = rotated * head_ratio
        d_scale = jnp.sum(grad_n * unit_vec, axis=0)
        d_unit = grad_n * scale_qk[None, :]
        d_rot = head_ratio * d_unit - rotated * (head_ratio * head_ratio * head_ratio) * spread(
            head_sum(d_unit * rotated) / HEAD_DIM
        )
        return (
            d_rot * record["cosine"] - partner(d_rot * record["sine_tab"], record["lower_half"]),
            d_scale,
        )

    received_in = jnp.zeros((tok_rows, col_width), jnp.bfloat16)
    records = []
    results = []
    for tick_no in range(micro_n + 1):
        early_mb = min(tick_no, micro_n - 1)
        late_mb = max(tick_no - 1, 0)
        lengths_row = jnp.where(first_section, lengths[early_mb], lengths[late_mb])
        layer_in = jnp.where(first_section, hidden_in[early_mb], received_in)
        hidden = layer_in.astype(jnp.float32)
        forward_q_segment, places = seq_table(lengths_row, q_index)
        cosine, sine_tab, lower_half = rope_tables(places, col_width)
        full_in = full_rows(hidden.astype(jnp.bfloat16))
        qkv = jnp.dot(full_in, qkv_mat, preferred_element_type=jnp.float32)
        q_raw = qkv[:, :col_width]
        k_raw = qkv[:, col_width : 2 * col_width]
        q_rot = q_raw * cosine + partner(q_raw, lower_half) * sine_tab
        k_rot = k_raw * cosine + partner(k_raw, lower_half) * sine_tab
        q_ratio = spread(lax.rsqrt(head_sum(q_rot * q_rot) / HEAD_DIM + EPSILON))
        k_ratio = spread(lax.rsqrt(head_sum(k_rot * k_rot) / HEAD_DIM + EPSILON))
        query_b = (q_rot * q_ratio * scale_qk[None, :]).astype(jnp.bfloat16)
        key_b = (k_rot * k_ratio * scale_qk[None, :]).astype(jnp.bfloat16)
        value_b = qkv[:, 2 * col_width :].astype(jnp.bfloat16)
        forward_q_heads = query_b.reshape(tok_rows, heads_here, HEAD_DIM)
        own_block = jnp.concatenate([key_b, value_b], axis=1)

        def lse_step(lse_state, kv_block, offset):
            key_mask, needed = block_info(lengths_row, forward_q_segment, offset)

            def update(previous):
                run_max, run_sum = previous
                masked = jnp.where(
                    key_mask[None], block_scores(forward_q_heads, kv_block), NEG_LARGE
                )
                new_max = jnp.maximum(run_max, jnp.max(masked, axis=2))
                exp_terms = jnp.where(key_mask[None], jnp.exp(masked - new_max[:, :, None]), 0.0)
                return (new_max, run_sum * jnp.exp(run_max - new_max) + jnp.sum(exp_terms, axis=2))

            return lax.cond(needed, update, unchanged, lse_state)

        init_state = (
            jnp.full((heads_here, tok_rows), NEG_LARGE, jnp.float32),
            jnp.zeros((heads_here, tok_rows), jnp.float32),
        )
        lse_state = lse_step(init_state, own_block, jnp.int32(0))

        def cycle_step(state_in, offset):
            kv_block, lse_now = state_in
            kv_block = from_behind(kv_block, "dp", 1)
            return ((kv_block, lse_step(lse_now, kv_block, offset)), kv_block)

        (forward_unused_block, lse_state), received = lax.scan(
            cycle_step, (own_block, lse_state), jnp.arange(1, reach_len + 1, dtype=jnp.int32)
        )
        kv_stack = jnp.concatenate([own_block[None], received], axis=0)
        forward_log_total = lse_state[0] + jnp.log(lse_state[1])

        def value_step(acc_heads, scan_item):
            kv_block, offset = scan_item
            key_mask, needed = block_info(lengths_row, forward_q_segment, offset)

            def add_values(previous):
                attn_prob = jnp.where(
                    key_mask[None],
                    jnp.exp(
                        block_scores(forward_q_heads, kv_block) - forward_log_total[:, :, None]
                    ),
                    0.0,
                ).astype(jnp.bfloat16)
                val_heads = kv_block[:, col_width:].reshape(tok_rows, heads_here, HEAD_DIM)
                return previous + jnp.einsum(
                    "hqk,khd->hqd", attn_prob, val_heads, preferred_element_type=jnp.float32
                )

            return (lax.cond(needed, add_values, unchanged, acc_heads), None)

        acc_heads, forward_unused_out = lax.scan(
            value_step,
            jnp.zeros((heads_here, tok_rows, HEAD_DIM), jnp.float32),
            (kv_stack, jnp.arange(reach_len + 1, dtype=jnp.int32)),
        )
        attended = jnp.transpose(acc_heads, (1, 0, 2)).reshape(tok_rows, col_width)
        attended_b = attended.astype(jnp.bfloat16)
        attn_raw = to_cols(jnp.dot(attended_b, out_mat, preferred_element_type=jnp.float32))
        attn_n, ratio_a = sphere(attn_raw)
        mix_one = hidden + alpha_attn[None, :] * (attn_n - hidden)
        normed_one, ratio_one = sphere(mix_one)
        inner_full = full_rows(normed_one.astype(jnp.bfloat16))
        forward_upgate = jnp.dot(inner_full, ug_mat, preferred_element_type=jnp.float32)
        forward_up_s = forward_upgate[:, :ff_here] * scale_up[None, :]
        forward_gate_s = forward_upgate[:, ff_here:] * scale_gate[None, :]
        act_b = (forward_up_s * jax.nn.silu(forward_gate_s)).astype(jnp.bfloat16)
        mlp_raw = to_cols(jnp.dot(act_b, down_mat, preferred_element_type=jnp.float32))
        mlp_n, ratio_m = sphere(mlp_raw)
        mix_two = normed_one + alpha_mlp[None, :] * (mlp_n - normed_one)
        result, ratio_two = sphere(mix_two)
        kept_blocks = own_block[None]
        forward_record = {
            "lengths_row": lengths_row,
            "q_segment": forward_q_segment,
            "cosine": cosine,
            "sine_tab": sine_tab,
            "lower_half": lower_half,
            "full_in": full_in,
            "q_rot": q_rot,
            "k_rot": k_rot,
            "q_ratio": q_ratio,
            "k_ratio": k_ratio,
            "query_b": query_b,
            "blocks": kept_blocks,
            "log_total": forward_log_total,
            "attended": attended,
            "attended_b": attended_b,
            "hidden": hidden,
            "attn_raw": attn_raw,
            "ratio_a": ratio_a,
            "attn_n": attn_n,
            "mix_one": mix_one,
            "ratio_one": ratio_one,
            "normed_one": normed_one,
            "inner_full": inner_full,
            "upgate": forward_upgate,
            "act_b": act_b,
            "mlp_raw": mlp_raw,
            "ratio_m": ratio_m,
            "mlp_n": mlp_n,
            "mix_two": mix_two,
            "ratio_two": ratio_two,
        }
        record, result = (forward_record, result)
        result_b = result.astype(jnp.bfloat16)
        records.append(record)
        results.append(result_b)
        if tick_no < micro_n:
            received_in = from_behind(result_b, "section", 1)
    layer_outputs = jnp.stack(
        [
            jnp.where(first_section, results[number], results[number + 1])
            for number in range(micro_n)
        ]
    )
    back_in = jnp.zeros((tok_rows, col_width), jnp.bfloat16)
    grad_totals = None
    back_results = []
    for tick_no in range(micro_n + 1):
        record = records[micro_n - tick_no]
        late_cot = cotangent[max(micro_n - 1 - tick_no, 0)].astype(jnp.float32)
        live_flag = jnp.where(
            first_section, 1.0 if tick_no >= 1 else 0.0, 1.0 if tick_no < micro_n else 0.0
        )
        grad_out = jnp.where(first_section, back_in.astype(jnp.float32), late_cot) * live_flag
        backward_lengths_row = record["lengths_row"]
        backward_q_segment = record["q_segment"]
        dz_two = sphere_back(record["mix_two"], record["ratio_two"], grad_out)
        d_normed = (1.0 - alpha_mlp)[None, :] * dz_two
        d_mlp_n = alpha_mlp[None, :] * dz_two
        d_alpha_mlp = jnp.sum(dz_two * (record["mlp_n"] - record["normed_one"]), axis=0)
        d_mlp = sphere_back(record["mlp_raw"], record["ratio_m"], d_mlp_n)
        d_mlp_full = grad_rows(d_mlp.astype(jnp.bfloat16))
        dw_down = contract_rows(record["act_b"], d_mlp_full)
        d_act = contract_cols(d_mlp_full, down_mat)
        upgate = record["upgate"]
        up_s = upgate[:, :ff_here] * scale_up[None, :]
        gate_s = upgate[:, ff_here:] * scale_gate[None, :]
        gate_sig = jax.nn.sigmoid(gate_s)
        d_up = d_act * gate_s * gate_sig
        d_gate = d_act * up_s * gate_sig * (1.0 + gate_s * (1.0 - gate_sig))
        d_scale_up = jnp.sum(d_up * upgate[:, :ff_here], axis=0)
        d_scale_gate = jnp.sum(d_gate * upgate[:, ff_here:], axis=0)
        d_upgate = jnp.concatenate(
            [d_up * scale_up[None, :], d_gate * scale_gate[None, :]], axis=1
        ).astype(jnp.bfloat16)
        dw_ug = contract_rows(record["inner_full"], d_upgate)
        d_normed = d_normed + grad_cols(contract_cols(d_upgate, ug_mat))
        dz_one = sphere_back(record["mix_one"], record["ratio_one"], d_normed)
        d_hidden = (1.0 - alpha_attn)[None, :] * dz_one
        d_attn_n = alpha_attn[None, :] * dz_one
        d_alpha_attn = jnp.sum(dz_one * (record["attn_n"] - record["hidden"]), axis=0)
        d_attn = sphere_back(record["attn_raw"], record["ratio_a"], d_attn_n)
        d_attn_full = grad_rows(d_attn.astype(jnp.bfloat16))
        dw_out = contract_rows(record["attended_b"], d_attn_full)
        d_attended = contract_cols(d_attn_full, out_mat).astype(jnp.bfloat16)
        row_delta = jnp.transpose(head_sum(d_attended.astype(jnp.float32) * record["attended"]))
        do_heads = d_attended.reshape(tok_rows, heads_here, HEAD_DIM)
        backward_q_heads = record["query_b"].reshape(tok_rows, heads_here, HEAD_DIM)
        log_total = record["log_total"]

        def block_grads(dq_now, kv_block, offset):
            key_mask, needed = block_info(backward_lengths_row, backward_q_segment, offset)

            def compute(previous):
                key_heads = kv_block[:, :col_width].reshape(tok_rows, heads_here, HEAD_DIM)
                val_heads = kv_block[:, col_width:].reshape(tok_rows, heads_here, HEAD_DIM)
                attn_prob = jnp.where(
                    key_mask[None],
                    jnp.exp(block_scores(backward_q_heads, kv_block) - log_total[:, :, None]),
                    0.0,
                )
                d_prob = jnp.einsum(
                    "qhd,khd->hqk", do_heads, val_heads, preferred_element_type=jnp.float32
                )
                d_val = jnp.einsum(
                    "hqk,qhd->khd",
                    attn_prob.astype(jnp.bfloat16),
                    do_heads,
                    preferred_element_type=jnp.float32,
                )
                d_score = (attn_prob * (d_prob - row_delta[:, :, None])).astype(jnp.bfloat16)
                new_dq = (
                    previous
                    + jnp.einsum(
                        "hqk,khd->hqd", d_score, key_heads, preferred_element_type=jnp.float32
                    )
                    / score_div
                )
                d_key = (
                    jnp.einsum(
                        "hqk,qhd->khd",
                        d_score,
                        backward_q_heads,
                        preferred_element_type=jnp.float32,
                    )
                    / score_div
                )
                return (
                    jnp.concatenate(
                        [d_key.reshape(tok_rows, col_width), d_val.reshape(tok_rows, col_width)],
                        axis=1,
                    ),
                    new_dq,
                )

            def skipped(previous):
                return (jnp.zeros((tok_rows, 2 * col_width), jnp.float32), previous)

            return lax.cond(needed, compute, skipped, dq_now)

        own_part, dq_acc = block_grads(
            jnp.zeros((heads_here, tok_rows, HEAD_DIM), jnp.float32),
            record["blocks"][0],
            jnp.int32(0),
        )
        offsets = jnp.arange(1, reach_len + 1, dtype=jnp.int32)

        def again_step(state_in, offset):
            dkv_sum, kv_block, dq_now = state_in
            dkv_sum = pass_on(dkv_sum)
            kv_block = from_behind(kv_block, "dp", 1)
            dkv_part, dq_now = block_grads(dq_now, kv_block, offset)
            return ((dkv_sum + dkv_part, kv_block, dq_now), None)

        (dkv_sum, unused_block, dq_acc), unused_out = lax.scan(
            again_step, (own_part, record["blocks"][0], dq_acc), offsets
        )
        dkv_home = passed_along(dkv_sum.astype(jnp.bfloat16), "dp", -reach_len).astype(
            dkv_sum.dtype
        )
        dq_full = jnp.transpose(dq_acc, (1, 0, 2)).reshape(tok_rows, col_width)
        dq_raw, ds_query = prep_back(dq_full, record["q_rot"], record["q_ratio"], record)
        dk_raw, ds_key = prep_back(
            dkv_home[:, :col_width], record["k_rot"], record["k_ratio"], record
        )
        d_qkv = jnp.concatenate([dq_raw, dk_raw, dkv_home[:, col_width:]], axis=1).astype(
            jnp.bfloat16
        )
        dw_qkv = contract_rows(record["full_in"], d_qkv)
        d_hidden = d_hidden + grad_cols(contract_cols(d_qkv, qkv_mat))
        grads = (
            dw_qkv.reshape(D, 3, col_width),
            dw_out,
            dw_ug.reshape(D, 2, ff_here),
            dw_down,
            ds_query + ds_key,
            jnp.stack([d_scale_up, d_scale_gate]),
            jnp.stack([d_alpha_attn, d_alpha_mlp]),
        )
        d_hidden, grads = (d_hidden, grads)
        grad_b = d_hidden.astype(jnp.bfloat16)
        back_results.append(grad_b)
        grad_totals = grads if grad_totals is None else jax.tree.map(jnp.add, grad_totals, grads)
        if tick_no < micro_n:
            back_in = from_behind(grad_b, "section", -1)
    input_grads = jnp.stack(
        [
            jnp.where(
                first_section, back_results[micro_n - number], back_results[micro_n - 1 - number]
            )
            for number in range(micro_n)
        ]
    )
    summed = (
        lax.psum_scatter(
            grad_totals[0].astype(jnp.bfloat16), "dp", scatter_dimension=0, tiled=True
        ).astype(jnp.float32),
        lax.psum_scatter(
            grad_totals[1].astype(jnp.bfloat16), "dp", scatter_dimension=0, tiled=True
        ).astype(jnp.float32),
        lax.psum_scatter(
            grad_totals[2].astype(jnp.bfloat16), "dp", scatter_dimension=0, tiled=True
        ).astype(jnp.float32),
        lax.psum_scatter(
            grad_totals[3].astype(jnp.bfloat16), "dp", scatter_dimension=0, tiled=True
        ).astype(jnp.float32),
        lax.psum_scatter(
            grad_totals[4].astype(jnp.bfloat16), "dp", scatter_dimension=0, tiled=True
        ).astype(jnp.float32),
        lax.psum_scatter(
            grad_totals[5].astype(jnp.bfloat16), "dp", scatter_dimension=1, tiled=True
        ).astype(jnp.float32),
        lax.psum_scatter(
            grad_totals[6].astype(jnp.bfloat16), "dp", scatter_dimension=1, tiled=True
        ).astype(jnp.float32),
    )
    return (
        layer_outputs[None],
        input_grads[None],
        summed[0][None],
        summed[1][None],
        summed[2][None],
        summed[3][None],
        summed[4][None],
        summed[5][None],
        summed[6][None],
    )


MESH = pl.DeviceIdType.MESH
MICRO = 2
F32 = jnp.float32
BF16 = jnp.bfloat16


def mul(left_op, right_op):
    return jnp.dot(left_op, right_op, preferred_element_type=F32)


def remote(src, dst, send_sem, recv_sem, device):
    return pltpu.make_async_remote_copy(
        src_ref=src, dst_ref=dst, send_sem=send_sem, recv_sem=recv_sem, device_id=device, device_id_type=MESH
    )


def ball(values, width):
    ratio = lax.rsqrt(jnp.sum(values * values, axis=1, keepdims=True) / width + EPSILON)
    return values * ratio, ratio


def ball_back(source, ratio, grad_in, width):
    inner = jnp.sum(grad_in * source, axis=1, keepdims=True)
    return ratio * grad_in - source * (ratio * ratio * ratio) * (inner / width)


def buffers(nt, nz, rows, width, cols, hidden, shard, section, chunk):
    vmem, dma = pltpu.VMEM, pltpu.SemaphoreType.DMA
    pair = 2 * rows
    return dict(
        wq=vmem((2, 3, width, cols), BF16),
        wo=vmem((2, cols, width), BF16),
        wu=vmem((2, 2, width, hidden), BF16),
        wd=vmem((2, hidden, width), BF16),
        sqk=vmem((2, 1, cols), F32),
        suv=vmem((2, 2, hidden), F32),
        alp=vmem((2, 2, width), F32),
        raw=vmem((2 * hidden // 128 * width, 128), BF16),
        raw_f=vmem((2 * hidden // 128 * 64, 128), F32),
        full_in=vmem((2, rows, width), BF16),
        mid_full=vmem((2, nt, shard, width), BF16),
        dml_full=vmem((2, nt, shard, width), BF16),
        dat_full=vmem((2, rows, width), BF16),
        fi_p=vmem((rows, width), BF16),
        at_p=vmem((rows, cols), BF16),
        da_p=vmem((rows, width), BF16),
        dq_p=vmem((rows, 3 * cols), BF16),
        xa=vmem((nt, nz * 2 * shard, width), BF16),
        da=vmem((nt, nz * 2 * shard, width), BF16),
        kv=vmem((2, pair, 2 * cols), BF16),
        dkv_f=vmem((pair, 2 * cols), F32),
        dkv_s=vmem((2, rows, 2 * cols), BF16),
        dkv_r=vmem((2, rows, 2 * cols), BF16),
        rs_s=vmem((8, rows, width), BF16),
        rs_r=vmem((8, nt - 1, shard, width), BF16),
        rot=vmem((2, 2, rows, cols), F32),
        rat=vmem((2, 2, rows, cols), F32),
        qb=vmem((2, rows, cols), BF16),
        prob=vmem((2, cols // HEAD_DIM, rows, pair), F32),
        at=vmem((2, rows, cols), BF16),
        araw=vmem((2, shard, width), F32),
        mraw=vmem((2, shard, width), F32),
        mid=vmem((2, shard, width), F32),
        zone=vmem((2, shard, width), F32),
        ztwo=vmem((2, shard, width), F32),
        up=vmem((2, rows, hidden), F32),
        gate=vmem((2, rows, hidden), F32),
        act=vmem((rows, hidden), BF16),
        duv=vmem((2, rows, hidden), BF16),
        dqkv=vmem((2, rows, 3 * cols), BF16),
        cot_rows=vmem((shard, width), BF16),
        out_s=vmem((2, shard, width), BF16),
        ig_s=vmem((2, shard, width), BF16),
        cosb=vmem((rows, cols), F32),
        sinb=vmem((rows, cols), F32),
        bias=vmem((rows, pair), F32),
        blk=vmem((cols, cols), BF16),
        al_s=vmem((2, 8, width), F32),
        al_r=vmem((2, nt - 1, 8, cols), F32),
        small=vmem((2, 8, cols), F32),
        sm_r=vmem((nz, 2, 8, cols), F32),
        wq_s=vmem((nz - 1, section, 3 * cols), BF16),
        wq_r=vmem((nz - 1, section, 3 * cols), BF16),
        wo_f=vmem((cols, width), F32),
        wo_s=vmem((cols, width), BF16),
        wo_r=vmem((nz - 1, chunk, width), BF16),
        act_b=vmem((nz * 2 * shard, hidden), BF16),
        suv_b=vmem((2, hidden), F32),
        acc=vmem((2, section, hidden), F32),
        w_l=dma((2, 4)), w_rs=dma((4,)),
        par_l=dma((2, 2)), par_s=dma((2,)),
        alp_r=dma((2, nt)), alp_s=dma((2, nt)),
        hid_r=dma((nt,)), hid_s=dma((2, nt)),
        cot_r=dma((nt,)), cot_s=dma((2, nt)),
        fi_rs=dma((2,)), at_rs=dma((2,)), dap_rs=dma((2,)), dq_rs=dma((2,)),
        kv_rs=dma((2, 2)), dkv_rs=dma((2, 2)),
        ag_ss=dma((7, nt - 1)), ag_rr=dma((7, nt - 1)),
        rs_ss=dma((8, nt - 1)), rs_rr=dma((8, nt - 1)),
        xa_r=dma((nz, 2)), xa_ss=dma((2, nz)),
        da_r=dma((nz, 2)), da_ss=dma((2, nz)),
        df_ss=dma((nz - 1, nt - 1)), df_rr=dma((nz - 1, nt - 1)),
        xf_ss=dma((nz - 1, nt - 1)), xf_rr=dma((nz - 1, nt - 1)),
        lo_ss=dma((2, nt)), lo_r=dma((2, nt)),
        ig_ss=dma((2, nt)), ig_r=dma((2, nt)),
        al_ss=dma((2, nt - 1)), al_rr=dma((2, nt - 1)),
        sm_ss=dma((2, nz)), sm_rr=dma((nz, 2)),
        wq_ss=dma((nz - 1,)), wq_rr=dma((nz - 1,)),
        wo_ss=dma((nz - 1,)), wo_rr=dma((nz - 1,)),
    )


def fused_kernel(names, nt, nz, *refs):
    hid, cot, lens, wq_in, wo_in, wu_in, wd_in, sqk_in, suv_in, alp_in, rates = refs[:11]
    lo, ig, gq, go, gu, gd, gsqk, gsuv, gal = refs[11:20]
    b = types.SimpleNamespace(**dict(zip(names, refs[20:])))
    rows, width = b.full_in.shape[1:]
    cols, hidden = b.qb.shape[2], b.wd.shape[1]
    shard = b.mid.shape[1]
    heads = cols // HEAD_DIM
    pair = 2 * rows
    section_rows = width // nz
    chunk = cols // nz
    tile = 512
    s, t, z = lax.axis_index("section"), lax.axis_index("tensor"), lax.axis_index("dp")
    p = lax.rem(z, 2)
    base = z - p
    peer = (1 - s, t, z)
    pending = []

    def around(k):
        return lax.rem(lax.div(t, 2) + k // 2, 2) * 2 + lax.rem(lax.rem(t, 2) + k % 2, 2)

    peers = (3, 1, 2)

    def along(k):
        return lax.rem(z + k, nz)

    def later(copy, when=None):
        pending.append((copy, when))

    def lanes(index, size):
        return pl.ds(pl.multiple_of(index * size, size), size)

    weights = [(wq_in, b.wq), (wo_in, b.wo), (None, b.wu), (wd_in, b.wd)]
    raw_copy = pltpu.make_async_copy(wu_in, b.raw, b.w_l.at[s, 2])
    raw_copy.start()
    for i in (0, 1, 3):
        src, dst = weights[i]
        pltpu.make_async_copy(src, dst.at[s], b.w_l.at[s, i]).start()
    params = [(sqk_in, b.sqk), (suv_in, b.suv)]
    for i, (src, dst) in enumerate(params):
        pltpu.make_async_copy(src, dst.at[s], b.par_l.at[s, i]).start()

    barrier = pltpu.get_barrier_semaphore()
    greeted = 0
    for dz in range(2):
        for dt in range(nt):
            for dc in range(2):
                if dz or dt or dc:
                    device = (lax.rem(s + dc, 2), around(dt), base + lax.rem(p + dz, 2))
                    pl.semaphore_signal(barrier, inc=1, device_id=device, device_id_type=MESH)
                    greeted += 1
    for dz in range(2, nz):
        for dc in range(2):
            device = (lax.rem(s + dc, 2), t, lax.rem(base + dz, nz))
            pl.semaphore_signal(barrier, inc=1, device_id=device, device_id_type=MESH)
            greeted += 1
    token0 = (base // 2) * pair
    pos_q = token0 + s * rows + lax.broadcasted_iota(jnp.int32, (rows, 1), 0)
    pos_k = token0 + lax.broadcasted_iota(jnp.int32, (1, pair), 1)

    def sequences(pos):
        seg = jnp.zeros_like(pos)
        first = jnp.zeros_like(pos)
        end = jnp.int32(0)
        for i in range(lens.shape[1]):
            end = end + lens[p, i]
            past = pos >= end
            seg = seg + past.astype(jnp.int32)
            first = jnp.where(past, end, first)
        return seg, pos - first

    seg_q, place_q = sequences(pos_q)
    seg_k, _ = sequences(pos_k)
    allowed = (seg_q == seg_k) & (pos_k <= pos_q)
    b.bias[...] = jnp.where(allowed, 0.0, NEG_LARGE)
    angle = place_q.astype(F32) * rates[...]
    b.cosb[...] = jnp.cos(angle)
    b.sinb[...] = jnp.sin(angle)
    col = lax.broadcasted_iota(jnp.int32, (1, cols), 1)
    lower = (col & (HEAD_DIM // 2)) == 0
    head_of = lax.shift_right_logical(col, 6)
    head_row = lax.shift_right_logical(lax.broadcasted_iota(jnp.int32, (cols, 1), 0), 6)
    b.blk[...] = jnp.where(head_row == head_of, 1.0, 0.0).astype(BF16)
    picks = [jnp.where(head_of == h, 1.0, 0.0) for h in range(heads)]
    b.al_s[...] = jnp.zeros_like(b.al_s)
    b.small[...] = jnp.zeros_like(b.small)

    @pl.when(s == 0)
    def _():
        b.kv[:, rows:pair, :] = jnp.zeros((2, rows, 2 * cols), BF16)

    @pl.when(s == 1)
    def _():
        b.dkv_r[...] = jnp.zeros_like(b.dkv_r)


    def to_order():
        raw_copy.wait()
        lines = 2 * hidden // 128

        def in_order(step, carry):
            b.raw_f[...] = b.raw[pl.ds(pl.multiple_of(step * lines * 64, lines * 64), lines * 64), :].astype(F32)
            at = pl.ds(pl.multiple_of(step * 64, 64), 64)
            for n in range(hidden // 128):
                for i in range(2):
                    b.wu[s, i, at, n * 128 : (n + 1) * 128] = b.raw_f[pl.ds(2 * n + i, 64, stride=lines), :].astype(BF16)
            return carry

        lax.fori_loop(0, width // 64, in_order, 0)

    pl.semaphore_wait(barrier, greeted)

    is_source = s == p
    for src, rs, ss in ((hid, b.hid_r, b.hid_s), (cot, b.cot_r, b.cot_s)):
        for dz in range(2):
            to_mb = lax.rem(p + dz, 2)
            for dt in peers + (0,):
                to_t = around(dt)
                if src is hid:
                    piece, place = src.at[to_mb], b.full_in.at[0, :, lanes(t, cols)]
                else:
                    piece = src.at[to_mb, pl.ds(pl.multiple_of(to_t * shard, shard), shard), :]
                    place = b.cot_rows.at[:, lanes(t, cols)]
                if dz == 0 and dt == 0:

                    @pl.when(is_source)
                    def _(piece=piece, place=place, rs=rs):
                        pltpu.make_async_copy(piece, place, rs.at[0]).start()
                else:
                    copy = remote(piece, place, ss.at[dz, dt], rs.at[dt], (s, to_t, base + to_mb))
                    pl.when(is_source)(copy.start)
                    later(copy, is_source)
        if src is hid:
            for i, (src_p, dst_p) in enumerate(params):
                copy = remote(src_p, dst_p.at[s], b.par_s.at[i], b.par_l.at[s, i], peer)
                copy.start()
                later(copy)
            alp_src, alp_dst = alp_in, b.alp.at[s, :, lanes(t, cols)]
            for dc in range(2):
                for dt in range(nt):
                    if dc == 0 and dt == 0:
                        pltpu.make_async_copy(alp_src, alp_dst, b.alp_r.at[s, 0]).start()
                    else:
                        copy = remote(alp_src, alp_dst, b.alp_s.at[dc, dt], b.alp_r.at[s, dt], (lax.rem(s + dc, 2), around(dt), z))
                        copy.start()
                        later(copy)
            for i in (0, 1, 3):
                src_w, dst_w = weights[i]
                copy = remote(src_w, dst_w.at[s], b.w_rs.at[i], b.w_l.at[s, i], peer)
                copy.start()
                later(copy)

    def wait_weight(layer, i):
        dst_w = weights[i][1].at[layer]
        wait = pltpu.make_async_copy(dst_w, dst_w, b.w_l.at[layer, i]).wait
        if i == 2:
            pl.when(s != layer)(wait)
        else:
            wait()

    to_order()
    copy = remote(b.wu.at[s], b.wu.at[s], b.w_rs.at[2], b.w_l.at[s, 2], peer)
    copy.start()
    later(copy)

    def partner_cols(x):
        half = HEAD_DIM // 2
        return jnp.where(lower, -pltpu.roll(x, cols - half, 1), pltpu.roll(x, half, 1))

    def head_total(x):
        high = x.astype(BF16)
        low = (x - high.astype(F32)).astype(BF16)
        return mul(high, b.blk[...]) + mul(low, b.blk[...])

    def shard_of(ref, index):
        return ref.at[index] if len(ref.shape) == 3 else ref.at[pl.ds(pl.multiple_of(index * shard, shard), shard), :]

    def gather(stage, ref):
        mine = shard_of(ref, t)
        for k in peers:
            copy = remote(mine, mine, b.ag_ss.at[stage, k - 1], b.ag_rr.at[stage, k - 1], (s, around(k), z))
            copy.start()
            later(copy)

    def gather_wait(stage, ref):
        for k in range(1, nt):
            theirs = shard_of(ref, around(k))
            remote(theirs, theirs, b.ag_ss.at[stage, k - 1], b.ag_rr.at[stage, k - 1], (s, around(k), z)).wait_recv()

    def scatter(stage):
        for k in peers:
            piece = b.rs_s.at[stage, pl.ds(pl.multiple_of(around(k) * shard, shard), shard), :]
            copy = remote(piece, b.rs_r.at[stage, k - 1], b.rs_ss.at[stage, k - 1], b.rs_rr.at[stage, k - 1], (s, around(k), z))
            copy.start()
            later(copy)

    def scatter_wait(stage):
        total = b.rs_s[stage, pl.ds(pl.multiple_of(t * shard, shard), shard), :].astype(F32)
        for k in range(1, nt):
            place = b.rs_r.at[stage, k - 1]
            remote(place, place, b.rs_ss.at[stage, k - 1], b.rs_rr.at[stage, k - 1], (s, around(k), z)).wait_recv()
            total = total + place[...].astype(F32)
        return total

    slot = pl.ds(pl.multiple_of((z * 2 + s) * shard, shard), shard)

    def my_rows(ref):
        return shard_of(ref, t)

    def to_owner(layer, ref, place_of, send_sems, recv_sems, hops=range(nz)):
        for k in hops:
            copy = remote(ref, place_of, send_sems.at[layer, k], recv_sems.at[k, s], (layer, t, along(k)))
            if k == 0:

                @pl.when(s == layer)
                def _():
                    pltpu.make_async_copy(ref, place_of, recv_sems.at[0, s]).start()

                pl.when(s != layer)(copy.start)
                later(copy, s != layer)
            else:
                copy.start()
                later(copy)

    x_rows = (b.xa, b.xa_r, b.xf_ss, b.xf_rr)
    d_rows = (b.da, b.da_r, b.df_ss, b.df_rr)

    def bundle(layer, hops, group):
        ref, arrived, send_sems, recv_sems = group
        for k in hops:
            from_z = along(nz - k)
            rows_of = pl.ds(pl.multiple_of(from_z * 2 * shard, 2 * shard), 2 * shard)

            @pl.when(s == layer)
            def _(k=k, from_z=from_z):
                for core in range(2):
                    row = pl.multiple_of((from_z * 2 + core) * shard, shard)
                    place = ref.at[t, pl.ds(row, shard), :]
                    pltpu.make_async_copy(place, place, arrived.at[k, core]).wait()

            for to in range(1, nt):
                place = ref.at[t, rows_of, :]
                copy = remote(place, place, send_sems.at[k - 1, to - 1], recv_sems.at[k - 1, to - 1], (s, around(to), z))
                pl.when(s == layer)(copy.start)
                later(copy, s == layer)

    def to_output(layer, ref, out, send_sems, recv_sems):
        to_z = base + s
        place = out.at[p, pl.ds(pl.multiple_of(t * shard, shard), shard), :]
        for k in range(nt):
            to_t = around(k)
            piece = ref.at[:, lanes(to_t, cols)]
            copy = remote(piece, place, send_sems.at[layer, k], recv_sems.at[p, k], (layer, to_t, to_z))
            if k == 0:
                here = (s == layer) & (to_z == z)

                @pl.when(here)
                def _(piece=piece):
                    pltpu.make_async_copy(piece, place, recv_sems.at[p, 0]).start()

                away = jnp.logical_not(here)
                pl.when(away)(copy.start)
                later(copy, away)
            else:
                copy.start()
                later(copy)

    for layer in range(2):
        full_in = b.full_in.at[layer]
        if layer == 0:
            for dt in range(nt):
                place = b.full_in.at[0, :, lanes(around(dt), cols)]
                pltpu.make_async_copy(hid.at[0], place, b.hid_r.at[dt]).wait()
            for src_core in range(2):
                for i, (src_p, dst_p) in enumerate(params):
                    pltpu.make_async_copy(src_p, dst_p.at[src_core], b.par_l.at[src_core, i]).wait()
                for dt in range(nt):
                    place = b.alp.at[src_core, :, lanes(around(dt), cols)]
                    pltpu.make_async_copy(alp_in, place, b.alp_r.at[src_core, dt]).wait()
        else:
            gather_wait(6, full_in)
        copy = remote(full_in, b.fi_p, b.fi_rs.at[0], b.fi_rs.at[1], peer)
        pl.when(s != layer)(copy.start)
        later(copy, s != layer)
        scale_qk = b.sqk[layer]
        wait_weight(layer, 0)
        x = full_in[...]
        own = pl.ds(pl.multiple_of(s * rows, rows), rows)
        for i in range(2):
            raw = mul(x, b.wq[layer, i])
            rotated = raw * b.cosb[...] + partner_cols(raw) * b.sinb[...]
            ratio = lax.rsqrt(head_total(rotated * rotated) / HEAD_DIM + EPSILON)
            b.rot[layer, i] = rotated
            b.rat[layer, i] = ratio
            normed = (rotated * ratio * scale_qk).astype(BF16)
            if i == 0:
                b.qb[layer] = normed
            else:
                b.kv[layer, own, 0:cols] = normed
        b.kv[layer, own, cols : 2 * cols] = mul(x, b.wq[layer, 2]).astype(BF16)
        mine = b.kv.at[layer, own, :]
        copy = remote(mine, mine, b.kv_rs.at[layer, 0], b.kv_rs.at[layer, 1], peer)
        pl.when(s == 0)(copy.start)
        later(copy, s == 0)
        pl.when(s == 1)(copy.wait_recv)
        att = jnp.zeros((rows, cols), F32)
        for h in range(heads):
            q_h = (b.qb[layer].astype(F32) * picks[h]).astype(BF16)
            scores = contract_cols(q_h, b.kv[layer, :, 0:cols]) * (1.0 / math.sqrt(HEAD_DIM)) + b.bias[...]
            top = jnp.max(scores, axis=1, keepdims=True)
            terms = jnp.exp(scores - top)
            prob = terms / jnp.sum(terms, axis=1, keepdims=True)
            b.prob[layer, h] = prob
            att = att + picks[h] * mul(prob.astype(BF16), b.kv[layer, :, cols : 2 * cols])
        b.at[layer] = att.astype(BF16)
        wait_weight(layer, 1)
        for n in range(0, width, tile):
            b.rs_s[layer, :, n : n + tile] = mul(b.at[layer], b.wo[layer, :, n : n + tile]).astype(BF16)
        scatter(layer)
        hin = my_rows(full_in)[...].astype(F32)
        rate_a = b.alp[layer, 0:1, :]
        rate_m = b.alp[layer, 1:2, :]
        araw = scatter_wait(layer)
        b.araw[layer] = araw
        zone = hin + rate_a * (ball(araw, width)[0] - hin)
        b.zone[layer] = zone
        mid = ball(zone, width)[0]
        b.mid[layer] = mid
        mid_full = b.mid_full.at[layer]
        my_rows(mid_full)[...] = mid.astype(BF16)
        gather(layer, mid_full)
        if layer == 1:
            to_owner(1, my_rows(mid_full), b.xa.at[t, slot, :], b.xa_ss, b.xa_r, range(1, nz))
        wait_weight(layer, 2)
        wait_weight(layer, 3)
        gather_wait(layer, mid_full)
        to_owner(layer, mid_full, b.xa.at[:, slot, :], b.xa_ss, b.xa_r, range(nz) if layer == 0 else (0,))
        x = mid_full[...].reshape(rows, width)
        for n in range(0, hidden, tile):
            cut = slice(n, n + tile)
            up = mul(x, b.wu[layer, 0, :, cut])
            gate = mul(x, b.wu[layer, 1, :, cut])
            b.up[layer, :, cut] = up
            b.gate[layer, :, cut] = gate
            gate_s = gate * b.suv[layer, 1:2, cut]
            b.act[:, cut] = (up * b.suv[layer, 0:1, cut] * (gate_s / (1.0 + jnp.exp(-gate_s)))).astype(BF16)
        for n in range(0, width, tile):
            b.rs_s[2 + layer, :, n : n + tile] = mul(b.act[...], b.wd[layer, :, n : n + tile]).astype(BF16)
        scatter(2 + layer)
        if layer == 1:
            bundle(1, (1,), x_rows)
        mraw = scatter_wait(2 + layer)
        b.mraw[layer] = mraw
        ztwo = mid + rate_m * (ball(mraw, width)[0] - mid)
        b.ztwo[layer] = ztwo
        b.out_s[layer] = ball(ztwo, width)[0].astype(BF16)
        if layer == 0:
            my_rows(b.full_in.at[1])[...] = b.out_s[0]
            gather(6, b.full_in.at[1])
        to_output(layer, b.out_s.at[layer], lo, b.lo_ss, b.lo_r)

    mine_cols = lanes(z, section_rows)

    def block(k, suv_now):
        at = lax.rem(lax.div(t, 2) + lax.div(k, 2), 2) * 2 + lax.rem(t + k, 2)
        first = suv_now is None
        if first:
            for hop in range(nz):
                for core in range(2):
                    rows_of = pl.ds(pl.multiple_of((along(nz - hop) * 2 + core) * shard, shard), shard)
                    for ref, sems in ((b.xa, b.xa_r), (b.da, b.da_r)):
                        place = ref.at[:, rows_of, :]
                        wait = pltpu.make_async_copy(place, place, sems.at[hop, core]).wait
                        if hop == 0:
                            wait()
                        elif ref is b.xa:
                            pl.when(s == 0)(wait)
        else:
            for hop in range(1, nz):
                for ref, _, ss, rr in (d_rows, x_rows):
                    place = ref.at[at, pl.ds(pl.multiple_of(along(nz - hop) * 2 * shard, 2 * shard), 2 * shard), :]
                    wait = remote(place, place, ss.at[hop - 1, k - 1], rr.at[hop - 1, k - 1], peer).wait_recv
                    if ref is b.da:
                        wait()
                    else:
                        pl.when(s == 1)(wait)

        def add(ref, value):
            ref[...] = value if first else ref[...] + value

        new = []
        for n in range(0, hidden, tile):
            cut = slice(n, n + tile)
            up = mul(b.xa[at], b.wu[s, 0, :, cut])
            gate = mul(b.xa[at], b.wu[s, 1, :, cut])
            d_act = contract_cols(b.da[at], b.wd[s, cut, :])
            scale_up, scale_gate = b.suv[s, 0:1, cut], b.suv[s, 1:2, cut]
            up_s = up * scale_up
            gate_s = gate * scale_gate
            sig = 1.0 / (1.0 + jnp.exp(-gate_s))
            b.act_b[:, cut] = (up_s * gate_s * sig).astype(BF16)
            d_up = d_act * gate_s * sig
            d_gate = d_act * up_s * sig * (1.0 + gate_s * (1.0 - sig))
            new.append((jnp.sum(d_up * up, axis=0, keepdims=True), jnp.sum(d_gate * gate, axis=0, keepdims=True)))
            x_cut = b.xa[at, :, mine_cols]
            add(b.acc.at[0, :, cut], contract_rows(x_cut, (d_up * scale_up).astype(BF16)))
            add(b.acc.at[1, :, cut], contract_rows(x_cut, (d_gate * scale_gate).astype(BF16)))
        for n in range(0, width, tile):
            cut = slice(n, n + tile)
            add(gd.at[:, cut], contract_rows(b.act_b[:, lanes(z, hidden // nz)], b.da[at, :, cut]))
        sums = tuple(jnp.concatenate([pair_of[i] for pair_of in new], axis=1) for i in range(2))
        return sums if first else tuple(now + more for now, more in zip(suv_now, sums))

    for dt in range(nt):
        place = b.cot_rows.at[:, lanes(around(dt), cols)]
        pltpu.make_async_copy(cot.at[0, pl.ds(0, shard), :], place, b.cot_r.at[dt]).wait()
    grad_out = b.cot_rows[...].astype(F32)
    for layer in (1, 0):
        own = pl.ds(pl.multiple_of(s * rows, rows), rows)
        other = pl.ds(pl.multiple_of((1 - s) * rows, rows), rows)
        rate_a = b.alp[layer, 0:1, :]
        rate_m = b.alp[layer, 1:2, :]
        scale_qk = b.sqk[layer]
        mid = b.mid[layer]
        mraw_n, ratio_m = ball(b.mraw[layer], width)
        ratio_two = ball(b.ztwo[layer], width)[1]
        d_two = ball_back(b.ztwo[layer], ratio_two, grad_out, width)
        d_mid = (1.0 - rate_m) * d_two
        b.al_s[layer, 1:2, :] = jnp.sum(d_two * (mraw_n - mid), axis=0, keepdims=True)
        dml_full = b.dml_full.at[layer]
        my_rows(dml_full)[...] = ball_back(b.mraw[layer], ratio_m, rate_m * d_two, width).astype(BF16)
        gather(2 + layer, dml_full)
        to_owner(layer, my_rows(dml_full), b.da.at[t, slot, :], b.da_ss, b.da_r, range(1, nz))
        if layer == 1:
            bundle(1, (2, 3), x_rows)
        gather_wait(2 + layer, dml_full)
        to_owner(layer, dml_full, b.da.at[:, slot, :], b.da_ss, b.da_r, (0,))
        if layer == 0:
            bundle(1, (3,), d_rows)
        x = dml_full[...].reshape(rows, width)
        for n in range(0, hidden, tile):
            cut = slice(n, n + tile)
            d_act = contract_cols(x, b.wd[layer, cut, :])
            scale_up, scale_gate = b.suv[layer, 0:1, cut], b.suv[layer, 1:2, cut]
            up_s = b.up[layer, :, cut] * scale_up
            gate_s = b.gate[layer, :, cut] * scale_gate
            sig = 1.0 / (1.0 + jnp.exp(-gate_s))
            b.duv[0, :, cut] = (d_act * gate_s * sig * scale_up).astype(BF16)
            b.duv[1, :, cut] = (d_act * up_s * sig * (1.0 + gate_s * (1.0 - sig)) * scale_gate).astype(BF16)
        for n in range(0, width, tile):
            cut = slice(n, n + tile)
            part = contract_cols(b.duv[0], b.wu[layer, 0, cut, :]) + contract_cols(b.duv[1], b.wu[layer, 1, cut, :])
            b.rs_s[4 + layer, :, cut] = part.astype(BF16)
        scatter(4 + layer)
        hin = my_rows(b.full_in.at[layer])[...].astype(F32)
        araw_n, ratio_a = ball(b.araw[layer], width)
        ratio_one = ball(b.zone[layer], width)[1]
        d_mid = d_mid + scatter_wait(4 + layer)
        d_one = ball_back(b.zone[layer], ratio_one, d_mid, width)
        b.al_s[layer, 0:1, :] = jnp.sum(d_one * (araw_n - hin), axis=0, keepdims=True)
        dat_full = b.dat_full.at[layer]
        my_rows(dat_full)[...] = ball_back(b.araw[layer], ratio_a, rate_a * d_one, width).astype(BF16)
        gather(4 + layer, dat_full)
        for k in range(1, nt):
            copy = remote(b.al_s.at[layer, :, lanes(around(k), cols)], b.al_r.at[layer, k - 1], b.al_ss.at[layer, k - 1], b.al_rr.at[layer, k - 1], (s, around(k), z))
            copy.start()
            later(copy)
        gather_wait(4 + layer, dat_full)
        for src_v, dst_v, sems in ((dat_full, b.da_p, b.dap_rs), (b.at.at[layer], b.at_p, b.at_rs)):
            copy = remote(src_v, dst_v, sems.at[0], sems.at[1], peer)
            pl.when(s != layer)(copy.start)
            later(copy, s != layer)
        d_att = contract_cols(dat_full[...], b.wo[layer])
        dq = jnp.zeros((rows, cols), F32)
        dk = jnp.zeros((pair, cols), F32)
        dv = jnp.zeros((pair, cols), F32)
        for h in range(heads):
            d_att_h = (d_att * picks[h]).astype(BF16)
            q_h = (b.qb[layer].astype(F32) * picks[h]).astype(BF16)
            prob = b.prob[layer, h]
            d_prob = contract_cols(d_att_h, b.kv[layer, :, cols : 2 * cols])
            d_score = (prob * (d_prob - jnp.sum(prob * d_prob, axis=1, keepdims=True))).astype(BF16)
            dv = dv + contract_rows(prob.astype(BF16), d_att_h)
            dq = dq + picks[h] * mul(d_score, b.kv[layer, :, 0:cols])
            dk = dk + contract_rows(d_score, q_h)
        bundle(layer, (1, 2), d_rows)
        b.dkv_f[:, 0:cols] = dk * (1.0 / math.sqrt(HEAD_DIM))
        b.dkv_f[:, cols : 2 * cols] = dv
        b.dkv_s[layer] = b.dkv_f[other, :].astype(BF16)
        copy = remote(b.dkv_s.at[layer], b.dkv_r.at[layer], b.dkv_rs.at[layer, 0], b.dkv_rs.at[layer, 1], peer)
        pl.when(s == 1)(copy.start)
        later(copy, s == 1)

        @pl.when(s == layer)
        def _(layer=layer):
            for dst_v, sems in ((b.da_p, b.dap_rs), (b.at_p, b.at_rs)):
                remote(dst_v, dst_v, sems.at[0], sems.at[1], peer).wait_recv()
            for n in range(0, width, tile):
                cut = slice(n, n + tile)
                part = contract_rows(b.at[layer], b.dat_full[layer, :, cut]) + contract_rows(b.at_p[...], b.da_p[:, cut])
                b.wo_f[:, cut] = part
                b.wo_s[:, cut] = part.astype(BF16)
            for k in range(1, nz):
                piece = b.wo_s.at[pl.ds(pl.multiple_of(along(k) * chunk, chunk), chunk), :]
                remote(piece, b.wo_r.at[k - 1], b.wo_ss.at[k - 1], b.wo_rr.at[k - 1], (layer, t, along(k))).start()

        d_scale = jnp.zeros((1, cols), F32)
        for i in range(2):
            if i == 0:
                grad_n = dq * (1.0 / math.sqrt(HEAD_DIM))
            else:
                pl.when(s == 0)(copy.wait_recv)
                grad_n = b.dkv_f[own, 0:cols] + b.dkv_r[layer, :, 0:cols].astype(F32)
            rotated, ratio = b.rot[layer, i], b.rat[layer, i]
            d_scale = d_scale + jnp.sum(grad_n * rotated * ratio, axis=0, keepdims=True)
            d_unit = grad_n * scale_qk
            d_rot = ratio * d_unit - rotated * (ratio * ratio * ratio) * (head_total(d_unit * rotated) / HEAD_DIM)
            d_raw = d_rot * b.cosb[...] - partner_cols(d_rot * b.sinb[...])
            b.dqkv[layer, :, i * cols : (i + 1) * cols] = d_raw.astype(BF16)
        d_val = b.dkv_f[own, cols : 2 * cols] + b.dkv_r[layer, :, cols : 2 * cols].astype(F32)
        b.dqkv[layer, :, 2 * cols : 3 * cols] = d_val.astype(BF16)
        for n in range(0, width, tile):
            part = contract_cols(b.dqkv[layer, :, 0:cols], b.wq[layer, 0, n : n + tile, :])
            for i in range(1, 3):
                part = part + contract_cols(b.dqkv[layer, :, i * cols : (i + 1) * cols], b.wq[layer, i, n : n + tile, :])
            b.rs_s[6 + layer, :, n : n + tile] = part.astype(BF16)
        scatter(6 + layer)
        copy = remote(b.dqkv.at[layer], b.dq_p, b.dq_rs.at[0], b.dq_rs.at[1], peer)
        pl.when(s != layer)(copy.start)
        later(copy, s != layer)
        total = b.al_s[layer, :, lanes(t, cols)]
        for k in range(1, nt):
            place = b.al_r.at[layer, k - 1]
            remote(place, place, b.al_ss.at[layer, k - 1], b.al_rr.at[layer, k - 1], peer).wait_recv()
            total = total + place[...]
        b.small[layer] = total
        b.small[layer, 2:3, :] = d_scale
        to_owner(layer, b.small.at[layer], b.sm_r.at[lax.rem(z, nz), s], b.sm_ss, b.sm_rr)

        @pl.when(s == layer)
        def _(layer=layer):
            for dst_v, sems in ((b.fi_p, b.fi_rs), (b.dq_p, b.dq_rs)):
                remote(dst_v, dst_v, sems.at[0], sems.at[1], peer).wait_recv()
            for k in (1, 2, 3, 0):
                cut = lanes(along(k), section_rows)
                part = contract_rows(b.full_in[layer, :, cut], b.dqkv[layer]) + contract_rows(b.fi_p[:, cut], b.dq_p[...])
                if k:
                    b.wq_s[k - 1] = part.astype(BF16)
                    remote(b.wq_s.at[k - 1], b.wq_r.at[k - 1], b.wq_ss.at[k - 1], b.wq_rr.at[k - 1], (layer, t, along(k))).start()
                else:
                    for i in range(3):
                        gq[i] = part[:, i * cols : (i + 1) * cols]

        if layer == 0:
            bundle(0, (3,), d_rows)
            suv = block(0, None)
        d_hin = (1.0 - rate_a) * d_one + scatter_wait(6 + layer)
        b.ig_s[layer] = d_hin.astype(BF16)
        to_output(layer, b.ig_s.at[layer], ig, b.ig_ss, b.ig_r)
        grad_out = b.ig_s[layer].astype(F32)

    suv = lax.fori_loop(1, nt, block, suv)
    for i in range(2):
        b.suv_b[i : i + 1, :] = suv[i]
    gsuv[...] = b.suv_b[:, lanes(z, hidden // nz)]
    per_row = 2 * hidden // 128
    for j in range(hidden // 128):
        for i in range(2):
            gu[pl.ds(2 * j + i, section_rows, stride=per_row), :] = b.acc[i, :, j * 128 : (j + 1) * 128]

    for k in range(1, nz):
        place = b.wq_r.at[k - 1]
        remote(place, place, b.wq_ss.at[k - 1], b.wq_rr.at[k - 1], peer).wait_recv()
        for i in range(3):
            gq[i] += b.wq_r[k - 1, :, i * cols : (i + 1) * cols].astype(F32)
    total = b.wo_f[pl.ds(pl.multiple_of(z * chunk, chunk), chunk), :]
    for k in range(1, nz):
        place = b.wo_r.at[k - 1]
        remote(place, place, b.wo_ss.at[k - 1], b.wo_rr.at[k - 1], peer).wait_recv()
        total = total + place[...].astype(F32)
    go[...] = total
    total = jnp.zeros((8, cols), F32)
    for k in range(nz):
        for core in range(2):
            place = b.sm_r.at[lax.rem(z + nz - k, nz), core]
            pltpu.make_async_copy(place, place, b.sm_rr.at[k, core]).wait()
            total = total + place[...]
    turned = pltpu.roll(total, lax.rem(cols - z * chunk, cols), 1)
    gal[...] = turned[0:2, 0:chunk]
    gsqk[...] = turned[2:3, 0:chunk]
    for out, sems in ((lo, b.lo_r), (ig, b.ig_r)):
        for m in range(2):
            for k in range(nt):
                place = out.at[m, pl.ds(pl.multiple_of(around(k) * shard, shard), shard), :]
                pltpu.make_async_copy(place, place, sems.at[m, k]).wait()
    for k in range(nz - 1):
        remote(b.wq_s.at[k], b.wq_r.at[k], b.wq_ss.at[k], b.wq_rr.at[k], peer).wait_send()
        piece = b.wo_s.at[pl.ds(0, chunk), :]
        remote(piece, b.wo_r.at[k], b.wo_ss.at[k], b.wo_rr.at[k], peer).wait_send()
    for copy, when in pending:
        if when is None:
            copy.wait_send()
        else:
            pl.when(when)(copy.wait_send)


def copy_kernel(*refs):
    count = len(refs) // 3
    sems = refs[-1]
    reads = [pltpu.make_async_copy(refs[i], refs[2 * count + i], sems.at[0, i]) for i in range(count)]
    writes = [pltpu.make_async_copy(refs[2 * count + i], refs[count + i], sems.at[1, i]) for i in range(count)]
    for copy in reads:
        copy.start()
    for read, write in zip(reads, writes):
        read.wait()
        write.start()
    for copy in writes:
        copy.wait()


def per_device_fused(hidden_in, cotangent, lengths, w_qkv, w_out, w_ug, w_down, s_qk, s_uv, alpha):
    nt, nz = lax.axis_size("tensor"), lax.axis_size("dp")
    rows, cols = hidden_in.shape[1:]
    width, hidden = w_out.shape[2], w_down.shape[1]
    shard, section, chunk = rows // nt, width // nz, cols // nz
    half = HEAD_DIM // 2
    rates = (10000.0 ** (-(np.arange(cols) % half).astype(np.float32) / half)).astype(np.float32)[None, :]
    pairs = w_ug[0].reshape(width, 2, hidden // 128, 128).transpose(0, 2, 1, 3).reshape(2 * hidden // 128 * width, 128)
    scratch = buffers(nt, nz, rows, width, cols, hidden, shard, section, chunk)
    anywhere = pl.BlockSpec(memory_space=pl.ANY)
    vmem = pl.BlockSpec(memory_space=pltpu.VMEM)
    smem = pl.BlockSpec(memory_space=pltpu.SMEM)
    outs = pl.pallas_call(
        functools.partial(fused_kernel, tuple(scratch), nt, nz),
        out_shape=(
            jax.ShapeDtypeStruct((MICRO, rows, cols), BF16),
            jax.ShapeDtypeStruct((MICRO, rows, cols), BF16),
            jax.ShapeDtypeStruct((3, section, cols), F32),
            jax.ShapeDtypeStruct((chunk, width), F32),
            jax.ShapeDtypeStruct((section * 2 * hidden // 128, 128), F32),
            jax.ShapeDtypeStruct((hidden // nz, width), F32),
            jax.ShapeDtypeStruct((1, chunk), F32),
            jax.ShapeDtypeStruct((2, hidden // nz), F32),
            jax.ShapeDtypeStruct((2, chunk), F32),
        ),
        in_specs=[anywhere, anywhere, smem] + [anywhere] * 7 + [vmem],
        out_specs=(anywhere, anywhere) + (vmem,) * 7,
        scratch_shapes=list(scratch.values()),
        compiler_params=pltpu.CompilerParams(
            collective_id=0, has_side_effects=True, vmem_limit_bytes=60 * 2**20
        ),
    )(
        hidden_in,
        cotangent,
        lengths,
        jnp.transpose(w_qkv[0], (1, 0, 2)),
        w_out[0],
        pairs,
        w_down[0],
        s_qk,
        s_uv[0],
        alpha[0],
        jnp.asarray(rates),
    )
    lo, ig, gq, go, gu, gd, gsqk, gsuv, gal = pl.pallas_call(
        copy_kernel,
        out_shape=tuple(jax.ShapeDtypeStruct(o.shape, o.dtype) for o in outs),
        in_specs=[anywhere] * len(outs),
        out_specs=(anywhere,) * len(outs),
        scratch_shapes=[pltpu.VMEM(o.shape, o.dtype) for o in outs] + [pltpu.SemaphoreType.DMA((2, len(outs)))],
        compiler_params=pltpu.CompilerParams(vmem_limit_bytes=60 * 2**20),
    )(*outs)
    gu = gu.reshape(section, hidden // 128, 2, 128).transpose(0, 2, 1, 3).reshape(section, 2, hidden)
    return (
        lo[None],
        ig[None],
        jnp.transpose(gq, (1, 0, 2))[None],
        go[None],
        gu[None],
        gd[None],
        gsqk,
        gsuv[None],
        gal[None],
    )


def solution(mesh):
    placed = (
        P(None, "dp", "tensor"),
        P(None, "dp", "tensor"),
        P(),
        P("section", None, None, "tensor"),
        P("section", "tensor", None),
        P("section", None, None, "tensor"),
        P("section", "tensor", None),
        P("section", "tensor"),
        P("section", None, "tensor"),
        P("section", None, "tensor"),
    )
    per_rank = per_device_fused if mesh.shape["dp"] == 2 * MICRO and mesh.shape["tensor"] == 4 else per_device
    return jax.shard_map(
        per_rank,
        mesh=mesh,
        in_specs=placed,
        out_specs=(
            P("section", None, "dp", "tensor"),
            P("section", None, "dp", "tensor"),
            P("section", "dp", None, "tensor"),
            P("section", ("tensor", "dp"), None),
            P("section", "dp", None, "tensor"),
            P("section", ("tensor", "dp"), None),
            P("section", ("tensor", "dp")),
            P("section", None, ("tensor", "dp")),
            P("section", None, ("tensor", "dp")),
        ),
        check_vma=False,
    )
```

```python
import functools
import math
import types

import jax
import jax.numpy as jnp
import numpy as np
from jax import lax
from jax.experimental import pallas as pl
from jax.experimental.pallas import tpu as pltpu
from jax.sharding import PartitionSpec as P

D = 1024
HEAD_DIM = 64
SEQ_CAP = 4096


EPSILON = 1e-05
HIGHEST = lax.Precision.HIGHEST
NEG_LARGE = -1e30


def passed_along(array, axis, by):
    count = lax.axis_size(axis)
    return lax.ppermute(array, axis, [(i, (i + by) % count) for i in range(count)])


def from_behind(array, axis, by):
    count = lax.axis_size(axis)
    pairs = [(i, i + by) for i in range(count) if 0 <= i + by < count]
    return lax.ppermute(array, axis, pairs)


def seq_table(lengths_row, positions):
    count = lengths_row.shape[0]
    order = jnp.arange(count, dtype=jnp.int32)
    seq_end = jnp.sum(jnp.where(order[None, :] <= order[:, None], lengths_row[None, :], 0), axis=1)
    seq_start = seq_end - lengths_row
    segment = jnp.sum((positions[:, None] >= seq_end[None, :]).astype(jnp.int32), axis=1)
    labels = jnp.arange(lengths_row.shape[0], dtype=jnp.int32)
    first_tok = jnp.sum(
        jnp.where(segment[:, None] == labels[None, :], seq_start[None, :], 0), axis=1
    )
    return (segment, positions - first_tok)


def rope_tables(places, col_width):
    column = jnp.arange(col_width, dtype=jnp.int32) % HEAD_DIM
    half_dim = HEAD_DIM // 2
    rope_rates = 10000.0 ** (-(column % half_dim).astype(jnp.float32) / half_dim)
    angles = places.astype(jnp.float32)[:, None] * rope_rates[None, :]
    return (jnp.cos(angles), jnp.sin(angles), column < half_dim)


def partner(values, lower_half):
    half_dim = HEAD_DIM // 2
    return jnp.where(
        lower_half[None, :],
        -jnp.roll(values, -half_dim, axis=1),
        jnp.roll(values, half_dim, axis=1),
    )


def contract_rows(left_op, right_op):
    return lax.dot_general(
        left_op, right_op, (((0,), (0,)), ((), ())), preferred_element_type=jnp.float32
    )


def contract_cols(left_op, right_op):
    return lax.dot_general(
        left_op, right_op, (((1,), (1,)), ((), ())), preferred_element_type=jnp.float32
    )


def full_rows(columns):
    return lax.all_gather(columns, "tensor", axis=1, tiled=True)


def to_cols(partial_sum):
    return lax.psum_scatter(
        partial_sum.astype(jnp.bfloat16), "tensor", scatter_dimension=1, tiled=True
    ).astype(jnp.float32)


def grad_rows(columns):
    return lax.all_gather(columns, "tensor", axis=1, tiled=True)


def grad_cols(partial_sum):
    return lax.psum_scatter(
        partial_sum.astype(jnp.bfloat16), "tensor", scatter_dimension=1, tiled=True
    ).astype(jnp.float32)


def row_total(values):
    return lax.psum(jnp.sum(values, axis=1), "tensor")


def sphere(values):
    row_ratio = lax.rsqrt(row_total(values * values) / D + EPSILON)[:, None]
    return (values * row_ratio, row_ratio)


def sphere_back(source, row_ratio, grad_in):
    inner_sum = row_total(grad_in * source)[:, None]
    return row_ratio * grad_in - source * (row_ratio * row_ratio * row_ratio) * inner_sum / D


def pass_on(dkv_sum):
    return passed_along(dkv_sum.astype(jnp.bfloat16), "dp", 1).astype(dkv_sum.dtype)


def unchanged(previous):
    return previous


def per_device(hidden_in, cotangent, lengths, w_qkv, w_out, w_ug, w_down, s_qk, s_uv, alpha):
    micro_n = hidden_in.shape[0]
    tok_rows = hidden_in.shape[1]
    col_width = hidden_in.shape[2]
    heads_here = col_width // HEAD_DIM
    ff_here = w_down.shape[1]
    dp_ranks = lax.axis_size("dp")
    dp_rank = lax.axis_index("dp")
    longest = min(SEQ_CAP, tok_rows * dp_ranks // 2)
    reach_len = min(dp_ranks - 1, (longest + tok_rows - 2) // tok_rows)
    first_section = lax.axis_index("section") == 0
    score_div = math.sqrt(HEAD_DIM)
    qkv_mat = w_qkv[0].reshape(D, 3 * col_width)
    out_mat = w_out[0]
    ug_mat = w_ug[0].reshape(D, 2 * ff_here)
    down_mat = w_down[0]
    scale_qk = s_qk[0]
    scale_up = s_uv[0, 0]
    scale_gate = s_uv[0, 1]
    alpha_attn = alpha[0, 0]
    alpha_mlp = alpha[0, 1]
    local_rows = jnp.arange(tok_rows, dtype=jnp.int32)
    q_index = dp_rank * tok_rows + local_rows
    indicator = (
        jnp.arange(col_width, dtype=jnp.int32)[:, None] // HEAD_DIM
        == jnp.arange(heads_here, dtype=jnp.int32)[None, :]
    ).astype(jnp.float32)

    def head_sum(values):
        return jnp.dot(values, indicator, precision=HIGHEST, preferred_element_type=jnp.float32)

    def spread(small):
        return jnp.dot(small, indicator.T, precision=HIGHEST, preferred_element_type=jnp.float32)

    def block_info(lengths_row, q_segment, offset):
        source = dp_rank - offset
        k_index = source * tok_rows + local_rows
        k_segment, unused = seq_table(lengths_row, k_index)
        key_mask = (
            (k_segment[None, :] == q_segment[:, None])
            & (k_index[None, :] <= q_index[:, None])
            & (k_index[None, :] >= 0)
        )
        needed = (source * tok_rows + tok_rows - 1 >= 0) & (k_segment[tok_rows - 1] >= q_segment[0])
        return (key_mask, needed)

    def block_scores(q_heads, kv_block):
        key_heads = kv_block[:, :col_width].reshape(tok_rows, heads_here, HEAD_DIM)
        return (
            jnp.einsum("qhd,khd->hqk", q_heads, key_heads, preferred_element_type=jnp.float32)
            / score_div
        )

    def prep_back(grad_n, rotated, head_ratio, record):
        unit_vec = rotated * head_ratio
        d_scale = jnp.sum(grad_n * unit_vec, axis=0)
        d_unit = grad_n * scale_qk[None, :]
        d_rot = head_ratio * d_unit - rotated * (head_ratio * head_ratio * head_ratio) * spread(
            head_sum(d_unit * rotated) / HEAD_DIM
        )
        return (
            d_rot * record["cosine"] - partner(d_rot * record["sine_tab"], record["lower_half"]),
            d_scale,
        )

    received_in = jnp.zeros((tok_rows, col_width), jnp.bfloat16)
    records = []
    results = []
    for tick_no in range(micro_n + 1):
        early_mb = min(tick_no, micro_n - 1)
        late_mb = max(tick_no - 1, 0)
        lengths_row = jnp.where(first_section, lengths[early_mb], lengths[late_mb])
        layer_in = jnp.where(first_section, hidden_in[early_mb], received_in)
        hidden = layer_in.astype(jnp.float32)
        forward_q_segment, places = seq_table(lengths_row, q_index)
        cosine, sine_tab, lower_half = rope_tables(places, col_width)
        full_in = full_rows(hidden.astype(jnp.bfloat16))
        qkv = jnp.dot(full_in, qkv_mat, preferred_element_type=jnp.float32)
        q_raw = qkv[:, :col_width]
        k_raw = qkv[:, col_width : 2 * col_width]
        q_rot = q_raw * cosine + partner(q_raw, lower_half) * sine_tab
        k_rot = k_raw * cosine + partner(k_raw, lower_half) * sine_tab
        q_ratio = spread(lax.rsqrt(head_sum(q_rot * q_rot) / HEAD_DIM + EPSILON))
        k_ratio = spread(lax.rsqrt(head_sum(k_rot * k_rot) / HEAD_DIM + EPSILON))
        query_b = (q_rot * q_ratio * scale_qk[None, :]).astype(jnp.bfloat16)
        key_b = (k_rot * k_ratio * scale_qk[None, :]).astype(jnp.bfloat16)
        value_b = qkv[:, 2 * col_width :].astype(jnp.bfloat16)
        forward_q_heads = query_b.reshape(tok_rows, heads_here, HEAD_DIM)
        own_block = jnp.concatenate([key_b, value_b], axis=1)

        def lse_step(lse_state, kv_block, offset):
            key_mask, needed = block_info(lengths_row, forward_q_segment, offset)

            def update(previous):
                run_max, run_sum = previous
                masked = jnp.where(
                    key_mask[None], block_scores(forward_q_heads, kv_block), NEG_LARGE
                )
                new_max = jnp.maximum(run_max, jnp.max(masked, axis=2))
                exp_terms = jnp.where(key_mask[None], jnp.exp(masked - new_max[:, :, None]), 0.0)
                return (new_max, run_sum * jnp.exp(run_max - new_max) + jnp.sum(exp_terms, axis=2))

            return lax.cond(needed, update, unchanged, lse_state)

        init_state = (
            jnp.full((heads_here, tok_rows), NEG_LARGE, jnp.float32),
            jnp.zeros((heads_here, tok_rows), jnp.float32),
        )
        lse_state = lse_step(init_state, own_block, jnp.int32(0))

        def cycle_step(state_in, offset):
            kv_block, lse_now = state_in
            kv_block = from_behind(kv_block, "dp", 1)
            return ((kv_block, lse_step(lse_now, kv_block, offset)), kv_block)

        (forward_unused_block, lse_state), received = lax.scan(
            cycle_step, (own_block, lse_state), jnp.arange(1, reach_len + 1, dtype=jnp.int32)
        )
        kv_stack = jnp.concatenate([own_block[None], received], axis=0)
        forward_log_total = lse_state[0] + jnp.log(lse_state[1])

        def value_step(acc_heads, scan_item):
            kv_block, offset = scan_item
            key_mask, needed = block_info(lengths_row, forward_q_segment, offset)

            def add_values(previous):
                attn_prob = jnp.where(
                    key_mask[None],
                    jnp.exp(
                        block_scores(forward_q_heads, kv_block) - forward_log_total[:, :, None]
                    ),
                    0.0,
                ).astype(jnp.bfloat16)
                val_heads = kv_block[:, col_width:].reshape(tok_rows, heads_here, HEAD_DIM)
                return previous + jnp.einsum(
                    "hqk,khd->hqd", attn_prob, val_heads, preferred_element_type=jnp.float32
                )

            return (lax.cond(needed, add_values, unchanged, acc_heads), None)

        acc_heads, forward_unused_out = lax.scan(
            value_step,
            jnp.zeros((heads_here, tok_rows, HEAD_DIM), jnp.float32),
            (kv_stack, jnp.arange(reach_len + 1, dtype=jnp.int32)),
        )
        attended = jnp.transpose(acc_heads, (1, 0, 2)).reshape(tok_rows, col_width)
        attended_b = attended.astype(jnp.bfloat16)
        attn_raw = to_cols(jnp.dot(attended_b, out_mat, preferred_element_type=jnp.float32))
        attn_n, ratio_a = sphere(attn_raw)
        mix_one = hidden + alpha_attn[None, :] * (attn_n - hidden)
        normed_one, ratio_one = sphere(mix_one)
        inner_full = full_rows(normed_one.astype(jnp.bfloat16))
        forward_upgate = jnp.dot(inner_full, ug_mat, preferred_element_type=jnp.float32)
        forward_up_s = forward_upgate[:, :ff_here] * scale_up[None, :]
        forward_gate_s = forward_upgate[:, ff_here:] * scale_gate[None, :]
        act_b = (forward_up_s * jax.nn.silu(forward_gate_s)).astype(jnp.bfloat16)
        mlp_raw = to_cols(jnp.dot(act_b, down_mat, preferred_element_type=jnp.float32))
        mlp_n, ratio_m = sphere(mlp_raw)
        mix_two = normed_one + alpha_mlp[None, :] * (mlp_n - normed_one)
        result, ratio_two = sphere(mix_two)
        kept_blocks = own_block[None]
        forward_record = {
            "lengths_row": lengths_row,
            "q_segment": forward_q_segment,
            "cosine": cosine,
            "sine_tab": sine_tab,
            "lower_half": lower_half,
            "full_in": full_in,
            "q_rot": q_rot,
            "k_rot": k_rot,
            "q_ratio": q_ratio,
            "k_ratio": k_ratio,
            "query_b": query_b,
            "blocks": kept_blocks,
            "log_total": forward_log_total,
            "attended": attended,
            "attended_b": attended_b,
            "hidden": hidden,
            "attn_raw": attn_raw,
            "ratio_a": ratio_a,
            "attn_n": attn_n,
            "mix_one": mix_one,
            "ratio_one": ratio_one,
            "normed_one": normed_one,
            "inner_full": inner_full,
            "upgate": forward_upgate,
            "act_b": act_b,
            "mlp_raw": mlp_raw,
            "ratio_m": ratio_m,
            "mlp_n": mlp_n,
            "mix_two": mix_two,
            "ratio_two": ratio_two,
        }
        record, result = (forward_record, result)
        result_b = result.astype(jnp.bfloat16)
        records.append(record)
        results.append(result_b)
        if tick_no < micro_n:
            received_in = from_behind(result_b, "section", 1)
    layer_outputs = jnp.stack(
        [
            jnp.where(first_section, results[number], results[number + 1])
            for number in range(micro_n)
        ]
    )
    back_in = jnp.zeros((tok_rows, col_width), jnp.bfloat16)
    grad_totals = None
    back_results = []
    for tick_no in range(micro_n + 1):
        record = records[micro_n - tick_no]
        late_cot = cotangent[max(micro_n - 1 - tick_no, 0)].astype(jnp.float32)
        live_flag = jnp.where(
            first_section, 1.0 if tick_no >= 1 else 0.0, 1.0 if tick_no < micro_n else 0.0
        )
        grad_out = jnp.where(first_section, back_in.astype(jnp.float32), late_cot) * live_flag
        backward_lengths_row = record["lengths_row"]
        backward_q_segment = record["q_segment"]
        dz_two = sphere_back(record["mix_two"], record["ratio_two"], grad_out)
        d_normed = (1.0 - alpha_mlp)[None, :] * dz_two
        d_mlp_n = alpha_mlp[None, :] * dz_two
        d_alpha_mlp = jnp.sum(dz_two * (record["mlp_n"] - record["normed_one"]), axis=0)
        d_mlp = sphere_back(record["mlp_raw"], record["ratio_m"], d_mlp_n)
        d_mlp_full = grad_rows(d_mlp.astype(jnp.bfloat16))
        dw_down = contract_rows(record["act_b"], d_mlp_full)
        d_act = contract_cols(d_mlp_full, down_mat)
        upgate = record["upgate"]
        up_s = upgate[:, :ff_here] * scale_up[None, :]
        gate_s = upgate[:, ff_here:] * scale_gate[None, :]
        gate_sig = jax.nn.sigmoid(gate_s)
        d_up = d_act * gate_s * gate_sig
        d_gate = d_act * up_s * gate_sig * (1.0 + gate_s * (1.0 - gate_sig))
        d_scale_up = jnp.sum(d_up * upgate[:, :ff_here], axis=0)
        d_scale_gate = jnp.sum(d_gate * upgate[:, ff_here:], axis=0)
        d_upgate = jnp.concatenate(
            [d_up * scale_up[None, :], d_gate * scale_gate[None, :]], axis=1
        ).astype(jnp.bfloat16)
        dw_ug = contract_rows(record["inner_full"], d_upgate)
        d_normed = d_normed + grad_cols(contract_cols(d_upgate, ug_mat))
        dz_one = sphere_back(record["mix_one"], record["ratio_one"], d_normed)
        d_hidden = (1.0 - alpha_attn)[None, :] * dz_one
        d_attn_n = alpha_attn[None, :] * dz_one
        d_alpha_attn = jnp.sum(dz_one * (record["attn_n"] - record["hidden"]), axis=0)
        d_attn = sphere_back(record["attn_raw"], record["ratio_a"], d_attn_n)
        d_attn_full = grad_rows(d_attn.astype(jnp.bfloat16))
        dw_out = contract_rows(record["attended_b"], d_attn_full)
        d_attended = contract_cols(d_attn_full, out_mat).astype(jnp.bfloat16)
        row_delta = jnp.transpose(head_sum(d_attended.astype(jnp.float32) * record["attended"]))
        do_heads = d_attended.reshape(tok_rows, heads_here, HEAD_DIM)
        backward_q_heads = record["query_b"].reshape(tok_rows, heads_here, HEAD_DIM)
        log_total = record["log_total"]

        def block_grads(dq_now, kv_block, offset):
            key_mask, needed = block_info(backward_lengths_row, backward_q_segment, offset)

            def compute(previous):
                key_heads = kv_block[:, :col_width].reshape(tok_rows, heads_here, HEAD_DIM)
                val_heads = kv_block[:, col_width:].reshape(tok_rows, heads_here, HEAD_DIM)
                attn_prob = jnp.where(
                    key_mask[None],
                    jnp.exp(block_scores(backward_q_heads, kv_block) - log_total[:, :, None]),
                    0.0,
                )
                d_prob = jnp.einsum(
                    "qhd,khd->hqk", do_heads, val_heads, preferred_element_type=jnp.float32
                )
                d_val = jnp.einsum(
                    "hqk,qhd->khd",
                    attn_prob.astype(jnp.bfloat16),
                    do_heads,
                    preferred_element_type=jnp.float32,
                )
                d_score = (attn_prob * (d_prob - row_delta[:, :, None])).astype(jnp.bfloat16)
                new_dq = (
                    previous
                    + jnp.einsum(
                        "hqk,khd->hqd", d_score, key_heads, preferred_element_type=jnp.float32
                    )
                    / score_div
                )
                d_key = (
                    jnp.einsum(
                        "hqk,qhd->khd",
                        d_score,
                        backward_q_heads,
                        preferred_element_type=jnp.float32,
                    )
                    / score_div
                )
                return (
                    jnp.concatenate(
                        [d_key.reshape(tok_rows, col_width), d_val.reshape(tok_rows, col_width)],
                        axis=1,
                    ),
                    new_dq,
                )

            def skipped(previous):
                return (jnp.zeros((tok_rows, 2 * col_width), jnp.float32), previous)

            return lax.cond(needed, compute, skipped, dq_now)

        own_part, dq_acc = block_grads(
            jnp.zeros((heads_here, tok_rows, HEAD_DIM), jnp.float32),
            record["blocks"][0],
            jnp.int32(0),
        )
        offsets = jnp.arange(1, reach_len + 1, dtype=jnp.int32)

        def again_step(state_in, offset):
            dkv_sum, kv_block, dq_now = state_in
            dkv_sum = pass_on(dkv_sum)
            kv_block = from_behind(kv_block, "dp", 1)
            dkv_part, dq_now = block_grads(dq_now, kv_block, offset)
            return ((dkv_sum + dkv_part, kv_block, dq_now), None)

        (dkv_sum, unused_block, dq_acc), unused_out = lax.scan(
            again_step, (own_part, record["blocks"][0], dq_acc), offsets
        )
        dkv_home = passed_along(dkv_sum.astype(jnp.bfloat16), "dp", -reach_len).astype(
            dkv_sum.dtype
        )
        dq_full = jnp.transpose(dq_acc, (1, 0, 2)).reshape(tok_rows, col_width)
        dq_raw, ds_query = prep_back(dq_full, record["q_rot"], record["q_ratio"], record)
        dk_raw, ds_key = prep_back(
            dkv_home[:, :col_width], record["k_rot"], record["k_ratio"], record
        )
        d_qkv = jnp.concatenate([dq_raw, dk_raw, dkv_home[:, col_width:]], axis=1).astype(
            jnp.bfloat16
        )
        dw_qkv = contract_rows(record["full_in"], d_qkv)
        d_hidden = d_hidden + grad_cols(contract_cols(d_qkv, qkv_mat))
        grads = (
            dw_qkv.reshape(D, 3, col_width),
            dw_out,
            dw_ug.reshape(D, 2, ff_here),
            dw_down,
            ds_query + ds_key,
            jnp.stack([d_scale_up, d_scale_gate]),
            jnp.stack([d_alpha_attn, d_alpha_mlp]),
        )
        d_hidden, grads = (d_hidden, grads)
        grad_b = d_hidden.astype(jnp.bfloat16)
        back_results.append(grad_b)
        grad_totals = grads if grad_totals is None else jax.tree.map(jnp.add, grad_totals, grads)
        if tick_no < micro_n:
            back_in = from_behind(grad_b, "section", -1)
    input_grads = jnp.stack(
        [
            jnp.where(
                first_section, back_results[micro_n - number], back_results[micro_n - 1 - number]
            )
            for number in range(micro_n)
        ]
    )
    summed = (
        lax.psum_scatter(
            grad_totals[0].astype(jnp.bfloat16), "dp", scatter_dimension=0, tiled=True
        ).astype(jnp.float32),
        lax.psum_scatter(
            grad_totals[1].astype(jnp.bfloat16), "dp", scatter_dimension=0, tiled=True
        ).astype(jnp.float32),
        lax.psum_scatter(
            grad_totals[2].astype(jnp.bfloat16), "dp", scatter_dimension=0, tiled=True
        ).astype(jnp.float32),
        lax.psum_scatter(
            grad_totals[3].astype(jnp.bfloat16), "dp", scatter_dimension=0, tiled=True
        ).astype(jnp.float32),
        lax.psum_scatter(
            grad_totals[4].astype(jnp.bfloat16), "dp", scatter_dimension=0, tiled=True
        ).astype(jnp.float32),
        lax.psum_scatter(
            grad_totals[5].astype(jnp.bfloat16), "dp", scatter_dimension=1, tiled=True
        ).astype(jnp.float32),
        lax.psum_scatter(
            grad_totals[6].astype(jnp.bfloat16), "dp", scatter_dimension=1, tiled=True
        ).astype(jnp.float32),
    )
    return (
        layer_outputs[None],
        input_grads[None],
        summed[0][None],
        summed[1][None],
        summed[2][None],
        summed[3][None],
        summed[4][None],
        summed[5][None],
        summed[6][None],
    )


MESH = pl.DeviceIdType.MESH
MICRO = 2
F32 = jnp.float32
BF16 = jnp.bfloat16


def mul(left_op, right_op):
    return jnp.dot(left_op, right_op, preferred_element_type=F32)


def remote(src, dst, send_sem, recv_sem, device):
    return pltpu.make_async_remote_copy(
        src_ref=src, dst_ref=dst, send_sem=send_sem, recv_sem=recv_sem, device_id=device, device_id_type=MESH
    )


def ball(values, width):
    ratio = lax.rsqrt(jnp.sum(values * values, axis=1, keepdims=True) / width + EPSILON)
    return values * ratio, ratio


def ball_back(source, ratio, grad_in, width):
    inner = jnp.sum(grad_in * source, axis=1, keepdims=True)
    return ratio * grad_in - source * (ratio * ratio * ratio) * (inner / width)


def buffers(nt, nz, rows, width, cols, hidden, shard, section, chunk):
    vmem, dma = pltpu.VMEM, pltpu.SemaphoreType.DMA
    pair = 2 * rows
    return dict(
        wq=vmem((2, 3, width, cols), BF16),
        wo=vmem((2, cols, width), BF16),
        wu=vmem((2, 2, width, hidden), BF16),
        wd=vmem((2, hidden, width), BF16),
        sqk=vmem((2, 1, cols), F32),
        suv=vmem((2, 2, hidden), F32),
        alp=vmem((2, 2, width), F32),
        raw=vmem((2 * hidden // 128 * width, 128), BF16),
        raw_f=vmem((2 * hidden // 128 * 64, 128), F32),
        full_in=vmem((2, rows, width), BF16),
        mid_full=vmem((2, nt, shard, width), BF16),
        dml_full=vmem((2, nt, shard, width), BF16),
        dat_full=vmem((2, rows, width), BF16),
        fi_p=vmem((rows, width), BF16),
        at_p=vmem((rows, cols), BF16),
        da_p=vmem((rows, width), BF16),
        dq_p=vmem((rows, 3 * cols), BF16),
        xa=vmem((nt, nz * 2 * shard, width), BF16),
        da=vmem((nt, nz * 2 * shard, width), BF16),
        kv=vmem((2, pair, 2 * cols), BF16),
        dkv_f=vmem((pair, 2 * cols), F32),
        dkv_s=vmem((2, rows, 2 * cols), BF16),
        dkv_r=vmem((2, rows, 2 * cols), BF16),
        rs_s=vmem((8, rows, width), BF16),
        rs_r=vmem((8, nt - 1, shard, width), BF16),
        rot=vmem((2, 2, rows, cols), F32),
        rat=vmem((2, 2, rows, cols), F32),
        qb=vmem((2, rows, cols), BF16),
        prob=vmem((2, cols // HEAD_DIM, rows, pair), F32),
        at=vmem((2, rows, cols), BF16),
        araw=vmem((2, shard, width), F32),
        mraw=vmem((2, shard, width), F32),
        mid=vmem((2, shard, width), F32),
        zone=vmem((2, shard, width), F32),
        ztwo=vmem((2, shard, width), F32),
        up=vmem((2, rows, hidden), F32),
        gate=vmem((2, rows, hidden), F32),
        act=vmem((rows, hidden), BF16),
        duv=vmem((2, rows, hidden), BF16),
        dqkv=vmem((2, rows, 3 * cols), BF16),
        cot_rows=vmem((shard, width), BF16),
        out_s=vmem((2, shard, width), BF16),
        ig_s=vmem((2, shard, width), BF16),
        cosb=vmem((rows, cols), F32),
        sinb=vmem((rows, cols), F32),
        bias=vmem((rows, pair), F32),
        blk=vmem((cols, cols), BF16),
        al_s=vmem((2, 8, width), F32),
        al_r=vmem((2, nt - 1, 8, cols), F32),
        small=vmem((2, 8, cols), F32),
        sm_r=vmem((nz, 2, 8, cols), F32),
        wq_s=vmem((nz - 1, section, 3 * cols), BF16),
        wq_r=vmem((nz, section, 3 * cols), BF16),
        wo_f=vmem((cols, width), F32),
        wo_s=vmem((cols, width), BF16),
        wo_r=vmem((nz - 1, chunk, width), BF16),
        act_b=vmem((nz * 2 * shard, hidden), BF16),
        suv_b=vmem((2, hidden), F32),
        acc=vmem((2, section, hidden), F32),
        w_l=dma((2, 4)), w_rs=dma((4,)),
        par_l=dma((2, 2)), par_s=dma((2,)),
        alp_r=dma((2, nt)), alp_s=dma((2, nt)),
        hid_r=dma((nt,)), hid_s=dma((2, nt)),
        cot_r=dma((nt,)), cot_s=dma((2, nt)),
        fi_rs=dma((2,)), at_rs=dma((2,)), dap_rs=dma((2,)), dq_rs=dma((2,)),
        kv_rs=dma((2, 2)), dkv_rs=dma((2, 2)),
        ag_ss=dma((7, nt - 1)), ag_rr=dma((7, nt - 1)),
        rs_ss=dma((8, 2, nt - 1)), rs_rr=dma((8, 2, nt - 1)),
        xa_r=dma((nz, 2)), xa_ss=dma((2, nz)),
        da_r=dma((nz, 2)), da_ss=dma((2, nz)),
        df_ss=dma((nz - 1, nt - 1)), df_rr=dma((nz - 1, nt - 1)),
        xf_ss=dma((nz - 1, nt - 1)), xf_rr=dma((nz - 1, nt - 1)),
        lo_ss=dma((2, nt)), lo_r=dma((2, nt)),
        ig_ss=dma((2, nt)), ig_r=dma((2, nt)),
        al_ss=dma((2, nt - 1)), al_rr=dma((2, nt - 1)),
        sm_ss=dma((2, nz)), sm_rr=dma((nz, 2)),
        wq_ss=dma((nz - 1,)), wq_rr=dma((nz,)),
        wo_ss=dma((nz - 1,)), wo_rr=dma((nz - 1,)),
    )


def fused_kernel(names, nt, nz, *refs):
    hid, cot, lens, wq_in, wo_in, wu_in, wd_in, sqk_in, suv_in, alp_in, rates = refs[:11]
    lo, ig, gq, go, gu, gd, gsqk, gsuv, gal = refs[11:20]
    b = types.SimpleNamespace(**dict(zip(names, refs[20:])))
    rows, width = b.full_in.shape[1:]
    cols, hidden = b.qb.shape[2], b.wd.shape[1]
    shard = b.mid.shape[1]
    heads = cols // HEAD_DIM
    pair = 2 * rows
    section_rows = width // nz
    chunk = cols // nz
    tile = 512
    s, t, z = lax.axis_index("section"), lax.axis_index("tensor"), lax.axis_index("dp")
    p = lax.rem(z, 2)
    base = z - p
    peer = (1 - s, t, z)
    pending = []

    def around(k):
        return lax.rem(lax.div(t, 2) + k // 2, 2) * 2 + lax.rem(lax.rem(t, 2) + k % 2, 2)

    peers = (3, 1, 2)

    def along(k):
        return lax.rem(z + k, nz)

    def later(copy, when=None):
        pending.append((copy, when))

    def lanes(index, size):
        return pl.ds(pl.multiple_of(index * size, size), size)

    weights = [(wq_in, b.wq), (wo_in, b.wo), (None, b.wu), (wd_in, b.wd)]
    raw_copy = pltpu.make_async_copy(wu_in, b.raw, b.w_l.at[s, 2])
    raw_copy.start()
    for i in (0, 1, 3):
        src, dst = weights[i]
        pltpu.make_async_copy(src, dst.at[s], b.w_l.at[s, i]).start()
    params = [(sqk_in, b.sqk), (suv_in, b.suv)]
    for i, (src, dst) in enumerate(params):
        pltpu.make_async_copy(src, dst.at[s], b.par_l.at[s, i]).start()

    barrier = pltpu.get_barrier_semaphore()
    greeted = 0
    for dz in range(2):
        for dt in range(nt):
            for dc in range(2):
                if dz or dt or dc:
                    device = (lax.rem(s + dc, 2), around(dt), base + lax.rem(p + dz, 2))
                    pl.semaphore_signal(barrier, inc=1, device_id=device, device_id_type=MESH)
                    greeted += 1
    for dz in range(2, nz):
        for dc in range(2):
            device = (lax.rem(s + dc, 2), t, lax.rem(base + dz, nz))
            pl.semaphore_signal(barrier, inc=1, device_id=device, device_id_type=MESH)
            greeted += 1
    token0 = (base // 2) * pair
    pos_q = token0 + s * rows + lax.broadcasted_iota(jnp.int32, (rows, 1), 0)
    pos_k = token0 + lax.broadcasted_iota(jnp.int32, (1, pair), 1)

    def sequences(pos):
        seg = jnp.zeros_like(pos)
        first = jnp.zeros_like(pos)
        end = jnp.int32(0)
        for i in range(lens.shape[1]):
            end = end + lens[p, i]
            past = pos >= end
            seg = seg + past.astype(jnp.int32)
            first = jnp.where(past, end, first)
        return seg, pos - first

    seg_q, place_q = sequences(pos_q)
    seg_k, _ = sequences(pos_k)
    allowed = (seg_q == seg_k) & (pos_k <= pos_q)
    b.bias[...] = jnp.where(allowed, 0.0, NEG_LARGE)
    angle = place_q.astype(F32) * rates[...]
    b.cosb[...] = jnp.cos(angle)
    b.sinb[...] = jnp.sin(angle)
    col = lax.broadcasted_iota(jnp.int32, (1, cols), 1)
    lower = (col & (HEAD_DIM // 2)) == 0
    head_of = lax.shift_right_logical(col, 6)
    head_row = lax.shift_right_logical(lax.broadcasted_iota(jnp.int32, (cols, 1), 0), 6)
    b.blk[...] = jnp.where(head_row == head_of, 1.0, 0.0).astype(BF16)
    picks = [jnp.where(head_of == h, 1.0, 0.0) for h in range(heads)]
    b.al_s[...] = jnp.zeros_like(b.al_s)
    b.small[...] = jnp.zeros_like(b.small)

    @pl.when(s == 0)
    def _():
        b.kv[:, rows:pair, :] = jnp.zeros((2, rows, 2 * cols), BF16)

    @pl.when(s == 1)
    def _():
        b.dkv_r[...] = jnp.zeros_like(b.dkv_r)


    def to_order():
        raw_copy.wait()
        lines = 2 * hidden // 128

        def in_order(step, carry):
            b.raw_f[...] = b.raw[pl.ds(pl.multiple_of(step * lines * 64, lines * 64), lines * 64), :].astype(F32)
            at = pl.ds(pl.multiple_of(step * 64, 64), 64)
            for n in range(hidden // 128):
                for i in range(2):
                    b.wu[s, i, at, n * 128 : (n + 1) * 128] = b.raw_f[pl.ds(2 * n + i, 64, stride=lines), :].astype(BF16)
            return carry

        lax.fori_loop(0, width // 64, in_order, 0)

    pl.semaphore_wait(barrier, greeted)

    is_source = s == p
    for src, rs, ss in ((hid, b.hid_r, b.hid_s), (cot, b.cot_r, b.cot_s)):
        for dz in range(2):
            to_mb = lax.rem(p + dz, 2)
            for dt in peers + (0,):
                to_t = around(dt)
                if src is hid:
                    piece, place = src.at[to_mb], b.full_in.at[0, :, lanes(t, cols)]
                else:
                    piece = src.at[to_mb, pl.ds(pl.multiple_of(to_t * shard, shard), shard), :]
                    place = b.cot_rows.at[:, lanes(t, cols)]
                if dz == 0 and dt == 0:

                    @pl.when(is_source)
                    def _(piece=piece, place=place, rs=rs):
                        pltpu.make_async_copy(piece, place, rs.at[0]).start()
                else:
                    copy = remote(piece, place, ss.at[dz, dt], rs.at[dt], (s, to_t, base + to_mb))
                    pl.when(is_source)(copy.start)
                    later(copy, is_source)
        if src is hid:
            for i, (src_p, dst_p) in enumerate(params):
                copy = remote(src_p, dst_p.at[s], b.par_s.at[i], b.par_l.at[s, i], peer)
                copy.start()
                later(copy)
            alp_src, alp_dst = alp_in, b.alp.at[s, :, lanes(t, cols)]
            for dc in range(2):
                for dt in range(nt):
                    if dc == 0 and dt == 0:
                        pltpu.make_async_copy(alp_src, alp_dst, b.alp_r.at[s, 0]).start()
                    else:
                        copy = remote(alp_src, alp_dst, b.alp_s.at[dc, dt], b.alp_r.at[s, dt], (lax.rem(s + dc, 2), around(dt), z))
                        copy.start()
                        later(copy)
            for i in (0, 1, 3):
                src_w, dst_w = weights[i]
                copy = remote(src_w, dst_w.at[s], b.w_rs.at[i], b.w_l.at[s, i], peer)
                copy.start()
                later(copy)

    def wait_weight(layer, i):
        dst_w = weights[i][1].at[layer]
        wait = pltpu.make_async_copy(dst_w, dst_w, b.w_l.at[layer, i]).wait
        if i == 2:
            pl.when(s != layer)(wait)
        else:
            wait()

    to_order()
    copy = remote(b.wu.at[s], b.wu.at[s], b.w_rs.at[2], b.w_l.at[s, 2], peer)
    copy.start()
    later(copy)

    def partner_cols(x):
        half = HEAD_DIM // 2
        return jnp.where(lower, -pltpu.roll(x, cols - half, 1), pltpu.roll(x, half, 1))

    def head_total(x):
        high = x.astype(BF16)
        low = (x - high.astype(F32)).astype(BF16)
        return mul(high, b.blk[...]) + mul(low, b.blk[...])

    def shard_of(ref, index):
        return ref.at[index] if len(ref.shape) == 3 else ref.at[pl.ds(pl.multiple_of(index * shard, shard), shard), :]

    def gather(stage, ref):
        mine = shard_of(ref, t)
        for k in peers:
            copy = remote(mine, mine, b.ag_ss.at[stage, k - 1], b.ag_rr.at[stage, k - 1], (s, around(k), z))
            copy.start()
            later(copy)

    def gather_wait(stage, ref):
        for k in range(1, nt):
            theirs = shard_of(ref, around(k))
            remote(theirs, theirs, b.ag_ss.at[stage, k - 1], b.ag_rr.at[stage, k - 1], (s, around(k), z)).wait_recv()

    def scatter(stage, n):
        cut = pl.ds(n * tile, tile)
        for k in peers:
            piece = b.rs_s.at[stage, pl.ds(pl.multiple_of(around(k) * shard, shard), shard), cut]
            copy = remote(piece, b.rs_r.at[stage, k - 1, :, cut], b.rs_ss.at[stage, n, k - 1], b.rs_rr.at[stage, n, k - 1], (s, around(k), z))
            copy.start()
            later(copy)

    def scatter_wait(stage):
        total = b.rs_s[stage, pl.ds(pl.multiple_of(t * shard, shard), shard), :].astype(F32)
        for n in range(width // tile):
            for k in range(1, nt):
                place = b.rs_r.at[stage, k - 1, :, pl.ds(n * tile, tile)]
                remote(place, place, b.rs_ss.at[stage, n, k - 1], b.rs_rr.at[stage, n, k - 1], (s, around(k), z)).wait_recv()
        for k in range(1, nt):
            total = total + b.rs_r[stage, k - 1].astype(F32)
        return total

    slot = pl.ds(pl.multiple_of((z * 2 + s) * shard, shard), shard)

    def my_rows(ref):
        return shard_of(ref, t)

    def to_owner(layer, ref, place_of, send_sems, recv_sems, hops=range(nz)):
        for k in hops:
            copy = remote(ref, place_of, send_sems.at[layer, k], recv_sems.at[k, s], (layer, t, along(k)))
            if k == 0:

                @pl.when(s == layer)
                def _():
                    pltpu.make_async_copy(ref, place_of, recv_sems.at[0, s]).start()

                pl.when(s != layer)(copy.start)
                later(copy, s != layer)
            else:
                copy.start()
                later(copy)

    x_rows = (b.xa, b.xa_r, b.xf_ss, b.xf_rr)
    d_rows = (b.da, b.da_r, b.df_ss, b.df_rr)

    def bundle(layer, hops, group):
        ref, arrived, send_sems, recv_sems = group
        for k in hops:
            from_z = along(nz - k)
            rows_of = pl.ds(pl.multiple_of(from_z * 2 * shard, 2 * shard), 2 * shard)

            @pl.when(s == layer)
            def _(k=k, from_z=from_z):
                for core in range(2):
                    row = pl.multiple_of((from_z * 2 + core) * shard, shard)
                    place = ref.at[t, pl.ds(row, shard), :]
                    pltpu.make_async_copy(place, place, arrived.at[k, core]).wait()

            for to in range(1, nt):
                place = ref.at[t, rows_of, :]
                copy = remote(place, place, send_sems.at[k - 1, to - 1], recv_sems.at[k - 1, to - 1], (s, around(to), z))
                pl.when(s == layer)(copy.start)
                later(copy, s == layer)

    def to_output(layer, ref, out, send_sems, recv_sems):
        to_z = base + s
        place = out.at[p, pl.ds(pl.multiple_of(t * shard, shard), shard), :]
        for k in range(nt):
            to_t = around(k)
            piece = ref.at[:, lanes(to_t, cols)]
            copy = remote(piece, place, send_sems.at[layer, k], recv_sems.at[p, k], (layer, to_t, to_z))
            if k == 0:
                here = (s == layer) & (to_z == z)

                @pl.when(here)
                def _(piece=piece):
                    pltpu.make_async_copy(piece, place, recv_sems.at[p, 0]).start()

                away = jnp.logical_not(here)
                pl.when(away)(copy.start)
                later(copy, away)
            else:
                copy.start()
                later(copy)

    upper = z // 2
    end, hub = 3 * upper, 1 + upper
    sibling = end + hub - z
    far_end, far_hub = 3 - end, 3 - hub

    def hub_step(layer, n):
        @pl.when((s == layer) & (z == hub))
        def _():
            remote(b.wq_s.at[n], b.wq_r.at[n], b.wq_ss.at[n], b.wq_rr.at[n], peer).wait_recv()
            b.wq_s[n] = (b.wq_s[n].astype(F32) + b.wq_r[n].astype(F32)).astype(BF16)
            to_z = far_hub if n else far_end
            remote(b.wq_s.at[n], b.wq_r.at[3], b.wq_ss.at[n], b.wq_rr.at[3], (layer, t, to_z)).start()

    for layer in range(2):
        full_in = b.full_in.at[layer]
        if layer == 0:
            for dt in range(nt):
                place = b.full_in.at[0, :, lanes(around(dt), cols)]
                pltpu.make_async_copy(hid.at[0], place, b.hid_r.at[dt]).wait()
            for src_core in range(2):
                for i, (src_p, dst_p) in enumerate(params):
                    pltpu.make_async_copy(src_p, dst_p.at[src_core], b.par_l.at[src_core, i]).wait()
                for dt in range(nt):
                    place = b.alp.at[src_core, :, lanes(around(dt), cols)]
                    pltpu.make_async_copy(alp_in, place, b.alp_r.at[src_core, dt]).wait()
        else:
            gather_wait(6, full_in)
        copy = remote(full_in, b.fi_p, b.fi_rs.at[0], b.fi_rs.at[1], peer)
        pl.when(s != layer)(copy.start)
        later(copy, s != layer)
        scale_qk = b.sqk[layer]
        wait_weight(layer, 0)
        x = full_in[...]
        own = pl.ds(pl.multiple_of(s * rows, rows), rows)
        for i in range(2):
            raw = mul(x, b.wq[layer, i])
            rotated = raw * b.cosb[...] + partner_cols(raw) * b.sinb[...]
            ratio = lax.rsqrt(head_total(rotated * rotated) / HEAD_DIM + EPSILON)
            b.rot[layer, i] = rotated
            b.rat[layer, i] = ratio
            normed = (rotated * ratio * scale_qk).astype(BF16)
            if i == 0:
                b.qb[layer] = normed
            else:
                b.kv[layer, own, 0:cols] = normed
        b.kv[layer, own, cols : 2 * cols] = mul(x, b.wq[layer, 2]).astype(BF16)
        mine = b.kv.at[layer, own, :]
        copy = remote(mine, mine, b.kv_rs.at[layer, 0], b.kv_rs.at[layer, 1], peer)
        pl.when(s == 0)(copy.start)
        later(copy, s == 0)
        pl.when(s == 1)(copy.wait_recv)
        att = jnp.zeros((rows, cols), F32)
        for h in range(heads):
            q_h = (b.qb[layer].astype(F32) * picks[h]).astype(BF16)
            scores = contract_cols(q_h, b.kv[layer, :, 0:cols]) * (1.0 / math.sqrt(HEAD_DIM)) + b.bias[...]
            top = jnp.max(scores, axis=1, keepdims=True)
            terms = jnp.exp(scores - top)
            prob = terms / jnp.sum(terms, axis=1, keepdims=True)
            b.prob[layer, h] = prob
            att = att + picks[h] * mul(prob.astype(BF16), b.kv[layer, :, cols : 2 * cols])
        b.at[layer] = att.astype(BF16)
        wait_weight(layer, 1)
        for n in range(0, width, tile):
            b.rs_s[layer, :, n : n + tile] = mul(b.at[layer], b.wo[layer, :, n : n + tile]).astype(BF16)
            scatter(layer, n // tile)
        hin = my_rows(full_in)[...].astype(F32)
        rate_a = b.alp[layer, 0:1, :]
        rate_m = b.alp[layer, 1:2, :]
        araw = scatter_wait(layer)
        b.araw[layer] = araw
        zone = hin + rate_a * (ball(araw, width)[0] - hin)
        b.zone[layer] = zone
        mid = ball(zone, width)[0]
        b.mid[layer] = mid
        mid_full = b.mid_full.at[layer]
        my_rows(mid_full)[...] = mid.astype(BF16)
        gather(layer, mid_full)
        if layer == 1:
            to_owner(1, my_rows(mid_full), b.xa.at[t, slot, :], b.xa_ss, b.xa_r, range(1, nz))
        wait_weight(layer, 2)
        wait_weight(layer, 3)
        gather_wait(layer, mid_full)
        to_owner(layer, mid_full, b.xa.at[:, slot, :], b.xa_ss, b.xa_r, range(nz) if layer == 0 else (0,))
        x = mid_full[...].reshape(rows, width)
        for n in range(0, hidden, tile):
            cut = slice(n, n + tile)
            up = mul(x, b.wu[layer, 0, :, cut])
            gate = mul(x, b.wu[layer, 1, :, cut])
            b.up[layer, :, cut] = up
            b.gate[layer, :, cut] = gate
            gate_s = gate * b.suv[layer, 1:2, cut]
            b.act[:, cut] = (up * b.suv[layer, 0:1, cut] * (gate_s / (1.0 + jnp.exp(-gate_s)))).astype(BF16)
        for n in range(0, width, tile):
            b.rs_s[2 + layer, :, n : n + tile] = mul(b.act[...], b.wd[layer, :, n : n + tile]).astype(BF16)
            scatter(2 + layer, n // tile)
        if layer == 1:
            bundle(1, (1,), x_rows)
        mraw = scatter_wait(2 + layer)
        b.mraw[layer] = mraw
        ztwo = mid + rate_m * (ball(mraw, width)[0] - mid)
        b.ztwo[layer] = ztwo
        b.out_s[layer] = ball(ztwo, width)[0].astype(BF16)
        if layer == 0:
            my_rows(b.full_in.at[1])[...] = b.out_s[0]
            gather(6, b.full_in.at[1])
        to_output(layer, b.out_s.at[layer], lo, b.lo_ss, b.lo_r)

    mine_cols = lanes(z, section_rows)

    def block(k, suv_now):
        at = lax.rem(lax.div(t, 2) + lax.div(k, 2), 2) * 2 + lax.rem(t + k, 2)
        first = suv_now is None
        if first:
            for hop in range(nz):
                for core in range(2):
                    rows_of = pl.ds(pl.multiple_of((along(nz - hop) * 2 + core) * shard, shard), shard)
                    for ref, sems in ((b.xa, b.xa_r), (b.da, b.da_r)):
                        place = ref.at[:, rows_of, :]
                        wait = pltpu.make_async_copy(place, place, sems.at[hop, core]).wait
                        if hop == 0:
                            wait()
                        elif ref is b.xa:
                            pl.when(s == 0)(wait)
        else:
            for hop in range(1, nz):
                for ref, _, ss, rr in (d_rows, x_rows):
                    place = ref.at[at, pl.ds(pl.multiple_of(along(nz - hop) * 2 * shard, 2 * shard), 2 * shard), :]
                    wait = remote(place, place, ss.at[hop - 1, k - 1], rr.at[hop - 1, k - 1], peer).wait_recv
                    if ref is b.da:
                        wait()
                    else:
                        pl.when(s == 1)(wait)

        def add(ref, value):
            ref[...] = value if first else ref[...] + value

        new = []
        for n in range(0, hidden, tile):
            cut = slice(n, n + tile)
            up = mul(b.xa[at], b.wu[s, 0, :, cut])
            gate = mul(b.xa[at], b.wu[s, 1, :, cut])
            d_act = contract_cols(b.da[at], b.wd[s, cut, :])
            scale_up, scale_gate = b.suv[s, 0:1, cut], b.suv[s, 1:2, cut]
            up_s = up * scale_up
            gate_s = gate * scale_gate
            sig = 1.0 / (1.0 + jnp.exp(-gate_s))
            b.act_b[:, cut] = (up_s * gate_s * sig).astype(BF16)
            d_up = d_act * gate_s * sig
            d_gate = d_act * up_s * sig * (1.0 + gate_s * (1.0 - sig))
            new.append((jnp.sum(d_up * up, axis=0, keepdims=True), jnp.sum(d_gate * gate, axis=0, keepdims=True)))
            x_cut = b.xa[at, :, mine_cols]
            add(b.acc.at[0, :, cut], contract_rows(x_cut, (d_up * scale_up).astype(BF16)))
            add(b.acc.at[1, :, cut], contract_rows(x_cut, (d_gate * scale_gate).astype(BF16)))
        for n in range(0, width, tile):
            cut = slice(n, n + tile)
            add(gd.at[:, cut], contract_rows(b.act_b[:, lanes(z, hidden // nz)], b.da[at, :, cut]))
        sums = tuple(jnp.concatenate([pair_of[i] for pair_of in new], axis=1) for i in range(2))
        return sums if first else tuple(now + more for now, more in zip(suv_now, sums))

    for dt in range(nt):
        place = b.cot_rows.at[:, lanes(around(dt), cols)]
        pltpu.make_async_copy(cot.at[0, pl.ds(0, shard), :], place, b.cot_r.at[dt]).wait()
    grad_out = b.cot_rows[...].astype(F32)
    for layer in (1, 0):
        own = pl.ds(pl.multiple_of(s * rows, rows), rows)
        other = pl.ds(pl.multiple_of((1 - s) * rows, rows), rows)
        rate_a = b.alp[layer, 0:1, :]
        rate_m = b.alp[layer, 1:2, :]
        scale_qk = b.sqk[layer]
        mid = b.mid[layer]
        mraw_n, ratio_m = ball(b.mraw[layer], width)
        ratio_two = ball(b.ztwo[layer], width)[1]
        d_two = ball_back(b.ztwo[layer], ratio_two, grad_out, width)
        d_mid = (1.0 - rate_m) * d_two
        b.al_s[layer, 1:2, :] = jnp.sum(d_two * (mraw_n - mid), axis=0, keepdims=True)
        dml_full = b.dml_full.at[layer]
        my_rows(dml_full)[...] = ball_back(b.mraw[layer], ratio_m, rate_m * d_two, width).astype(BF16)
        gather(2 + layer, dml_full)
        to_owner(layer, my_rows(dml_full), b.da.at[t, slot, :], b.da_ss, b.da_r, range(1, nz))
        if layer == 1:
            bundle(1, (2, 3), x_rows)
        gather_wait(2 + layer, dml_full)
        to_owner(layer, dml_full, b.da.at[:, slot, :], b.da_ss, b.da_r, (0,))
        if layer == 0:
            bundle(1, (3,), d_rows)
        x = dml_full[...].reshape(rows, width)
        for n in range(0, hidden, tile):
            cut = slice(n, n + tile)
            d_act = contract_cols(x, b.wd[layer, cut, :])
            scale_up, scale_gate = b.suv[layer, 0:1, cut], b.suv[layer, 1:2, cut]
            up_s = b.up[layer, :, cut] * scale_up
            gate_s = b.gate[layer, :, cut] * scale_gate
            sig = 1.0 / (1.0 + jnp.exp(-gate_s))
            b.duv[0, :, cut] = (d_act * gate_s * sig * scale_up).astype(BF16)
            b.duv[1, :, cut] = (d_act * up_s * sig * (1.0 + gate_s * (1.0 - sig)) * scale_gate).astype(BF16)
        for n in range(0, width, tile):
            cut = slice(n, n + tile)
            part = contract_cols(b.duv[0], b.wu[layer, 0, cut, :]) + contract_cols(b.duv[1], b.wu[layer, 1, cut, :])
            b.rs_s[4 + layer, :, cut] = part.astype(BF16)
            scatter(4 + layer, n // tile)
        hin = my_rows(b.full_in.at[layer])[...].astype(F32)
        araw_n, ratio_a = ball(b.araw[layer], width)
        ratio_one = ball(b.zone[layer], width)[1]
        d_mid = d_mid + scatter_wait(4 + layer)
        d_one = ball_back(b.zone[layer], ratio_one, d_mid, width)
        b.al_s[layer, 0:1, :] = jnp.sum(d_one * (araw_n - hin), axis=0, keepdims=True)
        dat_full = b.dat_full.at[layer]
        my_rows(dat_full)[...] = ball_back(b.araw[layer], ratio_a, rate_a * d_one, width).astype(BF16)
        gather(4 + layer, dat_full)
        for k in range(1, nt):
            copy = remote(b.al_s.at[layer, :, lanes(around(k), cols)], b.al_r.at[layer, k - 1], b.al_ss.at[layer, k - 1], b.al_rr.at[layer, k - 1], (s, around(k), z))
            copy.start()
            later(copy)
        if layer == 0:
            hub_step(1, 0)
            hub_step(1, 1)
        gather_wait(4 + layer, dat_full)
        for src_v, dst_v, sems in ((dat_full, b.da_p, b.dap_rs), (b.at.at[layer], b.at_p, b.at_rs)):
            copy = remote(src_v, dst_v, sems.at[0], sems.at[1], peer)
            pl.when(s != layer)(copy.start)
            later(copy, s != layer)
        d_att = contract_cols(dat_full[...], b.wo[layer])
        dq = jnp.zeros((rows, cols), F32)
        dk = jnp.zeros((pair, cols), F32)
        dv = jnp.zeros((pair, cols), F32)
        for h in range(heads):
            d_att_h = (d_att * picks[h]).astype(BF16)
            q_h = (b.qb[layer].astype(F32) * picks[h]).astype(BF16)
            prob = b.prob[layer, h]
            d_prob = contract_cols(d_att_h, b.kv[layer, :, cols : 2 * cols])
            d_score = (prob * (d_prob - jnp.sum(prob * d_prob, axis=1, keepdims=True))).astype(BF16)
            dv = dv + contract_rows(prob.astype(BF16), d_att_h)
            dq = dq + picks[h] * mul(d_score, b.kv[layer, :, 0:cols])
            dk = dk + contract_rows(d_score, q_h)
        bundle(layer, (1, 2), d_rows)
        b.dkv_f[:, 0:cols] = dk * (1.0 / math.sqrt(HEAD_DIM))
        b.dkv_f[:, cols : 2 * cols] = dv
        b.dkv_s[layer] = b.dkv_f[other, :].astype(BF16)
        copy = remote(b.dkv_s.at[layer], b.dkv_r.at[layer], b.dkv_rs.at[layer, 0], b.dkv_rs.at[layer, 1], peer)
        pl.when(s == 1)(copy.start)
        later(copy, s == 1)

        @pl.when(s == layer)
        def _(layer=layer):
            for dst_v, sems in ((b.da_p, b.dap_rs), (b.at_p, b.at_rs)):
                remote(dst_v, dst_v, sems.at[0], sems.at[1], peer).wait_recv()
            for n in range(0, width, tile):
                cut = slice(n, n + tile)
                part = contract_rows(b.at[layer], b.dat_full[layer, :, cut]) + contract_rows(b.at_p[...], b.da_p[:, cut])
                b.wo_f[:, cut] = part
                b.wo_s[:, cut] = part.astype(BF16)
            for k in range(1, nz):
                piece = b.wo_s.at[pl.ds(pl.multiple_of(along(k) * chunk, chunk), chunk), :]
                remote(piece, b.wo_r.at[k - 1], b.wo_ss.at[k - 1], b.wo_rr.at[k - 1], (layer, t, along(k))).start()

        d_scale = jnp.zeros((1, cols), F32)
        for i in range(2):
            if i == 0:
                grad_n = dq * (1.0 / math.sqrt(HEAD_DIM))
            else:
                pl.when(s == 0)(copy.wait_recv)
                grad_n = b.dkv_f[own, 0:cols] + b.dkv_r[layer, :, 0:cols].astype(F32)
            rotated, ratio = b.rot[layer, i], b.rat[layer, i]
            d_scale = d_scale + jnp.sum(grad_n * rotated * ratio, axis=0, keepdims=True)
            d_unit = grad_n * scale_qk
            d_rot = ratio * d_unit - rotated * (ratio * ratio * ratio) * (head_total(d_unit * rotated) / HEAD_DIM)
            d_raw = d_rot * b.cosb[...] - partner_cols(d_rot * b.sinb[...])
            b.dqkv[layer, :, i * cols : (i + 1) * cols] = d_raw.astype(BF16)
        d_val = b.dkv_f[own, cols : 2 * cols] + b.dkv_r[layer, :, cols : 2 * cols].astype(F32)
        b.dqkv[layer, :, 2 * cols : 3 * cols] = d_val.astype(BF16)
        copy = remote(b.dqkv.at[layer], b.dq_p, b.dq_rs.at[0], b.dq_rs.at[1], peer)
        pl.when(s != layer)(copy.start)
        later(copy, s != layer)
        for n in range(0, width, tile):
            part = contract_cols(b.dqkv[layer, :, 0:cols], b.wq[layer, 0, n : n + tile, :])
            for i in range(1, 3):
                part = part + contract_cols(b.dqkv[layer, :, i * cols : (i + 1) * cols], b.wq[layer, i, n : n + tile, :])
            b.rs_s[6 + layer, :, n : n + tile] = part.astype(BF16)
            scatter(6 + layer, n // tile)
        total = b.al_s[layer, :, lanes(t, cols)]
        for k in range(1, nt):
            place = b.al_r.at[layer, k - 1]
            remote(place, place, b.al_ss.at[layer, k - 1], b.al_rr.at[layer, k - 1], peer).wait_recv()
            total = total + place[...]
        b.small[layer] = total
        b.small[layer, 2:3, :] = d_scale
        to_owner(layer, b.small.at[layer], b.sm_r.at[lax.rem(z, nz), s], b.sm_ss, b.sm_rr)

        @pl.when(s == layer)
        def _(layer=layer):
            for dst_v, sems in ((b.fi_p, b.fi_rs), (b.dq_p, b.dq_rs)):
                remote(dst_v, dst_v, sems.at[0], sems.at[1], peer).wait_recv()
            for n, index in enumerate((far_end, far_hub, sibling, z)):
                cut = lanes(index, section_rows)
                part = contract_rows(b.full_in[layer, :, cut], b.dqkv[layer]) + contract_rows(b.fi_p[:, cut], b.dq_p[...])
                if n == 3:
                    for i in range(3):
                        gq[i] = part[:, i * cols : (i + 1) * cols]
                    continue
                b.wq_s[n] = part.astype(BF16)
                start = remote(b.wq_s.at[n], b.wq_r.at[n], b.wq_ss.at[n], b.wq_rr.at[n], (layer, t, sibling)).start
                if n == 2:
                    start()
                else:
                    pl.when(z == end)(start)

        if layer == 0:
            bundle(0, (3,), d_rows)
            suv = block(0, None)
            hub_step(0, 0)
        d_hin = (1.0 - rate_a) * d_one + scatter_wait(6 + layer)
        b.ig_s[layer] = d_hin.astype(BF16)
        to_output(layer, b.ig_s.at[layer], ig, b.ig_ss, b.ig_r)
        grad_out = b.ig_s[layer].astype(F32)

    suv = block(1, suv)
    hub_step(0, 1)
    suv = lax.fori_loop(2, nt, block, suv)
    for i in range(2):
        b.suv_b[i : i + 1, :] = suv[i]
    gsuv[...] = b.suv_b[:, lanes(z, hidden // nz)]
    per_row = 2 * hidden // 128
    for j in range(hidden // 128):
        for i in range(2):
            gu[pl.ds(2 * j + i, section_rows, stride=per_row), :] = b.acc[i, :, j * 128 : (j + 1) * 128]

    for n in (2, 3):
        place = b.wq_r.at[n]
        remote(place, place, b.wq_ss.at[2], b.wq_rr.at[n], peer).wait_recv()
        for i in range(3):
            gq[i] += b.wq_r[n, :, i * cols : (i + 1) * cols].astype(F32)
    total = b.wo_f[pl.ds(pl.multiple_of(z * chunk, chunk), chunk), :]
    for k in range(1, nz):
        place = b.wo_r.at[k - 1]
        remote(place, place, b.wo_ss.at[k - 1], b.wo_rr.at[k - 1], peer).wait_recv()
        total = total + place[...].astype(F32)
    go[...] = total
    total = jnp.zeros((8, cols), F32)
    for k in range(nz):
        for core in range(2):
            place = b.sm_r.at[lax.rem(z + nz - k, nz), core]
            pltpu.make_async_copy(place, place, b.sm_rr.at[k, core]).wait()
            total = total + place[...]
    turned = pltpu.roll(total, lax.rem(cols - z * chunk, cols), 1)
    gal[...] = turned[0:2, 0:chunk]
    gsqk[...] = turned[2:3, 0:chunk]
    for out, sems in ((lo, b.lo_r), (ig, b.ig_r)):
        for m in range(2):
            for k in range(nt):
                place = out.at[m, pl.ds(pl.multiple_of(around(k) * shard, shard), shard), :]
                pltpu.make_async_copy(place, place, sems.at[m, k]).wait()
    for k in range(nz - 1):
        remote(b.wq_s.at[k], b.wq_r.at[k], b.wq_ss.at[k], b.wq_rr.at[k], peer).wait_send()
        piece = b.wo_s.at[pl.ds(0, chunk), :]
        remote(piece, b.wo_r.at[k], b.wo_ss.at[k], b.wo_rr.at[k], peer).wait_send()
    for copy, when in pending:
        if when is None:
            copy.wait_send()
        else:
            pl.when(when)(copy.wait_send)


def copy_kernel(*refs):
    count = len(refs) // 3
    sems = refs[-1]
    reads = [pltpu.make_async_copy(refs[i], refs[2 * count + i], sems.at[0, i]) for i in range(count)]
    writes = [pltpu.make_async_copy(refs[2 * count + i], refs[count + i], sems.at[1, i]) for i in range(count)]
    for copy in reads:
        copy.start()
    for read, write in zip(reads, writes):
        read.wait()
        write.start()
    for copy in writes:
        copy.wait()


def per_device_fused(hidden_in, cotangent, lengths, w_qkv, w_out, w_ug, w_down, s_qk, s_uv, alpha):
    nt, nz = lax.axis_size("tensor"), lax.axis_size("dp")
    rows, cols = hidden_in.shape[1:]
    width, hidden = w_out.shape[2], w_down.shape[1]
    shard, section, chunk = rows // nt, width // nz, cols // nz
    half = HEAD_DIM // 2
    rates = (10000.0 ** (-(np.arange(cols) % half).astype(np.float32) / half)).astype(np.float32)[None, :]
    pairs = w_ug[0].reshape(width, 2, hidden // 128, 128).transpose(0, 2, 1, 3).reshape(2 * hidden // 128 * width, 128)
    scratch = buffers(nt, nz, rows, width, cols, hidden, shard, section, chunk)
    anywhere = pl.BlockSpec(memory_space=pl.ANY)
    vmem = pl.BlockSpec(memory_space=pltpu.VMEM)
    smem = pl.BlockSpec(memory_space=pltpu.SMEM)
    outs = pl.pallas_call(
        functools.partial(fused_kernel, tuple(scratch), nt, nz),
        out_shape=(
            jax.ShapeDtypeStruct((MICRO, rows, cols), BF16),
            jax.ShapeDtypeStruct((MICRO, rows, cols), BF16),
            jax.ShapeDtypeStruct((3, section, cols), F32),
            jax.ShapeDtypeStruct((chunk, width), F32),
            jax.ShapeDtypeStruct((section * 2 * hidden // 128, 128), F32),
            jax.ShapeDtypeStruct((hidden // nz, width), F32),
            jax.ShapeDtypeStruct((1, chunk), F32),
            jax.ShapeDtypeStruct((2, hidden // nz), F32),
            jax.ShapeDtypeStruct((2, chunk), F32),
        ),
        in_specs=[anywhere, anywhere, smem] + [anywhere] * 7 + [vmem],
        out_specs=(anywhere, anywhere) + (vmem,) * 7,
        scratch_shapes=list(scratch.values()),
        compiler_params=pltpu.CompilerParams(
            collective_id=0, has_side_effects=True, vmem_limit_bytes=60 * 2**20
        ),
    )(
        hidden_in,
        cotangent,
        lengths,
        jnp.transpose(w_qkv[0], (1, 0, 2)),
        w_out[0],
        pairs,
        w_down[0],
        s_qk,
        s_uv[0],
        alpha[0],
        jnp.asarray(rates),
    )
    lo, ig, gq, go, gu, gd, gsqk, gsuv, gal = pl.pallas_call(
        copy_kernel,
        out_shape=tuple(jax.ShapeDtypeStruct(o.shape, o.dtype) for o in outs),
        in_specs=[anywhere] * len(outs),
        out_specs=(anywhere,) * len(outs),
        scratch_shapes=[pltpu.VMEM(o.shape, o.dtype) for o in outs] + [pltpu.SemaphoreType.DMA((2, len(outs)))],
        compiler_params=pltpu.CompilerParams(vmem_limit_bytes=60 * 2**20),
    )(*outs)
    gu = gu.reshape(section, hidden // 128, 2, 128).transpose(0, 2, 1, 3).reshape(section, 2, hidden)
    return (
        lo[None],
        ig[None],
        jnp.transpose(gq, (1, 0, 2))[None],
        go[None],
        gu[None],
        gd[None],
        gsqk,
        gsuv[None],
        gal[None],
    )


def solution(mesh):
    placed = (
        P(None, "dp", "tensor"),
        P(None, "dp", "tensor"),
        P(),
        P("section", None, None, "tensor"),
        P("section", "tensor", None),
        P("section", None, None, "tensor"),
        P("section", "tensor", None),
        P("section", "tensor"),
        P("section", None, "tensor"),
        P("section", None, "tensor"),
    )
    per_rank = per_device_fused if mesh.shape["dp"] == 2 * MICRO and mesh.shape["tensor"] == 4 else per_device
    return jax.shard_map(
        per_rank,
        mesh=mesh,
        in_specs=placed,
        out_specs=(
            P("section", None, "dp", "tensor"),
            P("section", None, "dp", "tensor"),
            P("section", "dp", None, "tensor"),
            P("section", ("tensor", "dp"), None),
            P("section", "dp", None, "tensor"),
            P("section", ("tensor", "dp"), None),
            P("section", ("tensor", "dp")),
            P("section", None, ("tensor", "dp")),
            P("section", None, ("tensor", "dp")),
        ),
        check_vma=False,
    )
```

```python
import functools
import math
import types

import jax
import jax.numpy as jnp
import numpy as np
from jax import lax
from jax.experimental import pallas as pl
from jax.experimental.pallas import tpu as pltpu
from jax.sharding import PartitionSpec as P

D = 1024
HEAD_DIM = 64
SEQ_CAP = 4096


EPSILON = 1e-05
HIGHEST = lax.Precision.HIGHEST
NEG_LARGE = -1e30


def passed_along(array, axis, by):
    count = lax.axis_size(axis)
    return lax.ppermute(array, axis, [(i, (i + by) % count) for i in range(count)])


def from_behind(array, axis, by):
    count = lax.axis_size(axis)
    pairs = [(i, i + by) for i in range(count) if 0 <= i + by < count]
    return lax.ppermute(array, axis, pairs)


def seq_table(lengths_row, positions):
    count = lengths_row.shape[0]
    order = jnp.arange(count, dtype=jnp.int32)
    seq_end = jnp.sum(jnp.where(order[None, :] <= order[:, None], lengths_row[None, :], 0), axis=1)
    seq_start = seq_end - lengths_row
    segment = jnp.sum((positions[:, None] >= seq_end[None, :]).astype(jnp.int32), axis=1)
    labels = jnp.arange(lengths_row.shape[0], dtype=jnp.int32)
    first_tok = jnp.sum(
        jnp.where(segment[:, None] == labels[None, :], seq_start[None, :], 0), axis=1
    )
    return (segment, positions - first_tok)


def rope_tables(places, col_width):
    column = jnp.arange(col_width, dtype=jnp.int32) % HEAD_DIM
    half_dim = HEAD_DIM // 2
    rope_rates = 10000.0 ** (-(column % half_dim).astype(jnp.float32) / half_dim)
    angles = places.astype(jnp.float32)[:, None] * rope_rates[None, :]
    return (jnp.cos(angles), jnp.sin(angles), column < half_dim)


def partner(values, lower_half):
    half_dim = HEAD_DIM // 2
    return jnp.where(
        lower_half[None, :],
        -jnp.roll(values, -half_dim, axis=1),
        jnp.roll(values, half_dim, axis=1),
    )


def contract_rows(left_op, right_op):
    return lax.dot_general(
        left_op, right_op, (((0,), (0,)), ((), ())), preferred_element_type=jnp.float32
    )


def contract_cols(left_op, right_op):
    return lax.dot_general(
        left_op, right_op, (((1,), (1,)), ((), ())), preferred_element_type=jnp.float32
    )


def full_rows(columns):
    return lax.all_gather(columns, "tensor", axis=1, tiled=True)


def to_cols(partial_sum):
    return lax.psum_scatter(
        partial_sum.astype(jnp.bfloat16), "tensor", scatter_dimension=1, tiled=True
    ).astype(jnp.float32)


def grad_rows(columns):
    return lax.all_gather(columns, "tensor", axis=1, tiled=True)


def grad_cols(partial_sum):
    return lax.psum_scatter(
        partial_sum.astype(jnp.bfloat16), "tensor", scatter_dimension=1, tiled=True
    ).astype(jnp.float32)


def row_total(values):
    return lax.psum(jnp.sum(values, axis=1), "tensor")


def sphere(values):
    row_ratio = lax.rsqrt(row_total(values * values) / D + EPSILON)[:, None]
    return (values * row_ratio, row_ratio)


def sphere_back(source, row_ratio, grad_in):
    inner_sum = row_total(grad_in * source)[:, None]
    return row_ratio * grad_in - source * (row_ratio * row_ratio * row_ratio) * inner_sum / D


def pass_on(dkv_sum):
    return passed_along(dkv_sum.astype(jnp.bfloat16), "dp", 1).astype(dkv_sum.dtype)


def unchanged(previous):
    return previous


def per_device(hidden_in, cotangent, lengths, w_qkv, w_out, w_ug, w_down, s_qk, s_uv, alpha):
    micro_n = hidden_in.shape[0]
    tok_rows = hidden_in.shape[1]
    col_width = hidden_in.shape[2]
    heads_here = col_width // HEAD_DIM
    ff_here = w_down.shape[1]
    dp_ranks = lax.axis_size("dp")
    dp_rank = lax.axis_index("dp")
    longest = min(SEQ_CAP, tok_rows * dp_ranks // 2)
    reach_len = min(dp_ranks - 1, (longest + tok_rows - 2) // tok_rows)
    first_section = lax.axis_index("section") == 0
    score_div = math.sqrt(HEAD_DIM)
    qkv_mat = w_qkv[0].reshape(D, 3 * col_width)
    out_mat = w_out[0]
    ug_mat = w_ug[0].reshape(D, 2 * ff_here)
    down_mat = w_down[0]
    scale_qk = s_qk[0]
    scale_up = s_uv[0, 0]
    scale_gate = s_uv[0, 1]
    alpha_attn = alpha[0, 0]
    alpha_mlp = alpha[0, 1]
    local_rows = jnp.arange(tok_rows, dtype=jnp.int32)
    q_index = dp_rank * tok_rows + local_rows
    indicator = (
        jnp.arange(col_width, dtype=jnp.int32)[:, None] // HEAD_DIM
        == jnp.arange(heads_here, dtype=jnp.int32)[None, :]
    ).astype(jnp.float32)

    def head_sum(values):
        return jnp.dot(values, indicator, precision=HIGHEST, preferred_element_type=jnp.float32)

    def spread(small):
        return jnp.dot(small, indicator.T, precision=HIGHEST, preferred_element_type=jnp.float32)

    def block_info(lengths_row, q_segment, offset):
        source = dp_rank - offset
        k_index = source * tok_rows + local_rows
        k_segment, unused = seq_table(lengths_row, k_index)
        key_mask = (
            (k_segment[None, :] == q_segment[:, None])
            & (k_index[None, :] <= q_index[:, None])
            & (k_index[None, :] >= 0)
        )
        needed = (source * tok_rows + tok_rows - 1 >= 0) & (k_segment[tok_rows - 1] >= q_segment[0])
        return (key_mask, needed)

    def block_scores(q_heads, kv_block):
        key_heads = kv_block[:, :col_width].reshape(tok_rows, heads_here, HEAD_DIM)
        return (
            jnp.einsum("qhd,khd->hqk", q_heads, key_heads, preferred_element_type=jnp.float32)
            / score_div
        )

    def prep_back(grad_n, rotated, head_ratio, record):
        unit_vec = rotated * head_ratio
        d_scale = jnp.sum(grad_n * unit_vec, axis=0)
        d_unit = grad_n * scale_qk[None, :]
        d_rot = head_ratio * d_unit - rotated * (head_ratio * head_ratio * head_ratio) * spread(
            head_sum(d_unit * rotated) / HEAD_DIM
        )
        return (
            d_rot * record["cosine"] - partner(d_rot * record["sine_tab"], record["lower_half"]),
            d_scale,
        )

    received_in = jnp.zeros((tok_rows, col_width), jnp.bfloat16)
    records = []
    results = []
    for tick_no in range(micro_n + 1):
        early_mb = min(tick_no, micro_n - 1)
        late_mb = max(tick_no - 1, 0)
        lengths_row = jnp.where(first_section, lengths[early_mb], lengths[late_mb])
        layer_in = jnp.where(first_section, hidden_in[early_mb], received_in)
        hidden = layer_in.astype(jnp.float32)
        forward_q_segment, places = seq_table(lengths_row, q_index)
        cosine, sine_tab, lower_half = rope_tables(places, col_width)
        full_in = full_rows(hidden.astype(jnp.bfloat16))
        qkv = jnp.dot(full_in, qkv_mat, preferred_element_type=jnp.float32)
        q_raw = qkv[:, :col_width]
        k_raw = qkv[:, col_width : 2 * col_width]
        q_rot = q_raw * cosine + partner(q_raw, lower_half) * sine_tab
        k_rot = k_raw * cosine + partner(k_raw, lower_half) * sine_tab
        q_ratio = spread(lax.rsqrt(head_sum(q_rot * q_rot) / HEAD_DIM + EPSILON))
        k_ratio = spread(lax.rsqrt(head_sum(k_rot * k_rot) / HEAD_DIM + EPSILON))
        query_b = (q_rot * q_ratio * scale_qk[None, :]).astype(jnp.bfloat16)
        key_b = (k_rot * k_ratio * scale_qk[None, :]).astype(jnp.bfloat16)
        value_b = qkv[:, 2 * col_width :].astype(jnp.bfloat16)
        forward_q_heads = query_b.reshape(tok_rows, heads_here, HEAD_DIM)
        own_block = jnp.concatenate([key_b, value_b], axis=1)

        def lse_step(lse_state, kv_block, offset):
            key_mask, needed = block_info(lengths_row, forward_q_segment, offset)

            def update(previous):
                run_max, run_sum = previous
                masked = jnp.where(
                    key_mask[None], block_scores(forward_q_heads, kv_block), NEG_LARGE
                )
                new_max = jnp.maximum(run_max, jnp.max(masked, axis=2))
                exp_terms = jnp.where(key_mask[None], jnp.exp(masked - new_max[:, :, None]), 0.0)
                return (new_max, run_sum * jnp.exp(run_max - new_max) + jnp.sum(exp_terms, axis=2))

            return lax.cond(needed, update, unchanged, lse_state)

        init_state = (
            jnp.full((heads_here, tok_rows), NEG_LARGE, jnp.float32),
            jnp.zeros((heads_here, tok_rows), jnp.float32),
        )
        lse_state = lse_step(init_state, own_block, jnp.int32(0))

        def cycle_step(state_in, offset):
            kv_block, lse_now = state_in
            kv_block = from_behind(kv_block, "dp", 1)
            return ((kv_block, lse_step(lse_now, kv_block, offset)), kv_block)

        (forward_unused_block, lse_state), received = lax.scan(
            cycle_step, (own_block, lse_state), jnp.arange(1, reach_len + 1, dtype=jnp.int32)
        )
        kv_stack = jnp.concatenate([own_block[None], received], axis=0)
        forward_log_total = lse_state[0] + jnp.log(lse_state[1])

        def value_step(acc_heads, scan_item):
            kv_block, offset = scan_item
            key_mask, needed = block_info(lengths_row, forward_q_segment, offset)

            def add_values(previous):
                attn_prob = jnp.where(
                    key_mask[None],
                    jnp.exp(
                        block_scores(forward_q_heads, kv_block) - forward_log_total[:, :, None]
                    ),
                    0.0,
                ).astype(jnp.bfloat16)
                val_heads = kv_block[:, col_width:].reshape(tok_rows, heads_here, HEAD_DIM)
                return previous + jnp.einsum(
                    "hqk,khd->hqd", attn_prob, val_heads, preferred_element_type=jnp.float32
                )

            return (lax.cond(needed, add_values, unchanged, acc_heads), None)

        acc_heads, forward_unused_out = lax.scan(
            value_step,
            jnp.zeros((heads_here, tok_rows, HEAD_DIM), jnp.float32),
            (kv_stack, jnp.arange(reach_len + 1, dtype=jnp.int32)),
        )
        attended = jnp.transpose(acc_heads, (1, 0, 2)).reshape(tok_rows, col_width)
        attended_b = attended.astype(jnp.bfloat16)
        attn_raw = to_cols(jnp.dot(attended_b, out_mat, preferred_element_type=jnp.float32))
        attn_n, ratio_a = sphere(attn_raw)
        mix_one = hidden + alpha_attn[None, :] * (attn_n - hidden)
        normed_one, ratio_one = sphere(mix_one)
        inner_full = full_rows(normed_one.astype(jnp.bfloat16))
        forward_upgate = jnp.dot(inner_full, ug_mat, preferred_element_type=jnp.float32)
        forward_up_s = forward_upgate[:, :ff_here] * scale_up[None, :]
        forward_gate_s = forward_upgate[:, ff_here:] * scale_gate[None, :]
        act_b = (forward_up_s * jax.nn.silu(forward_gate_s)).astype(jnp.bfloat16)
        mlp_raw = to_cols(jnp.dot(act_b, down_mat, preferred_element_type=jnp.float32))
        mlp_n, ratio_m = sphere(mlp_raw)
        mix_two = normed_one + alpha_mlp[None, :] * (mlp_n - normed_one)
        result, ratio_two = sphere(mix_two)
        kept_blocks = own_block[None]
        forward_record = {
            "lengths_row": lengths_row,
            "q_segment": forward_q_segment,
            "cosine": cosine,
            "sine_tab": sine_tab,
            "lower_half": lower_half,
            "full_in": full_in,
            "q_rot": q_rot,
            "k_rot": k_rot,
            "q_ratio": q_ratio,
            "k_ratio": k_ratio,
            "query_b": query_b,
            "blocks": kept_blocks,
            "log_total": forward_log_total,
            "attended": attended,
            "attended_b": attended_b,
            "hidden": hidden,
            "attn_raw": attn_raw,
            "ratio_a": ratio_a,
            "attn_n": attn_n,
            "mix_one": mix_one,
            "ratio_one": ratio_one,
            "normed_one": normed_one,
            "inner_full": inner_full,
            "upgate": forward_upgate,
            "act_b": act_b,
            "mlp_raw": mlp_raw,
            "ratio_m": ratio_m,
            "mlp_n": mlp_n,
            "mix_two": mix_two,
            "ratio_two": ratio_two,
        }
        record, result = (forward_record, result)
        result_b = result.astype(jnp.bfloat16)
        records.append(record)
        results.append(result_b)
        if tick_no < micro_n:
            received_in = from_behind(result_b, "section", 1)
    layer_outputs = jnp.stack(
        [
            jnp.where(first_section, results[number], results[number + 1])
            for number in range(micro_n)
        ]
    )
    back_in = jnp.zeros((tok_rows, col_width), jnp.bfloat16)
    grad_totals = None
    back_results = []
    for tick_no in range(micro_n + 1):
        record = records[micro_n - tick_no]
        late_cot = cotangent[max(micro_n - 1 - tick_no, 0)].astype(jnp.float32)
        live_flag = jnp.where(
            first_section, 1.0 if tick_no >= 1 else 0.0, 1.0 if tick_no < micro_n else 0.0
        )
        grad_out = jnp.where(first_section, back_in.astype(jnp.float32), late_cot) * live_flag
        backward_lengths_row = record["lengths_row"]
        backward_q_segment = record["q_segment"]
        dz_two = sphere_back(record["mix_two"], record["ratio_two"], grad_out)
        d_normed = (1.0 - alpha_mlp)[None, :] * dz_two
        d_mlp_n = alpha_mlp[None, :] * dz_two
        d_alpha_mlp = jnp.sum(dz_two * (record["mlp_n"] - record["normed_one"]), axis=0)
        d_mlp = sphere_back(record["mlp_raw"], record["ratio_m"], d_mlp_n)
        d_mlp_full = grad_rows(d_mlp.astype(jnp.bfloat16))
        dw_down = contract_rows(record["act_b"], d_mlp_full)
        d_act = contract_cols(d_mlp_full, down_mat)
        upgate = record["upgate"]
        up_s = upgate[:, :ff_here] * scale_up[None, :]
        gate_s = upgate[:, ff_here:] * scale_gate[None, :]
        gate_sig = jax.nn.sigmoid(gate_s)
        d_up = d_act * gate_s * gate_sig
        d_gate = d_act * up_s * gate_sig * (1.0 + gate_s * (1.0 - gate_sig))
        d_scale_up = jnp.sum(d_up * upgate[:, :ff_here], axis=0)
        d_scale_gate = jnp.sum(d_gate * upgate[:, ff_here:], axis=0)
        d_upgate = jnp.concatenate(
            [d_up * scale_up[None, :], d_gate * scale_gate[None, :]], axis=1
        ).astype(jnp.bfloat16)
        dw_ug = contract_rows(record["inner_full"], d_upgate)
        d_normed = d_normed + grad_cols(contract_cols(d_upgate, ug_mat))
        dz_one = sphere_back(record["mix_one"], record["ratio_one"], d_normed)
        d_hidden = (1.0 - alpha_attn)[None, :] * dz_one
        d_attn_n = alpha_attn[None, :] * dz_one
        d_alpha_attn = jnp.sum(dz_one * (record["attn_n"] - record["hidden"]), axis=0)
        d_attn = sphere_back(record["attn_raw"], record["ratio_a"], d_attn_n)
        d_attn_full = grad_rows(d_attn.astype(jnp.bfloat16))
        dw_out = contract_rows(record["attended_b"], d_attn_full)
        d_attended = contract_cols(d_attn_full, out_mat).astype(jnp.bfloat16)
        row_delta = jnp.transpose(head_sum(d_attended.astype(jnp.float32) * record["attended"]))
        do_heads = d_attended.reshape(tok_rows, heads_here, HEAD_DIM)
        backward_q_heads = record["query_b"].reshape(tok_rows, heads_here, HEAD_DIM)
        log_total = record["log_total"]

        def block_grads(dq_now, kv_block, offset):
            key_mask, needed = block_info(backward_lengths_row, backward_q_segment, offset)

            def compute(previous):
                key_heads = kv_block[:, :col_width].reshape(tok_rows, heads_here, HEAD_DIM)
                val_heads = kv_block[:, col_width:].reshape(tok_rows, heads_here, HEAD_DIM)
                attn_prob = jnp.where(
                    key_mask[None],
                    jnp.exp(block_scores(backward_q_heads, kv_block) - log_total[:, :, None]),
                    0.0,
                )
                d_prob = jnp.einsum(
                    "qhd,khd->hqk", do_heads, val_heads, preferred_element_type=jnp.float32
                )
                d_val = jnp.einsum(
                    "hqk,qhd->khd",
                    attn_prob.astype(jnp.bfloat16),
                    do_heads,
                    preferred_element_type=jnp.float32,
                )
                d_score = (attn_prob * (d_prob - row_delta[:, :, None])).astype(jnp.bfloat16)
                new_dq = (
                    previous
                    + jnp.einsum(
                        "hqk,khd->hqd", d_score, key_heads, preferred_element_type=jnp.float32
                    )
                    / score_div
                )
                d_key = (
                    jnp.einsum(
                        "hqk,qhd->khd",
                        d_score,
                        backward_q_heads,
                        preferred_element_type=jnp.float32,
                    )
                    / score_div
                )
                return (
                    jnp.concatenate(
                        [d_key.reshape(tok_rows, col_width), d_val.reshape(tok_rows, col_width)],
                        axis=1,
                    ),
                    new_dq,
                )

            def skipped(previous):
                return (jnp.zeros((tok_rows, 2 * col_width), jnp.float32), previous)

            return lax.cond(needed, compute, skipped, dq_now)

        own_part, dq_acc = block_grads(
            jnp.zeros((heads_here, tok_rows, HEAD_DIM), jnp.float32),
            record["blocks"][0],
            jnp.int32(0),
        )
        offsets = jnp.arange(1, reach_len + 1, dtype=jnp.int32)

        def again_step(state_in, offset):
            dkv_sum, kv_block, dq_now = state_in
            dkv_sum = pass_on(dkv_sum)
            kv_block = from_behind(kv_block, "dp", 1)
            dkv_part, dq_now = block_grads(dq_now, kv_block, offset)
            return ((dkv_sum + dkv_part, kv_block, dq_now), None)

        (dkv_sum, unused_block, dq_acc), unused_out = lax.scan(
            again_step, (own_part, record["blocks"][0], dq_acc), offsets
        )
        dkv_home = passed_along(dkv_sum.astype(jnp.bfloat16), "dp", -reach_len).astype(
            dkv_sum.dtype
        )
        dq_full = jnp.transpose(dq_acc, (1, 0, 2)).reshape(tok_rows, col_width)
        dq_raw, ds_query = prep_back(dq_full, record["q_rot"], record["q_ratio"], record)
        dk_raw, ds_key = prep_back(
            dkv_home[:, :col_width], record["k_rot"], record["k_ratio"], record
        )
        d_qkv = jnp.concatenate([dq_raw, dk_raw, dkv_home[:, col_width:]], axis=1).astype(
            jnp.bfloat16
        )
        dw_qkv = contract_rows(record["full_in"], d_qkv)
        d_hidden = d_hidden + grad_cols(contract_cols(d_qkv, qkv_mat))
        grads = (
            dw_qkv.reshape(D, 3, col_width),
            dw_out,
            dw_ug.reshape(D, 2, ff_here),
            dw_down,
            ds_query + ds_key,
            jnp.stack([d_scale_up, d_scale_gate]),
            jnp.stack([d_alpha_attn, d_alpha_mlp]),
        )
        d_hidden, grads = (d_hidden, grads)
        grad_b = d_hidden.astype(jnp.bfloat16)
        back_results.append(grad_b)
        grad_totals = grads if grad_totals is None else jax.tree.map(jnp.add, grad_totals, grads)
        if tick_no < micro_n:
            back_in = from_behind(grad_b, "section", -1)
    input_grads = jnp.stack(
        [
            jnp.where(
                first_section, back_results[micro_n - number], back_results[micro_n - 1 - number]
            )
            for number in range(micro_n)
        ]
    )
    summed = (
        lax.psum_scatter(
            grad_totals[0].astype(jnp.bfloat16), "dp", scatter_dimension=0, tiled=True
        ).astype(jnp.float32),
        lax.psum_scatter(
            grad_totals[1].astype(jnp.bfloat16), "dp", scatter_dimension=0, tiled=True
        ).astype(jnp.float32),
        lax.psum_scatter(
            grad_totals[2].astype(jnp.bfloat16), "dp", scatter_dimension=0, tiled=True
        ).astype(jnp.float32),
        lax.psum_scatter(
            grad_totals[3].astype(jnp.bfloat16), "dp", scatter_dimension=0, tiled=True
        ).astype(jnp.float32),
        lax.psum_scatter(
            grad_totals[4].astype(jnp.bfloat16), "dp", scatter_dimension=0, tiled=True
        ).astype(jnp.float32),
        lax.psum_scatter(
            grad_totals[5].astype(jnp.bfloat16), "dp", scatter_dimension=1, tiled=True
        ).astype(jnp.float32),
        lax.psum_scatter(
            grad_totals[6].astype(jnp.bfloat16), "dp", scatter_dimension=1, tiled=True
        ).astype(jnp.float32),
    )
    return (
        layer_outputs[None],
        input_grads[None],
        summed[0][None],
        summed[1][None],
        summed[2][None],
        summed[3][None],
        summed[4][None],
        summed[5][None],
        summed[6][None],
    )


MESH = pl.DeviceIdType.MESH
MICRO = 2
F32 = jnp.float32
BF16 = jnp.bfloat16


def mul(left_op, right_op):
    return jnp.dot(left_op, right_op, preferred_element_type=F32)


def remote(src, dst, send_sem, recv_sem, device):
    return pltpu.make_async_remote_copy(
        src_ref=src, dst_ref=dst, send_sem=send_sem, recv_sem=recv_sem, device_id=device, device_id_type=MESH
    )


def ball(values, width):
    ratio = lax.rsqrt(jnp.sum(values * values, axis=1, keepdims=True) / width + EPSILON)
    return values * ratio, ratio


def ball_back(source, ratio, grad_in, width):
    inner = jnp.sum(grad_in * source, axis=1, keepdims=True)
    return ratio * grad_in - source * (ratio * ratio * ratio) * (inner / width)


def buffers(nt, nz, rows, width, cols, hidden, shard, section, chunk):
    vmem, dma = pltpu.VMEM, pltpu.SemaphoreType.DMA
    pair = 2 * rows
    return dict(
        wq=vmem((2, 3, width, cols), BF16),
        wo=vmem((2, cols, width), BF16),
        wu=vmem((2, 2, width, hidden), BF16),
        wd=vmem((2, hidden, width), BF16),
        sqk=vmem((2, 1, cols), F32),
        suv=vmem((2, 2, hidden), F32),
        alp=vmem((2, 2, width), F32),
        raw=vmem((2 * hidden // 128 * width, 128), BF16),
        raw_f=vmem((2 * hidden // 128 * 64, 128), F32),
        full_in=vmem((2, rows, width), BF16),
        mid_full=vmem((2, nt, shard, width), BF16),
        dml_full=vmem((2, nt, shard, width), BF16),
        dat_full=vmem((2, rows, width), BF16),
        fi_p=vmem((rows, width), BF16),
        at_p=vmem((rows, cols), BF16),
        da_p=vmem((rows, width), BF16),
        dq_p=vmem((rows, 3 * cols), BF16),
        xa=vmem((nt, nz * 2 * shard, width), BF16),
        da=vmem((nt, nz * 2 * shard, width), BF16),
        kv=vmem((2, pair, 2 * cols), BF16),
        dkv_f=vmem((pair, 2 * cols), F32),
        dkv_s=vmem((2, rows, 2 * cols), BF16),
        dkv_r=vmem((2, rows, 2 * cols), BF16),
        rs_s=vmem((8, rows, width), BF16),
        rs_r=vmem((8, nt - 1, shard, width), BF16),
        rot=vmem((2, 2, rows, cols), F32),
        rat=vmem((2, 2, rows, cols), F32),
        qb=vmem((2, rows, cols), BF16),
        prob=vmem((2, cols // HEAD_DIM, rows, pair), F32),
        at=vmem((2, rows, cols), BF16),
        araw=vmem((2, shard, width), F32),
        mraw=vmem((2, shard, width), F32),
        mid=vmem((2, shard, width), F32),
        zone=vmem((2, shard, width), F32),
        ztwo=vmem((2, shard, width), F32),
        up=vmem((2, rows, hidden), F32),
        gate=vmem((2, rows, hidden), F32),
        act=vmem((rows, hidden), BF16),
        duv=vmem((2, rows, hidden), BF16),
        dqkv=vmem((2, rows, 3 * cols), BF16),
        cot_rows=vmem((shard, width), BF16),
        out_s=vmem((2, shard, width), BF16),
        ig_s=vmem((2, shard, width), BF16),
        cosb=vmem((rows, cols), F32),
        sinb=vmem((rows, cols), F32),
        bias=vmem((rows, pair), F32),
        blk=vmem((cols, cols), BF16),
        al_s=vmem((2, 8, width), F32),
        al_r=vmem((2, nt - 1, 8, cols), F32),
        small=vmem((2, 8, cols), F32),
        sm_r=vmem((nz, 2, 8, cols), F32),
        wq_s=vmem((nz - 1, section, 3 * cols), BF16),
        wq_r=vmem((nz, section, 3 * cols), BF16),
        wo_f=vmem((cols, width), F32),
        wo_s=vmem((cols, width), BF16),
        wo_r=vmem((nz - 1, chunk, width), BF16),
        act_b=vmem((nz * 2 * shard, hidden), BF16),
        suv_b=vmem((2, hidden), F32),
        acc=vmem((2, section, hidden), F32),
        w_l=dma((2, 4)), w_rs=dma((4,)),
        par_l=dma((2, 2)), par_s=dma((2,)),
        alp_r=dma((2, nt)), alp_s=dma((2, nt)),
        hid_r=dma((nt,)), hid_s=dma((2, nt)),
        cot_r=dma((nt,)), cot_s=dma((2, nt)),
        fi_rs=dma((2,)), at_rs=dma((2,)), dap_rs=dma((2,)), dq_rs=dma((2,)),
        kv_rs=dma((2, 2)), dkv_rs=dma((2, 2)),
        ag_ss=dma((7, nt - 1)), ag_rr=dma((7, nt - 1)),
        rs_ss=dma((8, 2, nt - 1)), rs_rr=dma((8, 2, nt - 1)),
        xa_r=dma((nz, 2)), xa_ss=dma((2, nz)),
        da_r=dma((nz, 2)), da_ss=dma((2, nz)),
        df_ss=dma((nz - 1, nt - 1)), df_rr=dma((nz - 1, nt - 1)),
        xf_ss=dma((nz - 1, nt - 1)), xf_rr=dma((nz - 1, nt - 1)),
        lo_ss=dma((2, nt)), lo_r=dma((2, nt)),
        ig_ss=dma((2, nt)), ig_r=dma((2, nt)),
        al_ss=dma((2, nt - 1)), al_rr=dma((2, nt - 1)),
        sm_ss=dma((2, nz)), sm_rr=dma((nz, 2)),
        wq_ss=dma((nz - 1, 2)), wq_rr=dma((nz, 2)),
        wo_ss=dma((nz - 1,)), wo_rr=dma((nz - 1,)),
    )


def fused_kernel(names, nt, nz, *refs):
    hid, cot, lens, wq_in, wo_in, wu_in, wd_in, sqk_in, suv_in, alp_in, rates = refs[:11]
    lo, ig, gq, go, gu, gd, gsqk, gsuv, gal = refs[11:20]
    b = types.SimpleNamespace(**dict(zip(names, refs[20:])))
    rows, width = b.full_in.shape[1:]
    cols, hidden = b.qb.shape[2], b.wd.shape[1]
    shard = b.mid.shape[1]
    heads = cols // HEAD_DIM
    pair = 2 * rows
    section_rows = width // nz
    chunk = cols // nz
    tile = 512
    s, t, z = lax.axis_index("section"), lax.axis_index("tensor"), lax.axis_index("dp")
    p = lax.rem(z, 2)
    base = z - p
    peer = (1 - s, t, z)
    pending = []

    def around(k):
        return lax.rem(lax.div(t, 2) + k // 2, 2) * 2 + lax.rem(lax.rem(t, 2) + k % 2, 2)

    peers = (3, 1, 2)

    def along(k):
        return lax.rem(z + k, nz)

    def later(copy, when=None):
        pending.append((copy, when))

    def lanes(index, size):
        return pl.ds(pl.multiple_of(index * size, size), size)

    weights = [(wq_in, b.wq), (wo_in, b.wo), (None, b.wu), (wd_in, b.wd)]
    raw_copy = pltpu.make_async_copy(wu_in, b.raw, b.w_l.at[s, 2])
    raw_copy.start()
    for i in (0, 1, 3):
        src, dst = weights[i]
        pltpu.make_async_copy(src, dst.at[s], b.w_l.at[s, i]).start()
    params = [(sqk_in, b.sqk), (suv_in, b.suv)]
    for i, (src, dst) in enumerate(params):
        pltpu.make_async_copy(src, dst.at[s], b.par_l.at[s, i]).start()

    barrier = pltpu.get_barrier_semaphore()
    greeted = 0
    for dz in range(2):
        for dt in range(nt):
            for dc in range(2):
                if dz or dt or dc:
                    device = (lax.rem(s + dc, 2), around(dt), base + lax.rem(p + dz, 2))
                    pl.semaphore_signal(barrier, inc=1, device_id=device, device_id_type=MESH)
                    greeted += 1
    for dz in range(2, nz):
        for dc in range(2):
            device = (lax.rem(s + dc, 2), t, lax.rem(base + dz, nz))
            pl.semaphore_signal(barrier, inc=1, device_id=device, device_id_type=MESH)
            greeted += 1
    token0 = (base // 2) * pair
    pos_q = token0 + s * rows + lax.broadcasted_iota(jnp.int32, (rows, 1), 0)
    pos_k = token0 + lax.broadcasted_iota(jnp.int32, (1, pair), 1)

    def sequences(pos):
        seg = jnp.zeros_like(pos)
        first = jnp.zeros_like(pos)
        end = jnp.int32(0)
        for i in range(lens.shape[1]):
            end = end + lens[p, i]
            past = pos >= end
            seg = seg + past.astype(jnp.int32)
            first = jnp.where(past, end, first)
        return seg, pos - first

    seg_q, place_q = sequences(pos_q)
    seg_k, _ = sequences(pos_k)
    allowed = (seg_q == seg_k) & (pos_k <= pos_q)
    b.bias[...] = jnp.where(allowed, 0.0, NEG_LARGE)
    angle = place_q.astype(F32) * rates[...]
    b.cosb[...] = jnp.cos(angle)
    b.sinb[...] = jnp.sin(angle)
    col = lax.broadcasted_iota(jnp.int32, (1, cols), 1)
    lower = (col & (HEAD_DIM // 2)) == 0
    head_of = lax.shift_right_logical(col, 6)
    head_row = lax.shift_right_logical(lax.broadcasted_iota(jnp.int32, (cols, 1), 0), 6)
    b.blk[...] = jnp.where(head_row == head_of, 1.0, 0.0).astype(BF16)
    picks = [jnp.where(head_of == h, 1.0, 0.0) for h in range(heads)]
    b.al_s[...] = jnp.zeros_like(b.al_s)
    b.small[...] = jnp.zeros_like(b.small)

    @pl.when(s == 0)
    def _():
        b.kv[:, rows:pair, :] = jnp.zeros((2, rows, 2 * cols), BF16)

    @pl.when(s == 1)
    def _():
        b.dkv_r[...] = jnp.zeros_like(b.dkv_r)


    def to_order():
        raw_copy.wait()
        lines = 2 * hidden // 128

        def in_order(step, carry):
            b.raw_f[...] = b.raw[pl.ds(pl.multiple_of(step * lines * 64, lines * 64), lines * 64), :].astype(F32)
            at = pl.ds(pl.multiple_of(step * 64, 64), 64)
            for n in range(hidden // 128):
                for i in range(2):
                    b.wu[s, i, at, n * 128 : (n + 1) * 128] = b.raw_f[pl.ds(2 * n + i, 64, stride=lines), :].astype(BF16)
            return carry

        lax.fori_loop(0, width // 64, in_order, 0)

    pl.semaphore_wait(barrier, greeted)

    is_source = s == p
    def spread_rows(src, rs, ss):
        for dz in range(2):
            to_mb = lax.rem(p + dz, 2)
            for dt in peers + (0,):
                to_t = around(dt)
                if src is hid:
                    piece, place = src.at[to_mb], b.full_in.at[0, :, lanes(t, cols)]
                else:
                    piece = src.at[to_mb, pl.ds(pl.multiple_of(to_t * shard, shard), shard), :]
                    place = b.cot_rows.at[:, lanes(t, cols)]
                if dz == 0 and dt == 0:

                    @pl.when(is_source)
                    def _(piece=piece, place=place, rs=rs):
                        pltpu.make_async_copy(piece, place, rs.at[0]).start()
                else:
                    copy = remote(piece, place, ss.at[dz, dt], rs.at[dt], (s, to_t, base + to_mb))
                    pl.when(is_source)(copy.start)
                    later(copy, is_source)

    spread_rows(hid, b.hid_r, b.hid_s)
    for i, (src_p, dst_p) in enumerate(params):
        copy = remote(src_p, dst_p.at[s], b.par_s.at[i], b.par_l.at[s, i], peer)
        copy.start()
        later(copy)
    alp_src, alp_dst = alp_in, b.alp.at[s, :, lanes(t, cols)]
    for dc in range(2):
        for dt in range(nt):
            if dc == 0 and dt == 0:
                pltpu.make_async_copy(alp_src, alp_dst, b.alp_r.at[s, 0]).start()
            else:
                copy = remote(alp_src, alp_dst, b.alp_s.at[dc, dt], b.alp_r.at[s, dt], (lax.rem(s + dc, 2), around(dt), z))
                copy.start()
                later(copy)
    for i in (0, 1, 3):
        src_w, dst_w = weights[i]
        copy = remote(src_w, dst_w.at[s], b.w_rs.at[i], b.w_l.at[s, i], peer)
        copy.start()
        later(copy)

    def wait_weight(layer, i):
        dst_w = weights[i][1].at[layer]
        wait = pltpu.make_async_copy(dst_w, dst_w, b.w_l.at[layer, i]).wait
        if i == 2:
            pl.when(s != layer)(wait)
        else:
            wait()

    to_order()
    copy = remote(b.wu.at[s], b.wu.at[s], b.w_rs.at[2], b.w_l.at[s, 2], peer)
    copy.start()
    later(copy)

    def partner_cols(x):
        half = HEAD_DIM // 2
        return jnp.where(lower, -pltpu.roll(x, cols - half, 1), pltpu.roll(x, half, 1))

    def head_total(x):
        high = x.astype(BF16)
        low = (x - high.astype(F32)).astype(BF16)
        return mul(high, b.blk[...]) + mul(low, b.blk[...])

    def shard_of(ref, index):
        return ref.at[index] if len(ref.shape) == 3 else ref.at[pl.ds(pl.multiple_of(index * shard, shard), shard), :]

    def gather(stage, ref):
        mine = shard_of(ref, t)
        for k in peers:
            copy = remote(mine, mine, b.ag_ss.at[stage, k - 1], b.ag_rr.at[stage, k - 1], (s, around(k), z))
            copy.start()
            later(copy)

    def gather_wait(stage, ref):
        for k in range(1, nt):
            theirs = shard_of(ref, around(k))
            remote(theirs, theirs, b.ag_ss.at[stage, k - 1], b.ag_rr.at[stage, k - 1], (s, around(k), z)).wait_recv()

    def scatter(stage, n):
        cut = pl.ds(n * tile, tile)
        for k in peers:
            piece = b.rs_s.at[stage, pl.ds(pl.multiple_of(around(k) * shard, shard), shard), cut]
            copy = remote(piece, b.rs_r.at[stage, k - 1, :, cut], b.rs_ss.at[stage, n, k - 1], b.rs_rr.at[stage, n, k - 1], (s, around(k), z))
            copy.start()
            later(copy)

    def scatter_wait(stage):
        total = b.rs_s[stage, pl.ds(pl.multiple_of(t * shard, shard), shard), :].astype(F32)
        for n in range(width // tile):
            for k in range(1, nt):
                place = b.rs_r.at[stage, k - 1, :, pl.ds(n * tile, tile)]
                remote(place, place, b.rs_ss.at[stage, n, k - 1], b.rs_rr.at[stage, n, k - 1], (s, around(k), z)).wait_recv()
        for k in range(1, nt):
            total = total + b.rs_r[stage, k - 1].astype(F32)
        return total

    slot = pl.ds(pl.multiple_of((z * 2 + s) * shard, shard), shard)

    def my_rows(ref):
        return shard_of(ref, t)

    def to_owner(layer, ref, place_of, send_sems, recv_sems, hops=range(nz)):
        for k in hops:
            copy = remote(ref, place_of, send_sems.at[layer, k], recv_sems.at[k, s], (layer, t, along(k)))
            if k == 0:

                @pl.when(s == layer)
                def _():
                    pltpu.make_async_copy(ref, place_of, recv_sems.at[0, s]).start()

                pl.when(s != layer)(copy.start)
                later(copy, s != layer)
            else:
                copy.start()
                later(copy)

    x_rows = (b.xa, b.xa_r, b.xf_ss, b.xf_rr)
    d_rows = (b.da, b.da_r, b.df_ss, b.df_rr)

    def bundle(layer, hops, group):
        ref, arrived, send_sems, recv_sems = group
        for k in hops:
            from_z = along(nz - k)
            rows_of = pl.ds(pl.multiple_of(from_z * 2 * shard, 2 * shard), 2 * shard)

            @pl.when(s == layer)
            def _(k=k, from_z=from_z):
                for core in range(2):
                    row = pl.multiple_of((from_z * 2 + core) * shard, shard)
                    place = ref.at[t, pl.ds(row, shard), :]
                    pltpu.make_async_copy(place, place, arrived.at[k, core]).wait()

            for to in range(1, nt):
                place = ref.at[t, rows_of, :]
                copy = remote(place, place, send_sems.at[k - 1, to - 1], recv_sems.at[k - 1, to - 1], (s, around(to), z))
                pl.when(s == layer)(copy.start)
                later(copy, s == layer)

    def to_output(layer, ref, out, send_sems, recv_sems):
        to_z = base + s
        place = out.at[p, pl.ds(pl.multiple_of(t * shard, shard), shard), :]
        for k in range(nt):
            to_t = around(k)
            piece = ref.at[:, lanes(to_t, cols)]
            copy = remote(piece, place, send_sems.at[layer, k], recv_sems.at[p, k], (layer, to_t, to_z))
            if k == 0:
                here = (s == layer) & (to_z == z)

                @pl.when(here)
                def _(piece=piece):
                    pltpu.make_async_copy(piece, place, recv_sems.at[p, 0]).start()

                away = jnp.logical_not(here)
                pl.when(away)(copy.start)
                later(copy, away)
            else:
                copy.start()
                later(copy)

    upper = z // 2
    end, hub = 3 * upper, 1 + upper
    sibling = end + hub - z
    far_end, far_hub = 3 - end, 3 - hub

    def qkv_part(n, to, half, device):
        rows_of = pl.ds(half * (section_rows // 2), section_rows // 2)
        return remote(b.wq_s.at[n, rows_of], b.wq_r.at[to, rows_of], b.wq_ss.at[n, half], b.wq_rr.at[to, half], device)

    def hub_step(layer, n, half):
        @pl.when((s == layer) & (z == hub))
        def _():
            qkv_part(n, n, half, peer).wait_recv()
            rows_of = pl.ds(half * (section_rows // 2), section_rows // 2)
            b.wq_s[n, rows_of] = (b.wq_s[n, rows_of].astype(F32) + b.wq_r[n, rows_of].astype(F32)).astype(BF16)
            qkv_part(n, 3, half, (layer, t, far_hub if n else far_end)).start()

    for layer in range(2):
        full_in = b.full_in.at[layer]
        if layer == 0:
            for dt in range(nt):
                place = b.full_in.at[0, :, lanes(around(dt), cols)]
                pltpu.make_async_copy(hid.at[0], place, b.hid_r.at[dt]).wait()
            spread_rows(cot, b.cot_r, b.cot_s)
            for src_core in range(2):
                for i, (src_p, dst_p) in enumerate(params):
                    pltpu.make_async_copy(src_p, dst_p.at[src_core], b.par_l.at[src_core, i]).wait()
                for dt in range(nt):
                    place = b.alp.at[src_core, :, lanes(around(dt), cols)]
                    pltpu.make_async_copy(alp_in, place, b.alp_r.at[src_core, dt]).wait()
        else:
            gather_wait(6, full_in)
        copy = remote(full_in, b.fi_p, b.fi_rs.at[0], b.fi_rs.at[1], peer)
        pl.when(s != layer)(copy.start)
        later(copy, s != layer)
        scale_qk = b.sqk[layer]
        wait_weight(layer, 0)
        x = full_in[...]
        own = pl.ds(pl.multiple_of(s * rows, rows), rows)
        def normed_heads(i):
            raw = mul(x, b.wq[layer, i])
            rotated = raw * b.cosb[...] + partner_cols(raw) * b.sinb[...]
            ratio = lax.rsqrt(head_total(rotated * rotated) / HEAD_DIM + EPSILON)
            b.rot[layer, i] = rotated
            b.rat[layer, i] = ratio
            return (rotated * ratio * scale_qk).astype(BF16)

        b.kv[layer, own, 0:cols] = normed_heads(1)
        b.kv[layer, own, cols : 2 * cols] = mul(x, b.wq[layer, 2]).astype(BF16)
        mine = b.kv.at[layer, own, :]
        copy = remote(mine, mine, b.kv_rs.at[layer, 0], b.kv_rs.at[layer, 1], peer)
        pl.when(s == 0)(copy.start)
        later(copy, s == 0)
        b.qb[layer] = normed_heads(0)
        pl.when(s == 1)(copy.wait_recv)
        att = jnp.zeros((rows, cols), F32)
        for h in range(heads):
            q_h = (b.qb[layer].astype(F32) * picks[h]).astype(BF16)
            scores = contract_cols(q_h, b.kv[layer, :, 0:cols]) * (1.0 / math.sqrt(HEAD_DIM)) + b.bias[...]
            top = jnp.max(scores, axis=1, keepdims=True)
            terms = jnp.exp(scores - top)
            prob = terms / jnp.sum(terms, axis=1, keepdims=True)
            b.prob[layer, h] = prob
            att = att + picks[h] * mul(prob.astype(BF16), b.kv[layer, :, cols : 2 * cols])
        b.at[layer] = att.astype(BF16)
        wait_weight(layer, 1)
        for n in range(0, width, tile):
            b.rs_s[layer, :, n : n + tile] = mul(b.at[layer], b.wo[layer, :, n : n + tile]).astype(BF16)
            scatter(layer, n // tile)
        hin = my_rows(full_in)[...].astype(F32)
        rate_a = b.alp[layer, 0:1, :]
        rate_m = b.alp[layer, 1:2, :]
        araw = scatter_wait(layer)
        b.araw[layer] = araw
        zone = hin + rate_a * (ball(araw, width)[0] - hin)
        b.zone[layer] = zone
        mid = ball(zone, width)[0]
        b.mid[layer] = mid
        mid_full = b.mid_full.at[layer]
        my_rows(mid_full)[...] = mid.astype(BF16)
        gather(layer, mid_full)
        if layer == 1:
            to_owner(1, my_rows(mid_full), b.xa.at[t, slot, :], b.xa_ss, b.xa_r, range(1, nz))
        wait_weight(layer, 2)
        wait_weight(layer, 3)
        gather_wait(layer, mid_full)
        to_owner(layer, mid_full, b.xa.at[:, slot, :], b.xa_ss, b.xa_r, range(nz) if layer == 0 else (0,))
        x = mid_full[...].reshape(rows, width)
        for n in range(0, hidden, tile):
            cut = slice(n, n + tile)
            up = mul(x, b.wu[layer, 0, :, cut])
            gate = mul(x, b.wu[layer, 1, :, cut])
            b.up[layer, :, cut] = up
            b.gate[layer, :, cut] = gate
            gate_s = gate * b.suv[layer, 1:2, cut]
            b.act[:, cut] = (up * b.suv[layer, 0:1, cut] * (gate_s / (1.0 + jnp.exp(-gate_s)))).astype(BF16)
        for n in range(0, width, tile):
            b.rs_s[2 + layer, :, n : n + tile] = mul(b.act[...], b.wd[layer, :, n : n + tile]).astype(BF16)
            scatter(2 + layer, n // tile)
        if layer == 1:
            bundle(1, (1,), x_rows)
        mraw = scatter_wait(2 + layer)
        b.mraw[layer] = mraw
        ztwo = mid + rate_m * (ball(mraw, width)[0] - mid)
        b.ztwo[layer] = ztwo
        b.out_s[layer] = ball(ztwo, width)[0].astype(BF16)
        if layer == 0:
            my_rows(b.full_in.at[1])[...] = b.out_s[0]
            gather(6, b.full_in.at[1])
            to_output(0, b.out_s.at[0], lo, b.lo_ss, b.lo_r)

    mine_cols = lanes(z, section_rows)

    def block(k, suv_now, between=None):
        at = lax.rem(lax.div(t, 2) + lax.div(k, 2), 2) * 2 + lax.rem(t + k, 2)
        first = suv_now is None
        if first:
            for hop in range(nz):
                for core in range(2):
                    rows_of = pl.ds(pl.multiple_of((along(nz - hop) * 2 + core) * shard, shard), shard)
                    for ref, sems in ((b.xa, b.xa_r), (b.da, b.da_r)):
                        place = ref.at[:, rows_of, :]
                        wait = pltpu.make_async_copy(place, place, sems.at[hop, core]).wait
                        if hop == 0:
                            wait()
                        elif ref is b.xa:
                            pl.when(s == 0)(wait)
        else:
            for hop in range(1, nz):
                for ref, _, ss, rr in (d_rows, x_rows):
                    place = ref.at[at, pl.ds(pl.multiple_of(along(nz - hop) * 2 * shard, 2 * shard), 2 * shard), :]
                    wait = remote(place, place, ss.at[hop - 1, k - 1], rr.at[hop - 1, k - 1], peer).wait_recv
                    if ref is b.da:
                        wait()
                    else:
                        pl.when(s == 1)(wait)

        def add(ref, value):
            ref[...] = value if first else ref[...] + value

        new = []
        for n in range(0, hidden, tile):
            cut = slice(n, n + tile)
            up = mul(b.xa[at], b.wu[s, 0, :, cut])
            gate = mul(b.xa[at], b.wu[s, 1, :, cut])
            d_act = contract_cols(b.da[at], b.wd[s, cut, :])
            scale_up, scale_gate = b.suv[s, 0:1, cut], b.suv[s, 1:2, cut]
            up_s = up * scale_up
            gate_s = gate * scale_gate
            sig = 1.0 / (1.0 + jnp.exp(-gate_s))
            b.act_b[:, cut] = (up_s * gate_s * sig).astype(BF16)
            d_up = d_act * gate_s * sig
            d_gate = d_act * up_s * sig * (1.0 + gate_s * (1.0 - sig))
            new.append((jnp.sum(d_up * up, axis=0, keepdims=True), jnp.sum(d_gate * gate, axis=0, keepdims=True)))
            if between is not None and n:
                between()
            x_cut = b.xa[at, :, mine_cols]
            add(b.acc.at[0, :, cut], contract_rows(x_cut, (d_up * scale_up).astype(BF16)))
            add(b.acc.at[1, :, cut], contract_rows(x_cut, (d_gate * scale_gate).astype(BF16)))
        for n in range(0, width, tile):
            cut = slice(n, n + tile)
            add(gd.at[:, cut], contract_rows(b.act_b[:, lanes(z, hidden // nz)], b.da[at, :, cut]))
        sums = tuple(jnp.concatenate([pair_of[i] for pair_of in new], axis=1) for i in range(2))
        return sums if first else tuple(now + more for now, more in zip(suv_now, sums))

    for dt in range(nt):
        place = b.cot_rows.at[:, lanes(around(dt), cols)]
        pltpu.make_async_copy(cot.at[0, pl.ds(0, shard), :], place, b.cot_r.at[dt]).wait()
    grad_out = b.cot_rows[...].astype(F32)
    for layer in (1, 0):
        own = pl.ds(pl.multiple_of(s * rows, rows), rows)
        other = pl.ds(pl.multiple_of((1 - s) * rows, rows), rows)
        rate_a = b.alp[layer, 0:1, :]
        rate_m = b.alp[layer, 1:2, :]
        scale_qk = b.sqk[layer]
        mid = b.mid[layer]
        mraw_n, ratio_m = ball(b.mraw[layer], width)
        ratio_two = ball(b.ztwo[layer], width)[1]
        d_two = ball_back(b.ztwo[layer], ratio_two, grad_out, width)
        d_mid = (1.0 - rate_m) * d_two
        b.al_s[layer, 1:2, :] = jnp.sum(d_two * (mraw_n - mid), axis=0, keepdims=True)
        dml_full = b.dml_full.at[layer]
        my_rows(dml_full)[...] = ball_back(b.mraw[layer], ratio_m, rate_m * d_two, width).astype(BF16)
        gather(2 + layer, dml_full)
        if layer == 1:
            to_output(1, b.out_s.at[1], lo, b.lo_ss, b.lo_r)
        else:
            to_output(1, b.ig_s.at[1], ig, b.ig_ss, b.ig_r)
        to_owner(layer, my_rows(dml_full), b.da.at[t, slot, :], b.da_ss, b.da_r, range(1, nz))
        if layer == 1:
            bundle(1, (2, 3), x_rows)
        gather_wait(2 + layer, dml_full)
        to_owner(layer, dml_full, b.da.at[:, slot, :], b.da_ss, b.da_r, (0,))
        if layer == 0:
            bundle(1, (3,), d_rows)
        x = dml_full[...].reshape(rows, width)
        for n in range(0, hidden, tile):
            cut = slice(n, n + tile)
            d_act = contract_cols(x, b.wd[layer, cut, :])
            scale_up, scale_gate = b.suv[layer, 0:1, cut], b.suv[layer, 1:2, cut]
            up_s = b.up[layer, :, cut] * scale_up
            gate_s = b.gate[layer, :, cut] * scale_gate
            sig = 1.0 / (1.0 + jnp.exp(-gate_s))
            b.duv[0, :, cut] = (d_act * gate_s * sig * scale_up).astype(BF16)
            b.duv[1, :, cut] = (d_act * up_s * sig * (1.0 + gate_s * (1.0 - sig)) * scale_gate).astype(BF16)
        for n in range(0, width, tile):
            cut = slice(n, n + tile)
            part = contract_cols(b.duv[0], b.wu[layer, 0, cut, :]) + contract_cols(b.duv[1], b.wu[layer, 1, cut, :])
            b.rs_s[4 + layer, :, cut] = part.astype(BF16)
            scatter(4 + layer, n // tile)
        hin = my_rows(b.full_in.at[layer])[...].astype(F32)
        araw_n, ratio_a = ball(b.araw[layer], width)
        ratio_one = ball(b.zone[layer], width)[1]
        d_mid = d_mid + scatter_wait(4 + layer)
        d_one = ball_back(b.zone[layer], ratio_one, d_mid, width)
        b.al_s[layer, 0:1, :] = jnp.sum(d_one * (araw_n - hin), axis=0, keepdims=True)
        dat_full = b.dat_full.at[layer]
        my_rows(dat_full)[...] = ball_back(b.araw[layer], ratio_a, rate_a * d_one, width).astype(BF16)
        gather(4 + layer, dat_full)
        for k in range(1, nt):
            copy = remote(b.al_s.at[layer, :, lanes(around(k), cols)], b.al_r.at[layer, k - 1], b.al_ss.at[layer, k - 1], b.al_rr.at[layer, k - 1], (s, around(k), z))
            copy.start()
            later(copy)
        if layer == 0:
            for n in range(2):
                for half in range(2):
                    hub_step(1, n, half)
        gather_wait(4 + layer, dat_full)
        for src_v, dst_v, sems in ((dat_full, b.da_p, b.dap_rs), (b.at.at[layer], b.at_p, b.at_rs)):
            copy = remote(src_v, dst_v, sems.at[0], sems.at[1], peer)
            pl.when(s != layer)(copy.start)
            later(copy, s != layer)
        d_att = contract_cols(dat_full[...], b.wo[layer])
        d_scores = []
        dk = jnp.zeros((pair, cols), F32)
        dv = jnp.zeros((pair, cols), F32)
        for h in range(heads):
            d_att_h = (d_att * picks[h]).astype(BF16)
            q_h = (b.qb[layer].astype(F32) * picks[h]).astype(BF16)
            prob = b.prob[layer, h]
            d_prob = contract_cols(d_att_h, b.kv[layer, :, cols : 2 * cols])
            d_score = (prob * (d_prob - jnp.sum(prob * d_prob, axis=1, keepdims=True))).astype(BF16)
            dv = dv + contract_rows(prob.astype(BF16), d_att_h)
            d_scores.append(d_score)
            dk = dk + contract_rows(d_score, q_h)
        b.dkv_f[:, 0:cols] = dk * (1.0 / math.sqrt(HEAD_DIM))
        b.dkv_f[:, cols : 2 * cols] = dv
        b.dkv_s[layer] = b.dkv_f[other, :].astype(BF16)
        copy = remote(b.dkv_s.at[layer], b.dkv_r.at[layer], b.dkv_rs.at[layer, 0], b.dkv_rs.at[layer, 1], peer)
        pl.when(s == 1)(copy.start)
        later(copy, s == 1)
        bundle(layer, (1, 2), d_rows)
        dq = jnp.zeros((rows, cols), F32)
        for h in range(heads):
            dq = dq + picks[h] * mul(d_scores[h], b.kv[layer, :, 0:cols])

        @pl.when(s == layer)
        def _(layer=layer):
            for dst_v, sems in ((b.da_p, b.dap_rs), (b.at_p, b.at_rs)):
                remote(dst_v, dst_v, sems.at[0], sems.at[1], peer).wait_recv()
            for n in range(0, width, tile):
                cut = slice(n, n + tile)
                part = contract_rows(b.at[layer], b.dat_full[layer, :, cut]) + contract_rows(b.at_p[...], b.da_p[:, cut])
                b.wo_f[:, cut] = part
                b.wo_s[:, cut] = part.astype(BF16)
            for k in range(1, nz):
                piece = b.wo_s.at[pl.ds(pl.multiple_of(along(k) * chunk, chunk), chunk), :]
                remote(piece, b.wo_r.at[k - 1], b.wo_ss.at[k - 1], b.wo_rr.at[k - 1], (layer, t, along(k))).start()

        d_scale = jnp.zeros((1, cols), F32)
        for i in range(2):
            if i == 0:
                grad_n = dq * (1.0 / math.sqrt(HEAD_DIM))
            else:
                pl.when(s == 0)(copy.wait_recv)
                grad_n = b.dkv_f[own, 0:cols] + b.dkv_r[layer, :, 0:cols].astype(F32)
            rotated, ratio = b.rot[layer, i], b.rat[layer, i]
            d_scale = d_scale + jnp.sum(grad_n * rotated * ratio, axis=0, keepdims=True)
            d_unit = grad_n * scale_qk
            d_rot = ratio * d_unit - rotated * (ratio * ratio * ratio) * (head_total(d_unit * rotated) / HEAD_DIM)
            d_raw = d_rot * b.cosb[...] - partner_cols(d_rot * b.sinb[...])
            b.dqkv[layer, :, i * cols : (i + 1) * cols] = d_raw.astype(BF16)
        d_val = b.dkv_f[own, cols : 2 * cols] + b.dkv_r[layer, :, cols : 2 * cols].astype(F32)
        b.dqkv[layer, :, 2 * cols : 3 * cols] = d_val.astype(BF16)
        copy = remote(b.dqkv.at[layer], b.dq_p, b.dq_rs.at[0], b.dq_rs.at[1], peer)
        pl.when(s != layer)(copy.start)
        later(copy, s != layer)
        def qkv_pieces(layer=layer):
            for dst_v, sems in ((b.fi_p, b.fi_rs), (b.dq_p, b.dq_rs)):
                remote(dst_v, dst_v, sems.at[0], sems.at[1], peer).wait_recv()
            for n, index in enumerate((far_end, far_hub, sibling, z)):
                cut = lanes(index, section_rows)
                part = contract_rows(b.full_in[layer, :, cut], b.dqkv[layer]) + contract_rows(b.fi_p[:, cut], b.dq_p[...])
                if n == 3:
                    for i in range(3):
                        gq[i] = part[:, i * cols : (i + 1) * cols]
                    continue
                b.wq_s[n] = part.astype(BF16)
                for half in range(2):
                    start = qkv_part(n, n, half, (layer, t, sibling)).start
                    if n == 2:
                        start()
                    else:
                        pl.when(z == end)(start)

        def last_sum(layer=layer):
            for n in range(0, width, tile):
                part = contract_cols(b.dqkv[layer, :, 0:cols], b.wq[layer, 0, n : n + tile, :])
                for i in range(1, 3):
                    part = part + contract_cols(b.dqkv[layer, :, i * cols : (i + 1) * cols], b.wq[layer, i, n : n + tile, :])
                b.rs_s[6 + layer, :, n : n + tile] = part.astype(BF16)
                scatter(6 + layer, n // tile)

        if layer == 1:
            last_sum()
        pl.when(s == layer)(qkv_pieces)
        if layer == 0:
            last_sum()
        total = b.al_s[layer, :, lanes(t, cols)]
        for k in range(1, nt):
            place = b.al_r.at[layer, k - 1]
            remote(place, place, b.al_ss.at[layer, k - 1], b.al_rr.at[layer, k - 1], peer).wait_recv()
            total = total + place[...]
        b.small[layer] = total
        b.small[layer, 2:3, :] = d_scale
        to_owner(layer, b.small.at[layer], b.sm_r.at[lax.rem(z, nz), s], b.sm_ss, b.sm_rr)

        if layer == 0:
            bundle(0, (3,), d_rows)
            suv = block(0, None)
            hub_step(0, 0, 0)
        d_hin = (1.0 - rate_a) * d_one + scatter_wait(6 + layer)
        b.ig_s[layer] = d_hin.astype(BF16)
        if layer == 0:
            to_output(0, b.ig_s.at[0], ig, b.ig_ss, b.ig_r)
        grad_out = b.ig_s[layer].astype(F32)

    hub_step(0, 0, 1)
    suv = block(1, suv, lambda: hub_step(0, 1, 0))
    hub_step(0, 1, 1)
    suv = lax.fori_loop(2, nt, block, suv)
    for i in range(2):
        b.suv_b[i : i + 1, :] = suv[i]
    gsuv[...] = b.suv_b[:, lanes(z, hidden // nz)]
    per_row = 2 * hidden // 128
    for j in range(hidden // 128):
        for i in range(2):
            gu[pl.ds(2 * j + i, section_rows, stride=per_row), :] = b.acc[i, :, j * 128 : (j + 1) * 128]

    for n in (2, 3):
        for half in range(2):
            qkv_part(2, n, half, peer).wait_recv()
            rows_of = slice(half * (section_rows // 2), (half + 1) * (section_rows // 2))
            for i in range(3):
                gq[i, rows_of] += b.wq_r[n, rows_of, i * cols : (i + 1) * cols].astype(F32)
    total = b.wo_f[pl.ds(pl.multiple_of(z * chunk, chunk), chunk), :]
    for k in range(1, nz):
        place = b.wo_r.at[k - 1]
        remote(place, place, b.wo_ss.at[k - 1], b.wo_rr.at[k - 1], peer).wait_recv()
        total = total + place[...].astype(F32)
    go[...] = total
    total = jnp.zeros((8, cols), F32)
    for k in range(nz):
        for core in range(2):
            place = b.sm_r.at[lax.rem(z + nz - k, nz), core]
            pltpu.make_async_copy(place, place, b.sm_rr.at[k, core]).wait()
            total = total + place[...]
    turned = pltpu.roll(total, lax.rem(cols - z * chunk, cols), 1)
    gal[...] = turned[0:2, 0:chunk]
    gsqk[...] = turned[2:3, 0:chunk]
    for out, sems in ((lo, b.lo_r), (ig, b.ig_r)):
        for m in range(2):
            for k in range(nt):
                place = out.at[m, pl.ds(pl.multiple_of(around(k) * shard, shard), shard), :]
                pltpu.make_async_copy(place, place, sems.at[m, k]).wait()
    for k in range(nz - 1):
        for half in range(2):
            qkv_part(k, k, half, peer).wait_send()
        piece = b.wo_s.at[pl.ds(0, chunk), :]
        remote(piece, b.wo_r.at[k], b.wo_ss.at[k], b.wo_rr.at[k], peer).wait_send()
    for copy, when in pending:
        if when is None:
            copy.wait_send()
        else:
            pl.when(when)(copy.wait_send)


def copy_kernel(*refs):
    count = len(refs) // 3
    sems = refs[-1]
    reads = [pltpu.make_async_copy(refs[i], refs[2 * count + i], sems.at[0, i]) for i in range(count)]
    writes = [pltpu.make_async_copy(refs[2 * count + i], refs[count + i], sems.at[1, i]) for i in range(count)]
    for copy in reads:
        copy.start()
    for read, write in zip(reads, writes):
        read.wait()
        write.start()
    for copy in writes:
        copy.wait()


def per_device_fused(hidden_in, cotangent, lengths, w_qkv, w_out, w_ug, w_down, s_qk, s_uv, alpha):
    nt, nz = lax.axis_size("tensor"), lax.axis_size("dp")
    rows, cols = hidden_in.shape[1:]
    width, hidden = w_out.shape[2], w_down.shape[1]
    shard, section, chunk = rows // nt, width // nz, cols // nz
    half = HEAD_DIM // 2
    rates = (10000.0 ** (-(np.arange(cols) % half).astype(np.float32) / half)).astype(np.float32)[None, :]
    pairs = w_ug[0].reshape(width, 2, hidden // 128, 128).transpose(0, 2, 1, 3).reshape(2 * hidden // 128 * width, 128)
    scratch = buffers(nt, nz, rows, width, cols, hidden, shard, section, chunk)
    anywhere = pl.BlockSpec(memory_space=pl.ANY)
    vmem = pl.BlockSpec(memory_space=pltpu.VMEM)
    smem = pl.BlockSpec(memory_space=pltpu.SMEM)
    outs = pl.pallas_call(
        functools.partial(fused_kernel, tuple(scratch), nt, nz),
        out_shape=(
            jax.ShapeDtypeStruct((MICRO, rows, cols), BF16),
            jax.ShapeDtypeStruct((MICRO, rows, cols), BF16),
            jax.ShapeDtypeStruct((3, section, cols), F32),
            jax.ShapeDtypeStruct((chunk, width), F32),
            jax.ShapeDtypeStruct((section * 2 * hidden // 128, 128), F32),
            jax.ShapeDtypeStruct((hidden // nz, width), F32),
            jax.ShapeDtypeStruct((1, chunk), F32),
            jax.ShapeDtypeStruct((2, hidden // nz), F32),
            jax.ShapeDtypeStruct((2, chunk), F32),
        ),
        in_specs=[anywhere, anywhere, smem] + [anywhere] * 7 + [vmem],
        out_specs=(anywhere, anywhere) + (vmem,) * 7,
        scratch_shapes=list(scratch.values()),
        compiler_params=pltpu.CompilerParams(
            collective_id=0, has_side_effects=True, vmem_limit_bytes=60 * 2**20
        ),
    )(
        hidden_in,
        cotangent,
        lengths,
        jnp.transpose(w_qkv[0], (1, 0, 2)),
        w_out[0],
        pairs,
        w_down[0],
        s_qk,
        s_uv[0],
        alpha[0],
        jnp.asarray(rates),
    )
    lo, ig, gq, go, gu, gd, gsqk, gsuv, gal = pl.pallas_call(
        copy_kernel,
        out_shape=tuple(jax.ShapeDtypeStruct(o.shape, o.dtype) for o in outs),
        in_specs=[anywhere] * len(outs),
        out_specs=(anywhere,) * len(outs),
        scratch_shapes=[pltpu.VMEM(o.shape, o.dtype) for o in outs] + [pltpu.SemaphoreType.DMA((2, len(outs)))],
        compiler_params=pltpu.CompilerParams(vmem_limit_bytes=60 * 2**20),
    )(*outs)
    gu = gu.reshape(section, hidden // 128, 2, 128).transpose(0, 2, 1, 3).reshape(section, 2, hidden)
    return (
        lo[None],
        ig[None],
        jnp.transpose(gq, (1, 0, 2))[None],
        go[None],
        gu[None],
        gd[None],
        gsqk,
        gsuv[None],
        gal[None],
    )


def solution(mesh):
    placed = (
        P(None, "dp", "tensor"),
        P(None, "dp", "tensor"),
        P(),
        P("section", None, None, "tensor"),
        P("section", "tensor", None),
        P("section", None, None, "tensor"),
        P("section", "tensor", None),
        P("section", "tensor"),
        P("section", None, "tensor"),
        P("section", None, "tensor"),
    )
    per_rank = per_device_fused if mesh.shape["dp"] == 2 * MICRO and mesh.shape["tensor"] == 4 else per_device
    return jax.shard_map(
        per_rank,
        mesh=mesh,
        in_specs=placed,
        out_specs=(
            P("section", None, "dp", "tensor"),
            P("section", None, "dp", "tensor"),
            P("section", "dp", None, "tensor"),
            P("section", ("tensor", "dp"), None),
            P("section", "dp", None, "tensor"),
            P("section", ("tensor", "dp"), None),
            P("section", ("tensor", "dp")),
            P("section", None, ("tensor", "dp")),
            P("section", None, ("tensor", "dp")),
        ),
        check_vma=False,
    )
```

```python
import functools
import math
import types

import jax
import jax.numpy as jnp
import numpy as np
from jax import lax
from jax.experimental import pallas as pl
from jax.experimental.pallas import tpu as pltpu
from jax.sharding import PartitionSpec as P

D = 1024
HEAD_DIM = 64
SEQ_CAP = 4096


EPSILON = 1e-05
HIGHEST = lax.Precision.HIGHEST
NEG_LARGE = -1e30


def passed_along(array, axis, by):
    count = lax.axis_size(axis)
    return lax.ppermute(array, axis, [(i, (i + by) % count) for i in range(count)])


def from_behind(array, axis, by):
    count = lax.axis_size(axis)
    pairs = [(i, i + by) for i in range(count) if 0 <= i + by < count]
    return lax.ppermute(array, axis, pairs)


def seq_table(lengths_row, positions):
    count = lengths_row.shape[0]
    order = jnp.arange(count, dtype=jnp.int32)
    seq_end = jnp.sum(jnp.where(order[None, :] <= order[:, None], lengths_row[None, :], 0), axis=1)
    seq_start = seq_end - lengths_row
    segment = jnp.sum((positions[:, None] >= seq_end[None, :]).astype(jnp.int32), axis=1)
    labels = jnp.arange(lengths_row.shape[0], dtype=jnp.int32)
    first_tok = jnp.sum(
        jnp.where(segment[:, None] == labels[None, :], seq_start[None, :], 0), axis=1
    )
    return (segment, positions - first_tok)


def rope_tables(places, col_width):
    column = jnp.arange(col_width, dtype=jnp.int32) % HEAD_DIM
    half_dim = HEAD_DIM // 2
    rope_rates = 10000.0 ** (-(column % half_dim).astype(jnp.float32) / half_dim)
    angles = places.astype(jnp.float32)[:, None] * rope_rates[None, :]
    return (jnp.cos(angles), jnp.sin(angles), column < half_dim)


def partner(values, lower_half):
    half_dim = HEAD_DIM // 2
    return jnp.where(
        lower_half[None, :],
        -jnp.roll(values, -half_dim, axis=1),
        jnp.roll(values, half_dim, axis=1),
    )


def contract_rows(left_op, right_op):
    return lax.dot_general(
        left_op, right_op, (((0,), (0,)), ((), ())), preferred_element_type=jnp.float32
    )


def contract_cols(left_op, right_op):
    return lax.dot_general(
        left_op, right_op, (((1,), (1,)), ((), ())), preferred_element_type=jnp.float32
    )


def full_rows(columns):
    return lax.all_gather(columns, "tensor", axis=1, tiled=True)


def to_cols(partial_sum):
    return lax.psum_scatter(
        partial_sum.astype(jnp.bfloat16), "tensor", scatter_dimension=1, tiled=True
    ).astype(jnp.float32)


def grad_rows(columns):
    return lax.all_gather(columns, "tensor", axis=1, tiled=True)


def grad_cols(partial_sum):
    return lax.psum_scatter(
        partial_sum.astype(jnp.bfloat16), "tensor", scatter_dimension=1, tiled=True
    ).astype(jnp.float32)


def row_total(values):
    return lax.psum(jnp.sum(values, axis=1), "tensor")


def sphere(values):
    row_ratio = lax.rsqrt(row_total(values * values) / D + EPSILON)[:, None]
    return (values * row_ratio, row_ratio)


def sphere_back(source, row_ratio, grad_in):
    inner_sum = row_total(grad_in * source)[:, None]
    return row_ratio * grad_in - source * (row_ratio * row_ratio * row_ratio) * inner_sum / D


def pass_on(dkv_sum):
    return passed_along(dkv_sum.astype(jnp.bfloat16), "dp", 1).astype(dkv_sum.dtype)


def unchanged(previous):
    return previous


def per_device(hidden_in, cotangent, lengths, w_qkv, w_out, w_ug, w_down, s_qk, s_uv, alpha):
    micro_n = hidden_in.shape[0]
    tok_rows = hidden_in.shape[1]
    col_width = hidden_in.shape[2]
    heads_here = col_width // HEAD_DIM
    ff_here = w_down.shape[1]
    dp_ranks = lax.axis_size("dp")
    dp_rank = lax.axis_index("dp")
    longest = min(SEQ_CAP, tok_rows * dp_ranks // 2)
    reach_len = min(dp_ranks - 1, (longest + tok_rows - 2) // tok_rows)
    first_section = lax.axis_index("section") == 0
    score_div = math.sqrt(HEAD_DIM)
    qkv_mat = w_qkv[0].reshape(D, 3 * col_width)
    out_mat = w_out[0]
    ug_mat = w_ug[0].reshape(D, 2 * ff_here)
    down_mat = w_down[0]
    scale_qk = s_qk[0]
    scale_up = s_uv[0, 0]
    scale_gate = s_uv[0, 1]
    alpha_attn = alpha[0, 0]
    alpha_mlp = alpha[0, 1]
    local_rows = jnp.arange(tok_rows, dtype=jnp.int32)
    q_index = dp_rank * tok_rows + local_rows
    indicator = (
        jnp.arange(col_width, dtype=jnp.int32)[:, None] // HEAD_DIM
        == jnp.arange(heads_here, dtype=jnp.int32)[None, :]
    ).astype(jnp.float32)

    def head_sum(values):
        return jnp.dot(values, indicator, precision=HIGHEST, preferred_element_type=jnp.float32)

    def spread(small):
        return jnp.dot(small, indicator.T, precision=HIGHEST, preferred_element_type=jnp.float32)

    def block_info(lengths_row, q_segment, offset):
        source = dp_rank - offset
        k_index = source * tok_rows + local_rows
        k_segment, unused = seq_table(lengths_row, k_index)
        key_mask = (
            (k_segment[None, :] == q_segment[:, None])
            & (k_index[None, :] <= q_index[:, None])
            & (k_index[None, :] >= 0)
        )
        needed = (source * tok_rows + tok_rows - 1 >= 0) & (k_segment[tok_rows - 1] >= q_segment[0])
        return (key_mask, needed)

    def block_scores(q_heads, kv_block):
        key_heads = kv_block[:, :col_width].reshape(tok_rows, heads_here, HEAD_DIM)
        return (
            jnp.einsum("qhd,khd->hqk", q_heads, key_heads, preferred_element_type=jnp.float32)
            / score_div
        )

    def prep_back(grad_n, rotated, head_ratio, record):
        unit_vec = rotated * head_ratio
        d_scale = jnp.sum(grad_n * unit_vec, axis=0)
        d_unit = grad_n * scale_qk[None, :]
        d_rot = head_ratio * d_unit - rotated * (head_ratio * head_ratio * head_ratio) * spread(
            head_sum(d_unit * rotated) / HEAD_DIM
        )
        return (
            d_rot * record["cosine"] - partner(d_rot * record["sine_tab"], record["lower_half"]),
            d_scale,
        )

    received_in = jnp.zeros((tok_rows, col_width), jnp.bfloat16)
    records = []
    results = []
    for tick_no in range(micro_n + 1):
        early_mb = min(tick_no, micro_n - 1)
        late_mb = max(tick_no - 1, 0)
        lengths_row = jnp.where(first_section, lengths[early_mb], lengths[late_mb])
        layer_in = jnp.where(first_section, hidden_in[early_mb], received_in)
        hidden = layer_in.astype(jnp.float32)
        forward_q_segment, places = seq_table(lengths_row, q_index)
        cosine, sine_tab, lower_half = rope_tables(places, col_width)
        full_in = full_rows(hidden.astype(jnp.bfloat16))
        qkv = jnp.dot(full_in, qkv_mat, preferred_element_type=jnp.float32)
        q_raw = qkv[:, :col_width]
        k_raw = qkv[:, col_width : 2 * col_width]
        q_rot = q_raw * cosine + partner(q_raw, lower_half) * sine_tab
        k_rot = k_raw * cosine + partner(k_raw, lower_half) * sine_tab
        q_ratio = spread(lax.rsqrt(head_sum(q_rot * q_rot) / HEAD_DIM + EPSILON))
        k_ratio = spread(lax.rsqrt(head_sum(k_rot * k_rot) / HEAD_DIM + EPSILON))
        query_b = (q_rot * q_ratio * scale_qk[None, :]).astype(jnp.bfloat16)
        key_b = (k_rot * k_ratio * scale_qk[None, :]).astype(jnp.bfloat16)
        value_b = qkv[:, 2 * col_width :].astype(jnp.bfloat16)
        forward_q_heads = query_b.reshape(tok_rows, heads_here, HEAD_DIM)
        own_block = jnp.concatenate([key_b, value_b], axis=1)

        def lse_step(lse_state, kv_block, offset):
            key_mask, needed = block_info(lengths_row, forward_q_segment, offset)

            def update(previous):
                run_max, run_sum = previous
                masked = jnp.where(
                    key_mask[None], block_scores(forward_q_heads, kv_block), NEG_LARGE
                )
                new_max = jnp.maximum(run_max, jnp.max(masked, axis=2))
                exp_terms = jnp.where(key_mask[None], jnp.exp(masked - new_max[:, :, None]), 0.0)
                return (new_max, run_sum * jnp.exp(run_max - new_max) + jnp.sum(exp_terms, axis=2))

            return lax.cond(needed, update, unchanged, lse_state)

        init_state = (
            jnp.full((heads_here, tok_rows), NEG_LARGE, jnp.float32),
            jnp.zeros((heads_here, tok_rows), jnp.float32),
        )
        lse_state = lse_step(init_state, own_block, jnp.int32(0))

        def cycle_step(state_in, offset):
            kv_block, lse_now = state_in
            kv_block = from_behind(kv_block, "dp", 1)
            return ((kv_block, lse_step(lse_now, kv_block, offset)), kv_block)

        (forward_unused_block, lse_state), received = lax.scan(
            cycle_step, (own_block, lse_state), jnp.arange(1, reach_len + 1, dtype=jnp.int32)
        )
        kv_stack = jnp.concatenate([own_block[None], received], axis=0)
        forward_log_total = lse_state[0] + jnp.log(lse_state[1])

        def value_step(acc_heads, scan_item):
            kv_block, offset = scan_item
            key_mask, needed = block_info(lengths_row, forward_q_segment, offset)

            def add_values(previous):
                attn_prob = jnp.where(
                    key_mask[None],
                    jnp.exp(
                        block_scores(forward_q_heads, kv_block) - forward_log_total[:, :, None]
                    ),
                    0.0,
                ).astype(jnp.bfloat16)
                val_heads = kv_block[:, col_width:].reshape(tok_rows, heads_here, HEAD_DIM)
                return previous + jnp.einsum(
                    "hqk,khd->hqd", attn_prob, val_heads, preferred_element_type=jnp.float32
                )

            return (lax.cond(needed, add_values, unchanged, acc_heads), None)

        acc_heads, forward_unused_out = lax.scan(
            value_step,
            jnp.zeros((heads_here, tok_rows, HEAD_DIM), jnp.float32),
            (kv_stack, jnp.arange(reach_len + 1, dtype=jnp.int32)),
        )
        attended = jnp.transpose(acc_heads, (1, 0, 2)).reshape(tok_rows, col_width)
        attended_b = attended.astype(jnp.bfloat16)
        attn_raw = to_cols(jnp.dot(attended_b, out_mat, preferred_element_type=jnp.float32))
        attn_n, ratio_a = sphere(attn_raw)
        mix_one = hidden + alpha_attn[None, :] * (attn_n - hidden)
        normed_one, ratio_one = sphere(mix_one)
        inner_full = full_rows(normed_one.astype(jnp.bfloat16))
        forward_upgate = jnp.dot(inner_full, ug_mat, preferred_element_type=jnp.float32)
        forward_up_s = forward_upgate[:, :ff_here] * scale_up[None, :]
        forward_gate_s = forward_upgate[:, ff_here:] * scale_gate[None, :]
        act_b = (forward_up_s * jax.nn.silu(forward_gate_s)).astype(jnp.bfloat16)
        mlp_raw = to_cols(jnp.dot(act_b, down_mat, preferred_element_type=jnp.float32))
        mlp_n, ratio_m = sphere(mlp_raw)
        mix_two = normed_one + alpha_mlp[None, :] * (mlp_n - normed_one)
        result, ratio_two = sphere(mix_two)
        kept_blocks = own_block[None]
        forward_record = {
            "lengths_row": lengths_row,
            "q_segment": forward_q_segment,
            "cosine": cosine,
            "sine_tab": sine_tab,
            "lower_half": lower_half,
            "full_in": full_in,
            "q_rot": q_rot,
            "k_rot": k_rot,
            "q_ratio": q_ratio,
            "k_ratio": k_ratio,
            "query_b": query_b,
            "blocks": kept_blocks,
            "log_total": forward_log_total,
            "attended": attended,
            "attended_b": attended_b,
            "hidden": hidden,
            "attn_raw": attn_raw,
            "ratio_a": ratio_a,
            "attn_n": attn_n,
            "mix_one": mix_one,
            "ratio_one": ratio_one,
            "normed_one": normed_one,
            "inner_full": inner_full,
            "upgate": forward_upgate,
            "act_b": act_b,
            "mlp_raw": mlp_raw,
            "ratio_m": ratio_m,
            "mlp_n": mlp_n,
            "mix_two": mix_two,
            "ratio_two": ratio_two,
        }
        record, result = (forward_record, result)
        result_b = result.astype(jnp.bfloat16)
        records.append(record)
        results.append(result_b)
        if tick_no < micro_n:
            received_in = from_behind(result_b, "section", 1)
    layer_outputs = jnp.stack(
        [
            jnp.where(first_section, results[number], results[number + 1])
            for number in range(micro_n)
        ]
    )
    back_in = jnp.zeros((tok_rows, col_width), jnp.bfloat16)
    grad_totals = None
    back_results = []
    for tick_no in range(micro_n + 1):
        record = records[micro_n - tick_no]
        late_cot = cotangent[max(micro_n - 1 - tick_no, 0)].astype(jnp.float32)
        live_flag = jnp.where(
            first_section, 1.0 if tick_no >= 1 else 0.0, 1.0 if tick_no < micro_n else 0.0
        )
        grad_out = jnp.where(first_section, back_in.astype(jnp.float32), late_cot) * live_flag
        backward_lengths_row = record["lengths_row"]
        backward_q_segment = record["q_segment"]
        dz_two = sphere_back(record["mix_two"], record["ratio_two"], grad_out)
        d_normed = (1.0 - alpha_mlp)[None, :] * dz_two
        d_mlp_n = alpha_mlp[None, :] * dz_two
        d_alpha_mlp = jnp.sum(dz_two * (record["mlp_n"] - record["normed_one"]), axis=0)
        d_mlp = sphere_back(record["mlp_raw"], record["ratio_m"], d_mlp_n)
        d_mlp_full = grad_rows(d_mlp.astype(jnp.bfloat16))
        dw_down = contract_rows(record["act_b"], d_mlp_full)
        d_act = contract_cols(d_mlp_full, down_mat)
        upgate = record["upgate"]
        up_s = upgate[:, :ff_here] * scale_up[None, :]
        gate_s = upgate[:, ff_here:] * scale_gate[None, :]
        gate_sig = jax.nn.sigmoid(gate_s)
        d_up = d_act * gate_s * gate_sig
        d_gate = d_act * up_s * gate_sig * (1.0 + gate_s * (1.0 - gate_sig))
        d_scale_up = jnp.sum(d_up * upgate[:, :ff_here], axis=0)
        d_scale_gate = jnp.sum(d_gate * upgate[:, ff_here:], axis=0)
        d_upgate = jnp.concatenate(
            [d_up * scale_up[None, :], d_gate * scale_gate[None, :]], axis=1
        ).astype(jnp.bfloat16)
        dw_ug = contract_rows(record["inner_full"], d_upgate)
        d_normed = d_normed + grad_cols(contract_cols(d_upgate, ug_mat))
        dz_one = sphere_back(record["mix_one"], record["ratio_one"], d_normed)
        d_hidden = (1.0 - alpha_attn)[None, :] * dz_one
        d_attn_n = alpha_attn[None, :] * dz_one
        d_alpha_attn = jnp.sum(dz_one * (record["attn_n"] - record["hidden"]), axis=0)
        d_attn = sphere_back(record["attn_raw"], record["ratio_a"], d_attn_n)
        d_attn_full = grad_rows(d_attn.astype(jnp.bfloat16))
        dw_out = contract_rows(record["attended_b"], d_attn_full)
        d_attended = contract_cols(d_attn_full, out_mat).astype(jnp.bfloat16)
        row_delta = jnp.transpose(head_sum(d_attended.astype(jnp.float32) * record["attended"]))
        do_heads = d_attended.reshape(tok_rows, heads_here, HEAD_DIM)
        backward_q_heads = record["query_b"].reshape(tok_rows, heads_here, HEAD_DIM)
        log_total = record["log_total"]

        def block_grads(dq_now, kv_block, offset):
            key_mask, needed = block_info(backward_lengths_row, backward_q_segment, offset)

            def compute(previous):
                key_heads = kv_block[:, :col_width].reshape(tok_rows, heads_here, HEAD_DIM)
                val_heads = kv_block[:, col_width:].reshape(tok_rows, heads_here, HEAD_DIM)
                attn_prob = jnp.where(
                    key_mask[None],
                    jnp.exp(block_scores(backward_q_heads, kv_block) - log_total[:, :, None]),
                    0.0,
                )
                d_prob = jnp.einsum(
                    "qhd,khd->hqk", do_heads, val_heads, preferred_element_type=jnp.float32
                )
                d_val = jnp.einsum(
                    "hqk,qhd->khd",
                    attn_prob.astype(jnp.bfloat16),
                    do_heads,
                    preferred_element_type=jnp.float32,
                )
                d_score = (attn_prob * (d_prob - row_delta[:, :, None])).astype(jnp.bfloat16)
                new_dq = (
                    previous
                    + jnp.einsum(
                        "hqk,khd->hqd", d_score, key_heads, preferred_element_type=jnp.float32
                    )
                    / score_div
                )
                d_key = (
                    jnp.einsum(
                        "hqk,qhd->khd",
                        d_score,
                        backward_q_heads,
                        preferred_element_type=jnp.float32,
                    )
                    / score_div
                )
                return (
                    jnp.concatenate(
                        [d_key.reshape(tok_rows, col_width), d_val.reshape(tok_rows, col_width)],
                        axis=1,
                    ),
                    new_dq,
                )

            def skipped(previous):
                return (jnp.zeros((tok_rows, 2 * col_width), jnp.float32), previous)

            return lax.cond(needed, compute, skipped, dq_now)

        own_part, dq_acc = block_grads(
            jnp.zeros((heads_here, tok_rows, HEAD_DIM), jnp.float32),
            record["blocks"][0],
            jnp.int32(0),
        )
        offsets = jnp.arange(1, reach_len + 1, dtype=jnp.int32)

        def again_step(state_in, offset):
            dkv_sum, kv_block, dq_now = state_in
            dkv_sum = pass_on(dkv_sum)
            kv_block = from_behind(kv_block, "dp", 1)
            dkv_part, dq_now = block_grads(dq_now, kv_block, offset)
            return ((dkv_sum + dkv_part, kv_block, dq_now), None)

        (dkv_sum, unused_block, dq_acc), unused_out = lax.scan(
            again_step, (own_part, record["blocks"][0], dq_acc), offsets
        )
        dkv_home = passed_along(dkv_sum.astype(jnp.bfloat16), "dp", -reach_len).astype(
            dkv_sum.dtype
        )
        dq_full = jnp.transpose(dq_acc, (1, 0, 2)).reshape(tok_rows, col_width)
        dq_raw, ds_query = prep_back(dq_full, record["q_rot"], record["q_ratio"], record)
        dk_raw, ds_key = prep_back(
            dkv_home[:, :col_width], record["k_rot"], record["k_ratio"], record
        )
        d_qkv = jnp.concatenate([dq_raw, dk_raw, dkv_home[:, col_width:]], axis=1).astype(
            jnp.bfloat16
        )
        dw_qkv = contract_rows(record["full_in"], d_qkv)
        d_hidden = d_hidden + grad_cols(contract_cols(d_qkv, qkv_mat))
        grads = (
            dw_qkv.reshape(D, 3, col_width),
            dw_out,
            dw_ug.reshape(D, 2, ff_here),
            dw_down,
            ds_query + ds_key,
            jnp.stack([d_scale_up, d_scale_gate]),
            jnp.stack([d_alpha_attn, d_alpha_mlp]),
        )
        d_hidden, grads = (d_hidden, grads)
        grad_b = d_hidden.astype(jnp.bfloat16)
        back_results.append(grad_b)
        grad_totals = grads if grad_totals is None else jax.tree.map(jnp.add, grad_totals, grads)
        if tick_no < micro_n:
            back_in = from_behind(grad_b, "section", -1)
    input_grads = jnp.stack(
        [
            jnp.where(
                first_section, back_results[micro_n - number], back_results[micro_n - 1 - number]
            )
            for number in range(micro_n)
        ]
    )
    summed = (
        lax.psum_scatter(
            grad_totals[0].astype(jnp.bfloat16), "dp", scatter_dimension=0, tiled=True
        ).astype(jnp.float32),
        lax.psum_scatter(
            grad_totals[1].astype(jnp.bfloat16), "dp", scatter_dimension=0, tiled=True
        ).astype(jnp.float32),
        lax.psum_scatter(
            grad_totals[2].astype(jnp.bfloat16), "dp", scatter_dimension=0, tiled=True
        ).astype(jnp.float32),
        lax.psum_scatter(
            grad_totals[3].astype(jnp.bfloat16), "dp", scatter_dimension=0, tiled=True
        ).astype(jnp.float32),
        lax.psum_scatter(
            grad_totals[4].astype(jnp.bfloat16), "dp", scatter_dimension=0, tiled=True
        ).astype(jnp.float32),
        lax.psum_scatter(
            grad_totals[5].astype(jnp.bfloat16), "dp", scatter_dimension=1, tiled=True
        ).astype(jnp.float32),
        lax.psum_scatter(
            grad_totals[6].astype(jnp.bfloat16), "dp", scatter_dimension=1, tiled=True
        ).astype(jnp.float32),
    )
    return (
        layer_outputs[None],
        input_grads[None],
        summed[0][None],
        summed[1][None],
        summed[2][None],
        summed[3][None],
        summed[4][None],
        summed[5][None],
        summed[6][None],
    )


MESH = pl.DeviceIdType.MESH
MICRO = 2
F32 = jnp.float32
BF16 = jnp.bfloat16


def mul(left_op, right_op):
    return jnp.dot(left_op, right_op, preferred_element_type=F32)


def remote(src, dst, send_sem, recv_sem, device):
    return pltpu.make_async_remote_copy(
        src_ref=src, dst_ref=dst, send_sem=send_sem, recv_sem=recv_sem, device_id=device, device_id_type=MESH
    )


def ball(values, width):
    ratio = lax.rsqrt(jnp.sum(values * values, axis=1, keepdims=True) / width + EPSILON)
    return values * ratio, ratio


def ball_back(source, ratio, grad_in, width):
    inner = jnp.sum(grad_in * source, axis=1, keepdims=True)
    return ratio * grad_in - source * (ratio * ratio * ratio) * (inner / width)


def buffers(nt, nz, rows, width, cols, hidden, shard, section, chunk):
    vmem, dma = pltpu.VMEM, pltpu.SemaphoreType.DMA
    pair = 2 * rows
    return dict(
        wq=vmem((2, 3, width, cols), BF16),
        wo=vmem((2, cols, width), BF16),
        wu=vmem((2, 2, width, hidden), BF16),
        wd=vmem((2, hidden, width), BF16),
        sqk=vmem((2, 1, cols), F32),
        suv=vmem((2, 2, hidden), F32),
        alp=vmem((2, 2, width), F32),
        raw=vmem((2 * hidden // 128 * width, 128), BF16),
        raw_f=vmem((2 * hidden // 128 * 64, 128), F32),
        full_in=vmem((2, rows, width), BF16),
        mid_full=vmem((2, nt, shard, width), BF16),
        dml_full=vmem((2, nt, shard, width), BF16),
        dat_full=vmem((2, rows, width), BF16),
        fi_p=vmem((rows, width), BF16),
        at_p=vmem((rows, cols), BF16),
        da_p=vmem((rows, width), BF16),
        dq_p=vmem((rows, 3 * cols), BF16),
        xa=vmem((nt, nz * 2 * shard, width), BF16),
        da=vmem((nt, nz * 2 * shard, width), BF16),
        kv=vmem((2, pair, 2 * cols), BF16),
        dkv_f=vmem((pair, 2 * cols), F32),
        dkv_s=vmem((2, rows, 2 * cols), BF16),
        dkv_r=vmem((2, rows, 2 * cols), BF16),
        rs_s=vmem((8, rows, width), BF16),
        rs_r=vmem((8, nt - 1, shard, width), BF16),
        rot=vmem((2, 2, rows, cols), F32),
        rat=vmem((2, 2, rows, cols), F32),
        qb=vmem((2, rows, cols), BF16),
        prob=vmem((2, cols // HEAD_DIM, rows, pair), F32),
        at=vmem((2, rows, cols), BF16),
        araw=vmem((2, shard, width), F32),
        mraw=vmem((2, shard, width), F32),
        mid=vmem((2, shard, width), F32),
        zone=vmem((2, shard, width), F32),
        ztwo=vmem((2, shard, width), F32),
        up=vmem((2, rows, hidden), F32),
        gate=vmem((2, rows, hidden), F32),
        duv=vmem((2, rows, hidden), BF16),
        dqkv=vmem((2, rows, 3 * cols), BF16),
        cot_rows=vmem((shard, width), BF16),
        out_s=vmem((2, shard, width), BF16),
        ig_s=vmem((2, shard, width), BF16),
        cosb=vmem((rows, cols), F32),
        sinb=vmem((rows, cols), F32),
        bias=vmem((rows, pair), F32),
        blk=vmem((cols, cols), BF16),
        al_s=vmem((2, 8, width), F32),
        al_r=vmem((2, nt - 1, 8, cols), F32),
        small=vmem((2, 8, cols), F32),
        sm_r=vmem((nz, 2, 8, cols), F32),
        wq_s=vmem((nz - 1, section, 3 * cols), BF16),
        wq_r=vmem((nz, section, 3 * cols), BF16),
        wo_f=vmem((cols, width), F32),
        wo_s=vmem((cols, width), BF16),
        wo_r=vmem((nz - 1, chunk, width), BF16),
        act_b=vmem((nz * 2 * shard, hidden), BF16),
        suv_b=vmem((2, hidden), F32),
        ahead=vmem((2, nt - 2, pair, hidden), F32),
        acc=vmem((2, section, hidden), F32),
        w_l=dma((2, 4)), w_rs=dma((4,)),
        par_l=dma((2, 2)), par_s=dma((2,)),
        alp_r=dma((2, nt)), alp_s=dma((2, nt)),
        hid_r=dma((nt,)), hid_s=dma((2, nt)),
        cot_r=dma((nt,)), cot_s=dma((2, nt)),
        fi_rs=dma((2,)), at_rs=dma((2,)), dap_rs=dma((2,)), dq_rs=dma((2,)),
        kv_rs=dma((2, 2)), dkv_rs=dma((2, 2)),
        ag_ss=dma((7, nt - 1)), ag_rr=dma((7, nt - 1)),
        rs_ss=dma((8, 2, nt - 1)), rs_rr=dma((8, 2, nt - 1)),
        xa_r=dma((nz, 2)), xa_ss=dma((2, nz)),
        da_r=dma((nz, 2)), da_ss=dma((2, nz)),
        df_ss=dma((nz - 1, nt - 1)), df_rr=dma((nz - 1, nt - 1)),
        xf_ss=dma((nz - 1, nt - 1)), xf_rr=dma((nz - 1, nt - 1)),
        lo_ss=dma((2, nt)), lo_r=dma((2, nt)),
        ig_ss=dma((2, nt)), ig_r=dma((2, nt)),
        al_ss=dma((2, nt - 1)), al_rr=dma((2, nt - 1)),
        sm_ss=dma((2, nz)), sm_rr=dma((nz, 2)),
        wq_ss=dma((nz - 1, 2)), wq_rr=dma((nz, 2)),
        wo_ss=dma((nz - 1,)), wo_rr=dma((nz - 1,)),
    )


def fused_kernel(names, nt, nz, *refs):
    hid, cot, lens, wq_in, wo_in, wu_in, wd_in, sqk_in, suv_in, alp_in, rates = refs[:11]
    lo, ig, gq, go, gu, gd, gsqk, gsuv, gal = refs[11:20]
    b = types.SimpleNamespace(**dict(zip(names, refs[20:])))
    rows, width = b.full_in.shape[1:]
    cols, hidden = b.qb.shape[2], b.wd.shape[1]
    shard = b.mid.shape[1]
    heads = cols // HEAD_DIM
    pair = 2 * rows
    section_rows = width // nz
    chunk = cols // nz
    tile = 512
    s, t, z = lax.axis_index("section"), lax.axis_index("tensor"), lax.axis_index("dp")
    p = lax.rem(z, 2)
    base = z - p
    peer = (1 - s, t, z)
    pending = []

    def around(k):
        return lax.rem(lax.div(t, 2) + k // 2, 2) * 2 + lax.rem(lax.rem(t, 2) + k % 2, 2)

    peers = (3, 1, 2)

    def along(k):
        return lax.rem(z + k, nz)

    def later(copy, when=None):
        pending.append((copy, when))

    def lanes(index, size):
        return pl.ds(pl.multiple_of(index * size, size), size)

    weights = [(wq_in, b.wq), (wo_in, b.wo), (None, b.wu), (wd_in, b.wd)]
    raw_copy = pltpu.make_async_copy(wu_in, b.raw, b.w_l.at[s, 2])
    raw_copy.start()
    for i in (0, 1, 3):
        src, dst = weights[i]
        pltpu.make_async_copy(src, dst.at[s], b.w_l.at[s, i]).start()
    params = [(sqk_in, b.sqk), (suv_in, b.suv)]
    for i, (src, dst) in enumerate(params):
        pltpu.make_async_copy(src, dst.at[s], b.par_l.at[s, i]).start()

    barrier = pltpu.get_barrier_semaphore()
    greeted = 0
    for dz in range(2):
        for dt in range(nt):
            for dc in range(2):
                if dz or dt or dc:
                    device = (lax.rem(s + dc, 2), around(dt), base + lax.rem(p + dz, 2))
                    pl.semaphore_signal(barrier, inc=1, device_id=device, device_id_type=MESH)
                    greeted += 1
    for dz in range(2, nz):
        for dc in range(2):
            device = (lax.rem(s + dc, 2), t, lax.rem(base + dz, nz))
            pl.semaphore_signal(barrier, inc=1, device_id=device, device_id_type=MESH)
            greeted += 1
    token0 = (base // 2) * pair
    pos_q = token0 + s * rows + lax.broadcasted_iota(jnp.int32, (rows, 1), 0)
    pos_k = token0 + lax.broadcasted_iota(jnp.int32, (1, pair), 1)

    def sequences(pos):
        seg = jnp.zeros_like(pos)
        first = jnp.zeros_like(pos)
        end = jnp.int32(0)
        for i in range(lens.shape[1]):
            end = end + lens[p, i]
            past = pos >= end
            seg = seg + past.astype(jnp.int32)
            first = jnp.where(past, end, first)
        return seg, pos - first

    seg_q, place_q = sequences(pos_q)
    seg_k, _ = sequences(pos_k)
    allowed = (seg_q == seg_k) & (pos_k <= pos_q)
    b.bias[...] = jnp.where(allowed, 0.0, NEG_LARGE)
    angle = place_q.astype(F32) * rates[...]
    b.cosb[...] = jnp.cos(angle)
    b.sinb[...] = jnp.sin(angle)
    col = lax.broadcasted_iota(jnp.int32, (1, cols), 1)
    lower = (col & (HEAD_DIM // 2)) == 0
    head_of = lax.shift_right_logical(col, 6)
    head_row = lax.shift_right_logical(lax.broadcasted_iota(jnp.int32, (cols, 1), 0), 6)
    b.blk[...] = jnp.where(head_row == head_of, 1.0, 0.0).astype(BF16)
    picks = [jnp.where(head_of == h, 1.0, 0.0) for h in range(heads)]
    b.al_s[...] = jnp.zeros_like(b.al_s)
    b.small[...] = jnp.zeros_like(b.small)

    @pl.when(s == 0)
    def _():
        b.kv[:, rows:pair, :] = jnp.zeros((2, rows, 2 * cols), BF16)

    @pl.when(s == 1)
    def _():
        b.dkv_r[...] = jnp.zeros_like(b.dkv_r)


    def to_order():
        raw_copy.wait()
        lines = 2 * hidden // 128

        def in_order(step, carry):
            b.raw_f[...] = b.raw[pl.ds(pl.multiple_of(step * lines * 64, lines * 64), lines * 64), :].astype(F32)
            at = pl.ds(pl.multiple_of(step * 64, 64), 64)
            for n in range(hidden // 128):
                for i in range(2):
                    b.wu[s, i, at, n * 128 : (n + 1) * 128] = b.raw_f[pl.ds(2 * n + i, 64, stride=lines), :].astype(BF16)
            return carry

        lax.fori_loop(0, width // 64, in_order, 0)

    pl.semaphore_wait(barrier, greeted)

    is_source = s == p
    def spread_rows(src, rs, ss):
        for dz in range(2):
            to_mb = lax.rem(p + dz, 2)
            for dt in peers + (0,):
                to_t = around(dt)
                if src is hid:
                    piece, place = src.at[to_mb], b.full_in.at[0, :, lanes(t, cols)]
                else:
                    piece = src.at[to_mb, pl.ds(pl.multiple_of(to_t * shard, shard), shard), :]
                    place = b.cot_rows.at[:, lanes(t, cols)]
                if dz == 0 and dt == 0:

                    @pl.when(is_source)
                    def _(piece=piece, place=place, rs=rs):
                        pltpu.make_async_copy(piece, place, rs.at[0]).start()
                else:
                    copy = remote(piece, place, ss.at[dz, dt], rs.at[dt], (s, to_t, base + to_mb))
                    pl.when(is_source)(copy.start)
                    later(copy, is_source)

    spread_rows(hid, b.hid_r, b.hid_s)
    for i, (src_p, dst_p) in enumerate(params):
        copy = remote(src_p, dst_p.at[s], b.par_s.at[i], b.par_l.at[s, i], peer)
        copy.start()
        later(copy)
    alp_src, alp_dst = alp_in, b.alp.at[s, :, lanes(t, cols)]
    for dc in range(2):
        for dt in range(nt):
            if dc == 0 and dt == 0:
                pltpu.make_async_copy(alp_src, alp_dst, b.alp_r.at[s, 0]).start()
            else:
                copy = remote(alp_src, alp_dst, b.alp_s.at[dc, dt], b.alp_r.at[s, dt], (lax.rem(s + dc, 2), around(dt), z))
                copy.start()
                later(copy)
    for i in (0, 1, 3):
        src_w, dst_w = weights[i]
        copy = remote(src_w, dst_w.at[s], b.w_rs.at[i], b.w_l.at[s, i], peer)
        copy.start()
        later(copy)

    def wait_weight(layer, i):
        dst_w = weights[i][1].at[layer]
        wait = pltpu.make_async_copy(dst_w, dst_w, b.w_l.at[layer, i]).wait
        if i == 2:
            pl.when(s != layer)(wait)
        else:
            wait()

    to_order()
    copy = remote(b.wu.at[s], b.wu.at[s], b.w_rs.at[2], b.w_l.at[s, 2], peer)
    copy.start()
    later(copy)

    def partner_cols(x):
        half = HEAD_DIM // 2
        return jnp.where(lower, -pltpu.roll(x, cols - half, 1), pltpu.roll(x, half, 1))

    def head_total(x):
        high = x.astype(BF16)
        low = (x - high.astype(F32)).astype(BF16)
        return mul(high, b.blk[...]) + mul(low, b.blk[...])

    def shard_of(ref, index):
        return ref.at[index] if len(ref.shape) == 3 else ref.at[pl.ds(pl.multiple_of(index * shard, shard), shard), :]

    def gather(stage, ref):
        mine = shard_of(ref, t)
        for k in peers:
            copy = remote(mine, mine, b.ag_ss.at[stage, k - 1], b.ag_rr.at[stage, k - 1], (s, around(k), z))
            copy.start()
            later(copy)

    def gather_wait(stage, ref):
        for k in range(1, nt):
            theirs = shard_of(ref, around(k))
            remote(theirs, theirs, b.ag_ss.at[stage, k - 1], b.ag_rr.at[stage, k - 1], (s, around(k), z)).wait_recv()

    def scatter(stage, n):
        cut = pl.ds(n * tile, tile)
        for k in peers:
            piece = b.rs_s.at[stage, pl.ds(pl.multiple_of(around(k) * shard, shard), shard), cut]
            copy = remote(piece, b.rs_r.at[stage, k - 1, :, cut], b.rs_ss.at[stage, n, k - 1], b.rs_rr.at[stage, n, k - 1], (s, around(k), z))
            copy.start()
            later(copy)

    def scatter_wait(stage):
        total = b.rs_s[stage, pl.ds(pl.multiple_of(t * shard, shard), shard), :].astype(F32)
        for n in range(width // tile):
            for k in range(1, nt):
                place = b.rs_r.at[stage, k - 1, :, pl.ds(n * tile, tile)]
                remote(place, place, b.rs_ss.at[stage, n, k - 1], b.rs_rr.at[stage, n, k - 1], (s, around(k), z)).wait_recv()
        for k in range(1, nt):
            total = total + b.rs_r[stage, k - 1].astype(F32)
        return total

    slot = pl.ds(pl.multiple_of((z * 2 + s) * shard, shard), shard)

    def my_rows(ref):
        return shard_of(ref, t)

    def to_owner(layer, ref, place_of, send_sems, recv_sems, hops=range(nz)):
        for k in hops:
            copy = remote(ref, place_of, send_sems.at[layer, k], recv_sems.at[k, s], (layer, t, along(k)))
            if k == 0:

                @pl.when(s == layer)
                def _():
                    pltpu.make_async_copy(ref, place_of, recv_sems.at[0, s]).start()

                pl.when(s != layer)(copy.start)
                later(copy, s != layer)
            else:
                copy.start()
                later(copy)

    x_rows = (b.xa, b.xa_r, b.xf_ss, b.xf_rr)
    d_rows = (b.da, b.da_r, b.df_ss, b.df_rr)

    def bundle(layer, hops, group):
        ref, arrived, send_sems, recv_sems = group
        for k in hops:
            from_z = along(nz - k)
            rows_of = pl.ds(pl.multiple_of(from_z * 2 * shard, 2 * shard), 2 * shard)

            @pl.when(s == layer)
            def _(k=k, from_z=from_z):
                for core in range(2):
                    row = pl.multiple_of((from_z * 2 + core) * shard, shard)
                    place = ref.at[t, pl.ds(row, shard), :]
                    pltpu.make_async_copy(place, place, arrived.at[k, core]).wait()

            for to in range(1, nt):
                place = ref.at[t, rows_of, :]
                copy = remote(place, place, send_sems.at[k - 1, to - 1], recv_sems.at[k - 1, to - 1], (s, around(to), z))
                pl.when(s == layer)(copy.start)
                later(copy, s == layer)

    def to_output(layer, ref, out, send_sems, recv_sems):
        to_z = base + s
        place = out.at[p, pl.ds(pl.multiple_of(t * shard, shard), shard), :]
        for k in range(nt):
            to_t = around(k)
            piece = ref.at[:, lanes(to_t, cols)]
            copy = remote(piece, place, send_sems.at[layer, k], recv_sems.at[p, k], (layer, to_t, to_z))
            if k == 0:
                here = (s == layer) & (to_z == z)

                @pl.when(here)
                def _(piece=piece):
                    pltpu.make_async_copy(piece, place, recv_sems.at[p, 0]).start()

                away = jnp.logical_not(here)
                pl.when(away)(copy.start)
                later(copy, away)
            else:
                copy.start()
                later(copy)

    upper = z // 2
    end, hub = 3 * upper, 1 + upper
    sibling = end + hub - z
    far_end, far_hub = 3 - end, 3 - hub

    def qkv_part(n, to, half, device):
        rows_of = pl.ds(half * (section_rows // 2), section_rows // 2)
        return remote(b.wq_s.at[n, rows_of], b.wq_r.at[to, rows_of], b.wq_ss.at[n, half], b.wq_rr.at[to, half], device)

    def hub_step(layer, n, half):
        @pl.when((s == layer) & (z == hub))
        def _():
            qkv_part(n, n, half, peer).wait_recv()
            rows_of = pl.ds(half * (section_rows // 2), section_rows // 2)
            b.wq_s[n, rows_of] = (b.wq_s[n, rows_of].astype(F32) + b.wq_r[n, rows_of].astype(F32)).astype(BF16)
            qkv_part(n, 3, half, (layer, t, far_hub if n else far_end)).start()

    for layer in range(2):
        full_in = b.full_in.at[layer]
        if layer == 0:
            for dt in range(nt):
                place = b.full_in.at[0, :, lanes(around(dt), cols)]
                pltpu.make_async_copy(hid.at[0], place, b.hid_r.at[dt]).wait()
            spread_rows(cot, b.cot_r, b.cot_s)
            for src_core in range(2):
                for i, (src_p, dst_p) in enumerate(params):
                    pltpu.make_async_copy(src_p, dst_p.at[src_core], b.par_l.at[src_core, i]).wait()
                for dt in range(nt):
                    place = b.alp.at[src_core, :, lanes(around(dt), cols)]
                    pltpu.make_async_copy(alp_in, place, b.alp_r.at[src_core, dt]).wait()
        else:
            gather_wait(6, full_in)
        copy = remote(full_in, b.fi_p, b.fi_rs.at[0], b.fi_rs.at[1], peer)
        pl.when(s != layer)(copy.start)
        later(copy, s != layer)
        scale_qk = b.sqk[layer]
        wait_weight(layer, 0)
        x = full_in[...]
        own = pl.ds(pl.multiple_of(s * rows, rows), rows)
        def normed_heads(i):
            raw = mul(x, b.wq[layer, i])
            rotated = raw * b.cosb[...] + partner_cols(raw) * b.sinb[...]
            ratio = lax.rsqrt(head_total(rotated * rotated) / HEAD_DIM + EPSILON)
            b.rot[layer, i] = rotated
            b.rat[layer, i] = ratio
            return (rotated * ratio * scale_qk).astype(BF16)

        b.kv[layer, own, 0:cols] = normed_heads(1)
        b.kv[layer, own, cols : 2 * cols] = mul(x, b.wq[layer, 2]).astype(BF16)
        mine = b.kv.at[layer, own, :]
        copy = remote(mine, mine, b.kv_rs.at[layer, 0], b.kv_rs.at[layer, 1], peer)
        pl.when(s == 0)(copy.start)
        later(copy, s == 0)
        b.qb[layer] = normed_heads(0)
        pl.when(s == 1)(copy.wait_recv)
        att = jnp.zeros((rows, cols), F32)
        for h in range(heads):
            q_h = (b.qb[layer].astype(F32) * picks[h]).astype(BF16)
            scores = contract_cols(q_h, b.kv[layer, :, 0:cols]) * (1.0 / math.sqrt(HEAD_DIM)) + b.bias[...]
            top = jnp.max(scores, axis=1, keepdims=True)
            terms = jnp.exp(scores - top)
            prob = terms / jnp.sum(terms, axis=1, keepdims=True)
            b.prob[layer, h] = prob
            att = att + picks[h] * mul(prob.astype(BF16), b.kv[layer, :, cols : 2 * cols])
        b.at[layer] = att.astype(BF16)
        wait_weight(layer, 1)
        for n in range(0, width, tile):
            b.rs_s[layer, :, n : n + tile] = mul(b.at[layer], b.wo[layer, :, n : n + tile]).astype(BF16)
            scatter(layer, n // tile)
        hin = my_rows(full_in)[...].astype(F32)
        rate_a = b.alp[layer, 0:1, :]
        rate_m = b.alp[layer, 1:2, :]
        araw = scatter_wait(layer)
        b.araw[layer] = araw
        zone = hin + rate_a * (ball(araw, width)[0] - hin)
        b.zone[layer] = zone
        mid = ball(zone, width)[0]
        b.mid[layer] = mid
        mid_full = b.mid_full.at[layer]
        my_rows(mid_full)[...] = mid.astype(BF16)
        gather(layer, mid_full)
        if layer == 1:
            to_owner(1, my_rows(mid_full), b.xa.at[t, slot, :], b.xa_ss, b.xa_r, range(1, nz))
        wait_weight(layer, 2)
        wait_weight(layer, 3)
        gather_wait(layer, mid_full)
        to_owner(layer, mid_full, b.xa.at[:, slot, :], b.xa_ss, b.xa_r, range(nz) if layer == 0 else (0,))
        x = mid_full[...].reshape(rows, width)
        for n in range(0, hidden, tile):
            cut = slice(n, n + tile)
            up = mul(x, b.wu[layer, 0, :, cut])
            gate = mul(x, b.wu[layer, 1, :, cut])
            b.up[layer, :, cut] = up
            b.gate[layer, :, cut] = gate
            gate_s = gate * b.suv[layer, 1:2, cut]
            b.duv[0, :, cut] = (up * b.suv[layer, 0:1, cut] * (gate_s / (1.0 + jnp.exp(-gate_s)))).astype(BF16)
        for n in range(0, width, tile):
            b.rs_s[2 + layer, :, n : n + tile] = mul(b.duv[0], b.wd[layer, :, n : n + tile]).astype(BF16)
            scatter(2 + layer, n // tile)
        if layer == 1:
            bundle(1, (1,), x_rows)
        mraw = scatter_wait(2 + layer)
        b.mraw[layer] = mraw
        ztwo = mid + rate_m * (ball(mraw, width)[0] - mid)
        b.ztwo[layer] = ztwo
        b.out_s[layer] = ball(ztwo, width)[0].astype(BF16)
        if layer == 0:
            my_rows(b.full_in.at[1])[...] = b.out_s[0]
            gather(6, b.full_in.at[1])
            to_output(0, b.out_s.at[0], lo, b.lo_ss, b.lo_r)

    mine_cols = lanes(z, section_rows)

    def ahead(k):
        if k == 2:
            for hop in range(nz):
                for core in range(2):
                    place = b.xa.at[:, pl.ds(pl.multiple_of((along(nz - hop) * 2 + core) * shard, shard), shard), :]
                    pltpu.make_async_copy(place, place, b.xa_r.at[hop, core]).wait()
        for n in range(0, hidden, tile):
            for i in range(2):
                b.ahead[i, k - 2, :, n : n + tile] = mul(b.xa[around(k)], b.wu[0, i, :, n : n + tile])

    def block(layer, k, between=None):
        at, first = around(k), k == 0
        if first:
            for core in range(2):
                row = pl.multiple_of((z * 2 + core) * shard, shard)
                for ref, sems in ((b.xa, b.xa_r), (b.da, b.da_r)):
                    if ref is b.da or layer == 1:
                        place = ref.at[:, pl.ds(row, shard), :]
                        pltpu.make_async_copy(place, place, sems.at[0, core]).wait()
        else:
            for hop in range(1, nz):
                for ref, _, ss, rr in (d_rows, x_rows):
                    if ref is b.da or layer == 1:
                        place = ref.at[at, pl.ds(pl.multiple_of(along(nz - hop) * 2 * shard, 2 * shard), 2 * shard), :]
                        remote(place, place, ss.at[hop - 1, k - 1], rr.at[hop - 1, k - 1], peer).wait_recv()

        def add(ref, value):
            ref[...] = value if first else ref[...] + value

        for n in range(0, hidden, tile):
            cut = slice(n, n + tile)
            if layer == 0 and k >= 2:
                up, gate = b.ahead[0, k - 2, :, cut], b.ahead[1, k - 2, :, cut]
            else:
                up, gate = mul(b.xa[at], b.wu[layer, 0, :, cut]), mul(b.xa[at], b.wu[layer, 1, :, cut])
            d_act = contract_cols(b.da[at], b.wd[layer, cut, :])
            scale_up, scale_gate = b.suv[layer, 0:1, cut], b.suv[layer, 1:2, cut]
            up_s = up * scale_up
            gate_s = gate * scale_gate
            sig = 1.0 / (1.0 + jnp.exp(-gate_s))
            silu = gate_s * sig
            b.act_b[:, cut] = (up_s * silu).astype(BF16)
            d_up = d_act * silu
            d_gate = d_act * up_s * sig * (1.0 + gate_s * (1.0 - sig))
            add(b.suv_b.at[0:1, cut], jnp.sum(d_up * up, axis=0, keepdims=True))
            add(b.suv_b.at[1:2, cut], jnp.sum(d_gate * gate, axis=0, keepdims=True))
            if between is not None and n:
                between()
            x_cut = b.xa[at, :, mine_cols]
            add(b.acc.at[0, :, cut], contract_rows(x_cut, (d_up * scale_up).astype(BF16)))
            add(b.acc.at[1, :, cut], contract_rows(x_cut, (d_gate * scale_gate).astype(BF16)))
        for n in range(0, width, tile):
            cut = slice(n, n + tile)
            add(gd.at[:, cut], contract_rows(b.act_b[:, lanes(z, hidden // nz)], b.da[at, :, cut]))

    def spare(layer, place):
        if layer == 1:
            if place < 2:
                pl.when(s == 0)(lambda: ahead(place + 2))
        else:
            if place >= 2:
                pl.when(s == 1)(lambda: block(1, place - 2))
            if place == 3:
                pl.when(s == 0)(lambda: block(0, 0))

    for dt in range(nt):
        place = b.cot_rows.at[:, lanes(around(dt), cols)]
        pltpu.make_async_copy(cot.at[0, pl.ds(0, shard), :], place, b.cot_r.at[dt]).wait()
    grad_out = b.cot_rows[...].astype(F32)
    for layer in (1, 0):
        own = pl.ds(pl.multiple_of(s * rows, rows), rows)
        other = pl.ds(pl.multiple_of((1 - s) * rows, rows), rows)
        rate_a = b.alp[layer, 0:1, :]
        rate_m = b.alp[layer, 1:2, :]
        scale_qk = b.sqk[layer]
        mid = b.mid[layer]
        mraw_n, ratio_m = ball(b.mraw[layer], width)
        ratio_two = ball(b.ztwo[layer], width)[1]
        d_two = ball_back(b.ztwo[layer], ratio_two, grad_out, width)
        d_mid = (1.0 - rate_m) * d_two
        b.al_s[layer, 1:2, :] = jnp.sum(d_two * (mraw_n - mid), axis=0, keepdims=True)
        dml_full = b.dml_full.at[layer]
        my_rows(dml_full)[...] = ball_back(b.mraw[layer], ratio_m, rate_m * d_two, width).astype(BF16)
        gather(2 + layer, dml_full)
        if layer == 1:
            to_output(1, b.out_s.at[1], lo, b.lo_ss, b.lo_r)
        else:
            to_output(1, b.ig_s.at[1], ig, b.ig_ss, b.ig_r)
        to_owner(layer, my_rows(dml_full), b.da.at[t, slot, :], b.da_ss, b.da_r, range(1, nz))
        if layer == 1:
            bundle(1, (2, 3), x_rows)
        spare(layer, 0)
        gather_wait(2 + layer, dml_full)
        to_owner(layer, dml_full, b.da.at[:, slot, :], b.da_ss, b.da_r, (0,))
        if layer == 0:
            bundle(1, (3,), d_rows)
        x = dml_full[...].reshape(rows, width)
        for n in range(0, hidden, tile):
            cut = slice(n, n + tile)
            d_act = contract_cols(x, b.wd[layer, cut, :])
            scale_up, scale_gate = b.suv[layer, 0:1, cut], b.suv[layer, 1:2, cut]
            up_s = b.up[layer, :, cut] * scale_up
            gate_s = b.gate[layer, :, cut] * scale_gate
            sig = 1.0 / (1.0 + jnp.exp(-gate_s))
            b.duv[0, :, cut] = (d_act * gate_s * sig * scale_up).astype(BF16)
            b.duv[1, :, cut] = (d_act * up_s * sig * (1.0 + gate_s * (1.0 - sig)) * scale_gate).astype(BF16)
        for n in range(0, width, tile):
            cut = slice(n, n + tile)
            part = contract_cols(b.duv[0], b.wu[layer, 0, cut, :]) + contract_cols(b.duv[1], b.wu[layer, 1, cut, :])
            b.rs_s[4 + layer, :, cut] = part.astype(BF16)
            scatter(4 + layer, n // tile)
        spare(layer, 1)
        hin = my_rows(b.full_in.at[layer])[...].astype(F32)
        araw_n, ratio_a = ball(b.araw[layer], width)
        ratio_one = ball(b.zone[layer], width)[1]
        d_mid = d_mid + scatter_wait(4 + layer)
        d_one = ball_back(b.zone[layer], ratio_one, d_mid, width)
        b.al_s[layer, 0:1, :] = jnp.sum(d_one * (araw_n - hin), axis=0, keepdims=True)
        dat_full = b.dat_full.at[layer]
        my_rows(dat_full)[...] = ball_back(b.araw[layer], ratio_a, rate_a * d_one, width).astype(BF16)
        gather(4 + layer, dat_full)
        for k in range(1, nt):
            copy = remote(b.al_s.at[layer, :, lanes(around(k), cols)], b.al_r.at[layer, k - 1], b.al_ss.at[layer, k - 1], b.al_rr.at[layer, k - 1], (s, around(k), z))
            copy.start()
            later(copy)
        if layer == 0:
            for n in range(2):
                for half in range(2):
                    hub_step(1, n, half)
        spare(layer, 2)
        gather_wait(4 + layer, dat_full)
        for src_v, dst_v, sems in ((dat_full, b.da_p, b.dap_rs), (b.at.at[layer], b.at_p, b.at_rs)):
            copy = remote(src_v, dst_v, sems.at[0], sems.at[1], peer)
            pl.when(s != layer)(copy.start)
            later(copy, s != layer)
        d_att = contract_cols(dat_full[...], b.wo[layer])
        d_scores = []
        dk = jnp.zeros((pair, cols), F32)
        dv = jnp.zeros((pair, cols), F32)
        for h in range(heads):
            d_att_h = (d_att * picks[h]).astype(BF16)
            q_h = (b.qb[layer].astype(F32) * picks[h]).astype(BF16)
            prob = b.prob[layer, h]
            d_prob = contract_cols(d_att_h, b.kv[layer, :, cols : 2 * cols])
            d_score = (prob * (d_prob - jnp.sum(prob * d_prob, axis=1, keepdims=True))).astype(BF16)
            dv = dv + contract_rows(prob.astype(BF16), d_att_h)
            d_scores.append(d_score)
            dk = dk + contract_rows(d_score, q_h)
        b.dkv_f[:, 0:cols] = dk * (1.0 / math.sqrt(HEAD_DIM))
        b.dkv_f[:, cols : 2 * cols] = dv
        b.dkv_s[layer] = b.dkv_f[other, :].astype(BF16)
        copy = remote(b.dkv_s.at[layer], b.dkv_r.at[layer], b.dkv_rs.at[layer, 0], b.dkv_rs.at[layer, 1], peer)
        pl.when(s == 1)(copy.start)
        later(copy, s == 1)
        bundle(layer, (1, 2), d_rows)
        dq = jnp.zeros((rows, cols), F32)
        for h in range(heads):
            dq = dq + picks[h] * mul(d_scores[h], b.kv[layer, :, 0:cols])

        @pl.when(s == layer)
        def _(layer=layer):
            for dst_v, sems in ((b.da_p, b.dap_rs), (b.at_p, b.at_rs)):
                remote(dst_v, dst_v, sems.at[0], sems.at[1], peer).wait_recv()
            for n in range(0, width, tile):
                cut = slice(n, n + tile)
                part = contract_rows(b.at[layer], b.dat_full[layer, :, cut]) + contract_rows(b.at_p[...], b.da_p[:, cut])
                b.wo_f[:, cut] = part
                b.wo_s[:, cut] = part.astype(BF16)
            for k in range(1, nz):
                piece = b.wo_s.at[pl.ds(pl.multiple_of(along(k) * chunk, chunk), chunk), :]
                remote(piece, b.wo_r.at[k - 1], b.wo_ss.at[k - 1], b.wo_rr.at[k - 1], (layer, t, along(k))).start()

        d_scale = jnp.zeros((1, cols), F32)
        for i in range(2):
            if i == 0:
                grad_n = dq * (1.0 / math.sqrt(HEAD_DIM))
            else:
                pl.when(s == 0)(copy.wait_recv)
                grad_n = b.dkv_f[own, 0:cols] + b.dkv_r[layer, :, 0:cols].astype(F32)
            rotated, ratio = b.rot[layer, i], b.rat[layer, i]
            d_scale = d_scale + jnp.sum(grad_n * rotated * ratio, axis=0, keepdims=True)
            d_unit = grad_n * scale_qk
            d_rot = ratio * d_unit - rotated * (ratio * ratio * ratio) * (head_total(d_unit * rotated) / HEAD_DIM)
            d_raw = d_rot * b.cosb[...] - partner_cols(d_rot * b.sinb[...])
            b.dqkv[layer, :, i * cols : (i + 1) * cols] = d_raw.astype(BF16)
        d_val = b.dkv_f[own, cols : 2 * cols] + b.dkv_r[layer, :, cols : 2 * cols].astype(F32)
        b.dqkv[layer, :, 2 * cols : 3 * cols] = d_val.astype(BF16)
        copy = remote(b.dqkv.at[layer], b.dq_p, b.dq_rs.at[0], b.dq_rs.at[1], peer)
        pl.when(s != layer)(copy.start)
        later(copy, s != layer)
        def qkv_pieces(layer=layer):
            for dst_v, sems in ((b.fi_p, b.fi_rs), (b.dq_p, b.dq_rs)):
                remote(dst_v, dst_v, sems.at[0], sems.at[1], peer).wait_recv()
            for n, index in enumerate((far_end, far_hub, sibling, z)):
                cut = lanes(index, section_rows)
                part = contract_rows(b.full_in[layer, :, cut], b.dqkv[layer]) + contract_rows(b.fi_p[:, cut], b.dq_p[...])
                if n == 3:
                    for i in range(3):
                        gq[i] = part[:, i * cols : (i + 1) * cols]
                    continue
                b.wq_s[n] = part.astype(BF16)
                for half in range(2):
                    start = qkv_part(n, n, half, (layer, t, sibling)).start
                    if n == 2:
                        start()
                    else:
                        pl.when(z == end)(start)

        def last_sum(layer=layer):
            for n in range(0, width, tile):
                part = contract_cols(b.dqkv[layer, :, 0:cols], b.wq[layer, 0, n : n + tile, :])
                for i in range(1, 3):
                    part = part + contract_cols(b.dqkv[layer, :, i * cols : (i + 1) * cols], b.wq[layer, i, n : n + tile, :])
                b.rs_s[6 + layer, :, n : n + tile] = part.astype(BF16)
                scatter(6 + layer, n // tile)

        if layer == 1:
            last_sum()
        pl.when(s == layer)(qkv_pieces)
        if layer == 0:
            last_sum()
        total = b.al_s[layer, :, lanes(t, cols)]
        for k in range(1, nt):
            place = b.al_r.at[layer, k - 1]
            remote(place, place, b.al_ss.at[layer, k - 1], b.al_rr.at[layer, k - 1], peer).wait_recv()
            total = total + place[...]
        b.small[layer] = total
        b.small[layer, 2:3, :] = d_scale
        to_owner(layer, b.small.at[layer], b.sm_r.at[lax.rem(z, nz), s], b.sm_ss, b.sm_rr)

        if layer == 0:
            bundle(0, (3,), d_rows)
        spare(layer, 3)
        if layer == 0:
            hub_step(0, 0, 0)
        d_hin = (1.0 - rate_a) * d_one + scatter_wait(6 + layer)
        b.ig_s[layer] = d_hin.astype(BF16)
        if layer == 0:
            to_output(0, b.ig_s.at[0], ig, b.ig_ss, b.ig_r)
        grad_out = b.ig_s[layer].astype(F32)

    hub_step(0, 0, 1)

    @pl.when(s == 0)
    def _():
        block(0, 1, lambda: hub_step(0, 1, 0))
        hub_step(0, 1, 1)
        block(0, 2)
        block(0, 3)

    @pl.when(s == 1)
    def _():
        for k in (2, 3):
            block(1, k)

    gsuv[...] = b.suv_b[:, lanes(z, hidden // nz)]
    per_row = 2 * hidden // 128
    for j in range(hidden // 128):
        for i in range(2):
            gu[pl.ds(2 * j + i, section_rows, stride=per_row), :] = b.acc[i, :, j * 128 : (j + 1) * 128]

    for n in (2, 3):
        for half in range(2):
            qkv_part(2, n, half, peer).wait_recv()
            rows_of = slice(half * (section_rows // 2), (half + 1) * (section_rows // 2))
            for i in range(3):
                gq[i, rows_of] += b.wq_r[n, rows_of, i * cols : (i + 1) * cols].astype(F32)
    total = b.wo_f[pl.ds(pl.multiple_of(z * chunk, chunk), chunk), :]
    for k in range(1, nz):
        place = b.wo_r.at[k - 1]
        remote(place, place, b.wo_ss.at[k - 1], b.wo_rr.at[k - 1], peer).wait_recv()
        total = total + place[...].astype(F32)
    go[...] = total
    total = jnp.zeros((8, cols), F32)
    for k in range(nz):
        for core in range(2):
            place = b.sm_r.at[lax.rem(z + nz - k, nz), core]
            pltpu.make_async_copy(place, place, b.sm_rr.at[k, core]).wait()
            total = total + place[...]
    turned = pltpu.roll(total, lax.rem(cols - z * chunk, cols), 1)
    gal[...] = turned[0:2, 0:chunk]
    gsqk[...] = turned[2:3, 0:chunk]
    for out, sems in ((lo, b.lo_r), (ig, b.ig_r)):
        for m in range(2):
            for k in range(nt):
                place = out.at[m, pl.ds(pl.multiple_of(around(k) * shard, shard), shard), :]
                pltpu.make_async_copy(place, place, sems.at[m, k]).wait()
    for k in range(nz - 1):
        for half in range(2):
            qkv_part(k, k, half, peer).wait_send()
        piece = b.wo_s.at[pl.ds(0, chunk), :]
        remote(piece, b.wo_r.at[k], b.wo_ss.at[k], b.wo_rr.at[k], peer).wait_send()
    for copy, when in pending:
        if when is None:
            copy.wait_send()
        else:
            pl.when(when)(copy.wait_send)


def copy_kernel(*refs):
    count = len(refs) // 3
    sems = refs[-1]
    reads = [pltpu.make_async_copy(refs[i], refs[2 * count + i], sems.at[0, i]) for i in range(count)]
    writes = [pltpu.make_async_copy(refs[2 * count + i], refs[count + i], sems.at[1, i]) for i in range(count)]
    for copy in reads:
        copy.start()
    for read, write in zip(reads, writes):
        read.wait()
        write.start()
    for copy in writes:
        copy.wait()


def per_device_fused(hidden_in, cotangent, lengths, w_qkv, w_out, w_ug, w_down, s_qk, s_uv, alpha):
    nt, nz = lax.axis_size("tensor"), lax.axis_size("dp")
    rows, cols = hidden_in.shape[1:]
    width, hidden = w_out.shape[2], w_down.shape[1]
    shard, section, chunk = rows // nt, width // nz, cols // nz
    half = HEAD_DIM // 2
    rates = (10000.0 ** (-(np.arange(cols) % half).astype(np.float32) / half)).astype(np.float32)[None, :]
    pairs = w_ug[0].reshape(width, 2, hidden // 128, 128).transpose(0, 2, 1, 3).reshape(2 * hidden // 128 * width, 128)
    scratch = buffers(nt, nz, rows, width, cols, hidden, shard, section, chunk)
    anywhere = pl.BlockSpec(memory_space=pl.ANY)
    vmem = pl.BlockSpec(memory_space=pltpu.VMEM)
    smem = pl.BlockSpec(memory_space=pltpu.SMEM)
    outs = pl.pallas_call(
        functools.partial(fused_kernel, tuple(scratch), nt, nz),
        out_shape=(
            jax.ShapeDtypeStruct((MICRO, rows, cols), BF16),
            jax.ShapeDtypeStruct((MICRO, rows, cols), BF16),
            jax.ShapeDtypeStruct((3, section, cols), F32),
            jax.ShapeDtypeStruct((chunk, width), F32),
            jax.ShapeDtypeStruct((section * 2 * hidden // 128, 128), F32),
            jax.ShapeDtypeStruct((hidden // nz, width), F32),
            jax.ShapeDtypeStruct((1, chunk), F32),
            jax.ShapeDtypeStruct((2, hidden // nz), F32),
            jax.ShapeDtypeStruct((2, chunk), F32),
        ),
        in_specs=[anywhere, anywhere, smem] + [anywhere] * 7 + [vmem],
        out_specs=(anywhere, anywhere) + (vmem,) * 7,
        scratch_shapes=list(scratch.values()),
        compiler_params=pltpu.CompilerParams(
            collective_id=0, has_side_effects=True, vmem_limit_bytes=60 * 2**20
        ),
    )(
        hidden_in,
        cotangent,
        lengths,
        jnp.transpose(w_qkv[0], (1, 0, 2)),
        w_out[0],
        pairs,
        w_down[0],
        s_qk,
        s_uv[0],
        alpha[0],
        jnp.asarray(rates),
    )
    lo, ig, gq, go, gu, gd, gsqk, gsuv, gal = pl.pallas_call(
        copy_kernel,
        out_shape=tuple(jax.ShapeDtypeStruct(o.shape, o.dtype) for o in outs),
        in_specs=[anywhere] * len(outs),
        out_specs=(anywhere,) * len(outs),
        scratch_shapes=[pltpu.VMEM(o.shape, o.dtype) for o in outs] + [pltpu.SemaphoreType.DMA((2, len(outs)))],
        compiler_params=pltpu.CompilerParams(vmem_limit_bytes=60 * 2**20),
    )(*outs)
    gu = gu.reshape(section, hidden // 128, 2, 128).transpose(0, 2, 1, 3).reshape(section, 2, hidden)
    return (
        lo[None],
        ig[None],
        jnp.transpose(gq, (1, 0, 2))[None],
        go[None],
        gu[None],
        gd[None],
        gsqk,
        gsuv[None],
        gal[None],
    )


def solution(mesh):
    placed = (
        P(None, "dp", "tensor"),
        P(None, "dp", "tensor"),
        P(),
        P("section", None, None, "tensor"),
        P("section", "tensor", None),
        P("section", None, None, "tensor"),
        P("section", "tensor", None),
        P("section", "tensor"),
        P("section", None, "tensor"),
        P("section", None, "tensor"),
    )
    per_rank = per_device_fused if mesh.shape["dp"] == 2 * MICRO and mesh.shape["tensor"] == 4 else per_device
    return jax.shard_map(
        per_rank,
        mesh=mesh,
        in_specs=placed,
        out_specs=(
            P("section", None, "dp", "tensor"),
            P("section", None, "dp", "tensor"),
            P("section", "dp", None, "tensor"),
            P("section", ("tensor", "dp"), None),
            P("section", "dp", None, "tensor"),
            P("section", ("tensor", "dp"), None),
            P("section", ("tensor", "dp")),
            P("section", None, ("tensor", "dp")),
            P("section", None, ("tensor", "dp")),
        ),
        check_vma=False,
    )
```
